256 devices in a mesh: row: 16 (over x, z_hi), col: 16 (over y, z_lo, core).
Axes of the slice: x: 4, y: 4, z: 8 (z_hi: 4, z_lo: 2; z = z_hi * 2 + z_lo), core: 2. Of those that a mesh axis runs over, the one named last changes fastest.
Arguments:
- gradient: bfloat16 [8192, 28672], P('row', 'col')
Outputs:
- left_gram: float32 [8192, 2048], P('row', 'col')
- right_gram: float32 [28672, 1792], P(('col', 'row'))
All inputs are finite; a program needn't handle non-finite values.
Results may differ from the reference program's by a relative error of at most 0.0003.
Values may be sent and summed in bfloat16 or wider, within the bound.
No kernel may reach another device: no remote copies, remote signals or barrier semaphores. Data moves between devices by JAX's collectives and lax.ppermute only.
A program may use at most 64 MiB of HBM per device.

```python
import jax
import jax.numpy as jnp
from jax import lax

LBLK = 2048
CBLK = 1792
M_WIN = 8192
NCOL = 28672


def draw_gradient(key, part):
    key = jax.random.fold_in(key, 7)
    keys = jax.random.split(key, 3)
    row_scale = jnp.exp(jax.random.uniform(keys[0], (M_WIN, 1), jnp.float32, -1.15, 1.15))
    col_scale = jnp.exp(jax.random.uniform(keys[1], (1, NCOL), jnp.float32, -1.15, 1.15))
    base = jax.random.normal(keys[2], (M_WIN, NCOL), jnp.float32)
    return (base * row_scale * col_scale * 0.3).astype(jnp.bfloat16)


def setup_inputs(seed: int = 0) -> dict:
    key_of = jax.random.split(jax.random.key(seed), 2)
    gradient = draw_gradient(jax.random.fold_in(key_of[1], 71), 0)
    return {"gradient": gradient}


def reference(gradient):
    blocks = gradient.reshape(M_WIN // LBLK, LBLK, NCOL)

    def left_one(piece):
        return jnp.dot(piece, piece.T, preferred_element_type=jnp.float32) * (1.0 / NCOL)

    left_gram = lax.map(left_one, blocks).reshape(M_WIN, LBLK)
    columns = gradient.reshape(M_WIN, NCOL // CBLK, CBLK).transpose(1, 0, 2)

    def right_one(piece):
        return jnp.dot(piece.T, piece, preferred_element_type=jnp.float32) * (1.0 / M_WIN)

    right_gram = lax.map(right_one, columns).reshape(NCOL, CBLK)
    return left_gram, right_gram
```

```python
import itertools

import jax
import jax.numpy as jnp
from jax import lax
from jax.sharding import PartitionSpec as P

LBLK = 2048
F32, BF16 = jnp.float32, jnp.bfloat16

SIZES = (4, 4, 4, 2, 2)
PLACES = list(itertools.product(*(range(n) for n in SIZES)))


def number(place):
    x, zh, y, zl, core = (p % n for p, n in zip(place, SIZES))
    return (4 * x + zh) * 16 + 4 * y + 2 * zl + core


def send(array, to):
    return lax.ppermute(array, ("row", "col"), [(number(p), number(to(*p))) for p in PLACES])


POWER = 13
LIFT = 120 / POWER


def inverse_norm(squares):
    return jnp.where(squares > 0, lax.rsqrt(jnp.where(squares > 0, squares, 1.0)), 0.0)


def norm(squares):
    return jnp.sqrt(squares)


def encode(value, rows, cols):
    ratio = value * rows[:, None] * (cols * 2.0**LIFT)[None, :]
    p2 = ratio * ratio
    p4 = p2 * p2
    return (p4 * p4 * (p4 * ratio)).astype(BF16)


def decode(code):
    wide = code.astype(F32)
    size = jnp.exp2(jnp.log2(jnp.abs(wide)) * (1.0 / POWER) - LIFT)
    return jnp.where(wide < 0, -size, size)


def dot(left, right, dim):
    return lax.dot_general(
        left, right, (((dim,), (dim,)), ((), ())), preferred_element_type=F32
    )


def shards(gradient):
    rows, width = gradient.shape
    row, col = lax.axis_index("row"), lax.axis_index("col")
    x, zh = row // 4, row % 4
    y, zl, core = col // 4, col // 2 % 2, col % 2
    total_rows, total_cols = rows * 16, width * 16

    squares = jnp.square(gradient.astype(F32))
    row_squares = jnp.sum(lax.all_gather(jnp.sum(squares, 1), "col"), 0)
    groups = [[4 * a + b for b in range(4)] for a in range(4)]
    row_squares = lax.all_gather(row_squares, "row", axis_index_groups=groups)
    own_squares = jnp.sum(squares, 0)
    col_squares = lax.all_gather(own_squares, "row")

    half = width // 2

    def columns(parity):
        return lax.dynamic_slice_in_dim(gradient, parity * half, half, 1)

    near = send(
        columns((zh + 1) % 2), lambda x, zh, y, zl, core: (x, 2 * core + (zh + 1) % 2, y, zl, zh // 2)
    )
    far = send(columns(zh % 2), lambda x, zh, y, zl, core: (x, 2 * core + zh % 2, y, zl, zh // 2))

    block = width // 4
    inverse_own = inverse_norm(own_squares)
    index = lambda s: (x + s) % 4

    def right_part(s):
        mine = lax.dynamic_slice_in_dim(gradient, index(s) * block, block, 1)
        return dot(mine, gradient, 0)

    right_total = right_part(0)
    right_in = []
    for s in (1, 3, 2):
        scale = lax.dynamic_slice_in_dim(inverse_own, index(s) * block, block, 0)
        code = encode(right_part(s), scale, inverse_own)
        right_in.append((s, send(code, lambda x, zh, y, zl, core: (x + s, zh, y, zl, core))))

    swap = lambda x, zh, y, zl, core: (x, zh, y, zl, 1 - core)
    other_near = send(near, swap)
    other_far = send(far, swap)
    held = jnp.stack([far, near, other_far, other_near])
    place = lambda j: 2 * ((j // 2) ^ core) + (j + zh) % 2
    order = jnp.stack([2 * core + zh % 2, 2 * core + 1 - zh % 2, 2 * (1 - core) + zh % 2, 2 * (1 - core) + 1 - zh % 2])
    held_squares = row_squares[order].reshape(-1)
    flat = held.reshape(LBLK, half)
    inverse_rows = inverse_norm(held_squares)

    def pick(array, j):
        part = lax.dynamic_index_in_dim(array, j, 0, False).reshape(2, 2, 128, *array.shape[2:])
        return lax.dynamic_index_in_dim(part, core, 1, False).reshape(256, *array.shape[2:])

    def left_part(j):
        return dot(flat, pick(held, place(j)), 1)

    left_in = []
    for s in (1, 3, 2):
        j = (y + s) % 4
        code = encode(left_part(j), inverse_rows, inverse_norm(pick(row_squares, j)))
        left_in.append(send(code, lambda x, zh, y, zl, core: (x, zh, y + s, zl, core)))
    left_own = left_part(y)
    left_cols = pick(row_squares, y)
    left_sum = left_own + sum(decode(c) for c in left_in) * (
        norm(held_squares)[:, None] * norm(left_cols)[None, :]
    )

    right_sum = right_total
    for s, code in right_in:
        their = norm(lax.dynamic_index_in_dim(col_squares, (x - s) % 4 * 4 + zh, 0, False))
        mine = lax.dynamic_slice_in_dim(their, x * block, block, 0)
        right_sum = right_sum + decode(code) * mine[:, None] * their[None, :]
    all_squares = jnp.sum(col_squares, 0)
    my_squares = lax.dynamic_slice_in_dim(all_squares, x * block, block, 0)
    right_code = encode(right_sum, inverse_norm(my_squares), inverse_norm(all_squares))
    chunk = block // 4
    right_final = []
    for s in (1, 3, 2):
        piece = lax.dynamic_slice_in_dim(right_code, (zh + s) % 4 * chunk, chunk, 0)
        right_final.append(send(piece, lambda x, zh, y, zl, core: (x, zh + s, y, zl, core)))
    own = lax.dynamic_slice_in_dim(right_sum, zh * chunk, chunk, 0)
    chunk_squares = lax.dynamic_slice_in_dim(my_squares, zh * chunk, chunk, 0)
    right_gram = (
        own + sum(decode(c) for c in right_final) * (norm(chunk_squares)[:, None] * norm(all_squares)[None, :])
    ) * (1.0 / total_rows)

    left_code = encode(left_sum, inverse_rows, inverse_norm(left_cols))

    def final_piece(array, zh_to, zl_to):
        start = place(zh_to) * 512
        return lax.dynamic_slice(array, (start, zl_to * 128), (512, 128))

    left_final = []
    for s in (1, 7, 2, 6, 3, 5, 4):
        z = (2 * zh + zl + s) % 8
        piece = final_piece(left_code, z // 2, z % 2)

        def to(x, zh, y, zl, core):
            z = (2 * zh + zl + s) % 8
            return (x, z // 2, y, z % 2, core)

        left_final.append(send(piece, to))
    mine = final_piece(left_sum, zh, zl)
    out_rows = norm(lax.dynamic_index_in_dim(row_squares, zh, 0, False))
    out_cols = norm(lax.dynamic_slice_in_dim(left_cols, zl * 128, 128, 0))
    left_gram = (mine + sum(decode(c) for c in left_final) * (out_rows[:, None] * out_cols[None, :])) * (
        1.0 / total_cols
    )
    return (left_gram, right_gram)


def solution(mesh):
    in_specs = (P("row", "col"),)
    out_specs = (P("row", "col"), P(("col", "row"), None))
    return jax.shard_map(shards, mesh=mesh, in_specs=in_specs, out_specs=out_specs, check_vma=False)
```

```python
import itertools

import jax
import jax.numpy as jnp
from jax import lax
from jax.sharding import PartitionSpec as P

LBLK = 2048
F32, BF16 = jnp.float32, jnp.bfloat16

SIZES = (4, 4, 4, 2, 2)
PLACES = list(itertools.product(*(range(n) for n in SIZES)))


def number(place):
    x, zh, y, zl, core = (p % n for p, n in zip(place, SIZES))
    return (4 * x + zh) * 16 + 4 * y + 2 * zl + core


def send(array, to):
    return lax.ppermute(array, ("row", "col"), [(number(p), number(to(*p))) for p in PLACES])


POWER = 13
LIFT = 120 / POWER


def inverse_norm(squares):
    return jnp.where(squares > 0, lax.rsqrt(jnp.where(squares > 0, squares, 1.0)), 0.0)


def norm(squares):
    return jnp.sqrt(squares)


def encode(value, rows, cols):
    ratio = value * rows[:, None] * (cols * 2.0**LIFT)[None, :]
    p2 = ratio * ratio
    p4 = p2 * p2
    return (p4 * p4 * (p4 * ratio)).astype(BF16)


def decode(code):
    wide = code.astype(F32)
    size = jnp.exp2(jnp.log2(jnp.abs(wide)) * (1.0 / POWER) - LIFT)
    return jnp.where(wide < 0, -size, size)


def dot(left, right, dim):
    return lax.dot_general(
        left, right, (((dim,), (dim,)), ((), ())), preferred_element_type=F32
    )


def shards(gradient):
    rows, width = gradient.shape
    row, col = lax.axis_index("row"), lax.axis_index("col")
    x, zh = row // 4, row % 4
    y, zl, core = col // 4, col // 2 % 2, col % 2
    total_rows, total_cols = rows * 16, width * 16

    squares = jnp.square(gradient.astype(F32))
    row_squares = jnp.sum(squares, 1)
    row_squares += send(row_squares, lambda x, zh, y, zl, core: (x, zh, y, zl, 1 - core))
    row_squares += send(row_squares, lambda x, zh, y, zl, core: (x, zh, y, 1 - zl, core))
    row_squares += send(row_squares, lambda x, zh, y, zl, core: (x, zh, y ^ 1, zl, core))
    row_squares += send(row_squares, lambda x, zh, y, zl, core: (x, zh, y ^ 2, zl, core))
    row_squares = row_squares[None]
    for bit in (1, 2):
        there = send(row_squares, lambda x, zh, y, zl, core: (x, zh ^ bit, y, zl, core))
        upper = (zh & bit) > 0
        row_squares = jnp.concatenate(
            [jnp.where(upper, there, row_squares), jnp.where(upper, row_squares, there)]
        )
    own_squares = jnp.sum(squares, 0)
    their_squares = {
        s: send(own_squares, lambda x, zh, y, zl, core: (x + s, zh, y, zl, core)) for s in (1, 3, 2)
    }
    all_squares = own_squares + sum(their_squares.values())
    for bit in (1, 2):
        all_squares += send(all_squares, lambda x, zh, y, zl, core: (x, zh ^ bit, y, zl, core))

    half = width // 2

    def columns(parity):
        return lax.dynamic_slice_in_dim(gradient, parity * half, half, 1)

    near = send(
        columns((zh + 1) % 2), lambda x, zh, y, zl, core: (x, 2 * core + (zh + 1) % 2, y, zl, zh // 2)
    )
    far = send(columns(zh % 2), lambda x, zh, y, zl, core: (x, 2 * core + zh % 2, y, zl, zh // 2))

    block = width // 4
    inverse_own = inverse_norm(own_squares)
    index = lambda s: (x + s) % 4

    def right_part(s):
        mine = lax.dynamic_slice_in_dim(gradient, index(s) * block, block, 1)
        return dot(mine, gradient, 0)

    right_total = right_part(0)
    right_in = []
    for s in (1, 3, 2):
        scale = lax.dynamic_slice_in_dim(inverse_own, index(s) * block, block, 0)
        code = encode(right_part(s), scale, inverse_own)
        right_in.append((s, send(code, lambda x, zh, y, zl, core: (x + s, zh, y, zl, core))))

    swap = lambda x, zh, y, zl, core: (x, zh, y, zl, 1 - core)
    other_near = send(near, swap)
    other_far = send(far, swap)
    held = jnp.stack([far, near, other_far, other_near])
    place = lambda j: 2 * ((j // 2) ^ core) + (j + zh) % 2
    order = jnp.stack([2 * core + zh % 2, 2 * core + 1 - zh % 2, 2 * (1 - core) + zh % 2, 2 * (1 - core) + 1 - zh % 2])
    held_squares = row_squares[order].reshape(-1)
    flat = held.reshape(LBLK, half)
    inverse_rows = inverse_norm(held_squares)

    def pick(array, j):
        part = lax.dynamic_index_in_dim(array, j, 0, False).reshape(2, 2, 128, *array.shape[2:])
        return lax.dynamic_index_in_dim(part, core, 1, False).reshape(256, *array.shape[2:])

    def left_part(j):
        return dot(flat, pick(held, place(j)), 1)

    left_in = []
    for s in (1, 3, 2):
        j = (y + s) % 4
        code = encode(left_part(j), inverse_rows, inverse_norm(pick(row_squares, j)))
        left_in.append(send(code, lambda x, zh, y, zl, core: (x, zh, y + s, zl, core)))
    left_own = left_part(y)
    left_cols = pick(row_squares, y)
    left_sum = left_own + sum(decode(c) for c in left_in) * (
        norm(held_squares)[:, None] * norm(left_cols)[None, :]
    )

    right_sum = right_total
    for s, code in right_in:
        their = norm(their_squares[s])
        mine = lax.dynamic_slice_in_dim(their, x * block, block, 0)
        right_sum = right_sum + decode(code) * mine[:, None] * their[None, :]
    my_squares = lax.dynamic_slice_in_dim(all_squares, x * block, block, 0)
    right_code = encode(right_sum, inverse_norm(my_squares), inverse_norm(all_squares))
    chunk = block // 4
    right_final = []
    for s in (1, 3, 2):
        piece = lax.dynamic_slice_in_dim(right_code, (zh + s) % 4 * chunk, chunk, 0)
        right_final.append(send(piece, lambda x, zh, y, zl, core: (x, zh + s, y, zl, core)))
    own = lax.dynamic_slice_in_dim(right_sum, zh * chunk, chunk, 0)
    chunk_squares = lax.dynamic_slice_in_dim(my_squares, zh * chunk, chunk, 0)
    right_gram = (
        own + sum(decode(c) for c in right_final) * (norm(chunk_squares)[:, None] * norm(all_squares)[None, :])
    ) * (1.0 / total_rows)

    left_code = encode(left_sum, inverse_rows, inverse_norm(left_cols))

    def final_piece(array, zh_to, zl_to):
        start = place(zh_to) * 512
        return lax.dynamic_slice(array, (start, zl_to * 128), (512, 128))

    left_final = []
    for s in (1, 7, 2, 6, 3, 5, 4):
        z = (2 * zh + zl + s) % 8
        piece = final_piece(left_code, z // 2, z % 2)

        def to(x, zh, y, zl, core):
            z = (2 * zh + zl + s) % 8
            return (x, z // 2, y, z % 2, core)

        left_final.append(send(piece, to))
    mine = final_piece(left_sum, zh, zl)
    out_rows = norm(lax.dynamic_index_in_dim(row_squares, zh, 0, False))
    out_cols = norm(lax.dynamic_slice_in_dim(left_cols, zl * 128, 128, 0))
    left_gram = (mine + sum(decode(c) for c in left_final) * (out_rows[:, None] * out_cols[None, :])) * (
        1.0 / total_cols
    )
    return (left_gram, right_gram)


def solution(mesh):
    in_specs = (P("row", "col"),)
    out_specs = (P("row", "col"), P(("col", "row"), None))
    return jax.shard_map(shards, mesh=mesh, in_specs=in_specs, out_specs=out_specs, check_vma=False)
```

```python
import itertools

import jax
import jax.numpy as jnp
from jax import lax
from jax.sharding import PartitionSpec as P

LBLK = 2048
F32, BF16 = jnp.float32, jnp.bfloat16

SIZES = (4, 4, 4, 2, 2)
PLACES = list(itertools.product(*(range(n) for n in SIZES)))


def number(place):
    x, zh, y, zl, core = (p % n for p, n in zip(place, SIZES))
    return (4 * x + zh) * 16 + 4 * y + 2 * zl + core


def send(array, to):
    return lax.ppermute(array, ("row", "col"), [(number(p), number(to(*p))) for p in PLACES])


POWER = 13
LIFT = 120 / POWER


def after(array, done):
    return lax.optimization_barrier((array, done))[0]


def split(norms):
    lead = lax.reduce_precision(norms, 8, 7)
    trail = lax.reduce_precision(norms - lead, 8, 7)
    return lead.astype(BF16), trail.astype(BF16), lead + trail


def inverse(norms):
    return jnp.where(norms > 0, 1.0 / jnp.where(norms > 0, norms, 1.0), 0.0)


def encode(value, rows, cols):
    ratio = value * inverse(rows)[:, None] * (inverse(cols) * 2.0**LIFT)[None, :]
    p2 = ratio * ratio
    p4 = p2 * p2
    return (p4 * p4 * (p4 * ratio)).astype(BF16)


def decode(code, rows, cols):
    wide = code.astype(F32)
    size = jnp.exp2(jnp.log2(jnp.abs(wide)) * (1.0 / POWER) - LIFT)
    return jnp.where(wide < 0, -size, size) * (rows[:, None] * cols[None, :])


def pack(code, parts):
    width = code.shape[1]
    tail = []
    for part in parts:
        part = jnp.pad(part, (0, -part.size % width))
        tail.append(part.reshape(-1, width))
    count = sum(t.shape[0] for t in tail)
    tail.append(jnp.zeros((-count % 8, width), BF16))
    return jnp.concatenate([code, *tail])


def unpack(packed, rows, sizes):
    width = packed.shape[1]
    tail, norms = packed[rows:].astype(F32), []
    for size in sizes:
        count = -(-size // width)
        lead, trail = (tail[i * count : (i + 1) * count].reshape(-1)[:size] for i in (0, 1))
        norms.append(lead + trail)
        tail = tail[2 * count :]
    return packed[:rows], *norms


def ring_reduce(part, norms, rows_of, cols_of, rows, move):
    def ship(value, s, h, norms, step):
        lead, trail, norms = split(norms)
        code = encode(value, rows_of(norms, s), cols_of(norms, s, h))
        return send(pack(code, [lead, trail]), move(step))

    def take(packed, s, h):
        code, norms = unpack(packed, rows, [norms_size])
        return decode(code, rows_of(norms, s), cols_of(norms, s, h)), norms

    norms_size = norms.size
    total = []
    far_a = ship(part(2, 0), 2, 0, norms, 1)
    direct_a = ship(part(3, 0), 3, 0, norms, 3)
    far_b = ship(part(2, 1), 2, 1, norms, 3)
    value, far_norms = take(far_a, 1, 0)
    merged_a = ship(part(1, 0) + value, 1, 0, jnp.sqrt(norms**2 + far_norms**2), 1)
    direct_b = ship(after(part(1, 1), far_a), 1, 1, norms, 1)
    value, far_norms = take(far_b, 3, 1)
    merged_b = ship(part(3, 1) + value, 3, 1, jnp.sqrt(norms**2 + far_norms**2), 3)
    for h, inputs in enumerate([(direct_a, merged_a), (direct_b, merged_b)]):
        value, squares = part(0, h), norms**2
        for packed in inputs:
            got, their = take(packed, 0, h)
            value, squares = value + got, squares + their**2
        total.append((value, jnp.sqrt(squares)))
    return total


def dot(left, right, dim):
    return lax.dot_general(
        left, right, (((dim,), (dim,)), ((), ())), preferred_element_type=F32
    )


def cut(array, start, size, dim=0):
    return lax.dynamic_slice_in_dim(array, start, size, dim)


def shards(gradient):
    rows, width = gradient.shape
    row, col = lax.axis_index("row"), lax.axis_index("col")
    x, zh = row // 4, row % 4
    y, zl, core = col // 4, col // 2 % 2, col % 2
    total_rows, total_cols = rows * 16, width * 16

    half = width // 2
    near = cut(gradient, (zh + 1) % 2 * half, half, 1)
    far = cut(gradient, zh % 2 * half, half, 1)
    near, far, gradient = lax.optimization_barrier((near, far, gradient))
    near = send(
        near,
        lambda x, zh, y, zl, core: (x, 2 * core + (zh + 1) % 2, y, zl, zh // 2),
    )
    far = send(
        far,
        lambda x, zh, y, zl, core: (x, 2 * core + zh % 2, y, zl, zh // 2),
    )

    block = width // 4

    def right_part(s, h):
        return dot(cut(gradient, (x + s) % 4 * block, block, 1), gradient[:, h * half : (h + 1) * half], 0)

    right_norms = jnp.sqrt(jnp.sum(jnp.square(gradient.astype(F32)), 0))
    right_halves = ring_reduce(
        right_part,
        right_norms,
        lambda norms, s: cut(norms, (x + s) % 4 * block, block),
        lambda norms, s, h: norms[h * half : (h + 1) * half],
        block,
        lambda step: lambda x, zh, y, zl, core: (x + step, zh, y, zl, core),
    )

    swap = lambda x, zh, y, zl, core: (x, zh, y, zl, 1 - core)
    held = jnp.stack([far, near, send(far, swap), send(near, swap)])
    place = lambda j: 2 * ((j // 2) ^ core) + (j + zh) % 2
    flat = held.reshape(LBLK, half)
    columns = lambda s, h: place((y + s) % 4) * 512 + (zl ^ h) * 256 + core * 128
    left_norms = jnp.sqrt(jnp.sum(jnp.square(flat.astype(F32)), 1))
    left_halves = ring_reduce(
        lambda s, h: dot(flat, cut(flat, columns(s, h), 128), 1),
        left_norms,
        lambda norms, s: norms,
        lambda norms, s, h: cut(norms, columns(s, h), 128),
        LBLK,
        lambda step: lambda x, zh, y, zl, core: (x, zh, y + step, zl, core),
    )

    chunk = block // 4
    right_gram = []
    for h, (value, norms) in enumerate(right_halves):
        lead, trail, norms = split(norms)
        norms_of = lambda array, s: (
            cut(array, x * block + (zh + s) % 4 * chunk, chunk),
            array[h * half : (h + 1) * half],
        )
        total = cut(value, zh * chunk, chunk)
        code = encode(value, cut(norms, x * block, block), norms_of(norms, 0)[1])
        arrived = []
        for s in (1, 3, 2):
            (lead_r, lead_c), (trail_r, trail_c) = norms_of(lead, s), norms_of(trail, s)
            piece = pack(cut(code, (zh + s) % 4 * chunk, chunk), [lead_c, trail_c, lead_r, trail_r])
            arrived.append(send(piece, lambda x, zh, y, zl, core: (x, zh + s, y, zl, core)))
        for packed in arrived:
            code, cols, rows = unpack(packed, chunk, [half, chunk])
            total += decode(code, rows, cols)
        right_gram.append(total * (1.0 / total_rows))
    right_gram = jnp.concatenate(right_gram, 1)

    left_gram = 0.0
    for h, (value, norms) in enumerate(left_halves):
        lead, trail, norms = split(norms)
        start = columns(0, h)
        code = encode(value, norms, cut(norms, start, 128))
        if h == 0:
            left_gram = cut(value, place(zh) * 512, 512)
        arrived = []
        for s in (1, 3, 2) if h == 0 else (0, 3, 1, 2):
            begin = place((zh + s) % 4) * 512
            parts = [cut(lead, begin, 512), cut(trail, begin, 512), cut(lead, start, 128), cut(trail, start, 128)]
            piece = pack(cut(code, begin, 512), parts)
            arrived.append(send(piece, lambda x, zh, y, zl, core: (x, zh + s, y, zl ^ h, core)))
        for packed in arrived:
            code, rows, cols = unpack(packed, 512, [512, 128])
            left_gram += decode(code, rows, cols)
    return (left_gram * (1.0 / total_cols), right_gram)


def solution(mesh):
    in_specs = (P("row", "col"),)
    out_specs = (P("row", "col"), P(("col", "row"), None))
    return jax.shard_map(shards, mesh=mesh, in_specs=in_specs, out_specs=out_specs, check_vma=False)
```

```python
import itertools

import jax
import jax.numpy as jnp
from jax import lax
from jax.sharding import PartitionSpec as P

LBLK = 2048
F32, BF16 = jnp.float32, jnp.bfloat16

SIZES = (4, 4, 4, 2, 2)
PLACES = list(itertools.product(*(range(n) for n in SIZES)))


def number(place):
    x, zh, y, zl, core = (p % n for p, n in zip(place, SIZES))
    return (4 * x + zh) * 16 + 4 * y + 2 * zl + core


def send(array, to):
    return lax.ppermute(array, ("row", "col"), [(number(p), number(to(*p))) for p in PLACES])


POWER = 13
LIFT = 120 / POWER
STEPS = (1, 3, 2)


def after(array, done):
    return lax.optimization_barrier((array, done))[0]


def split(norms):
    lead = lax.reduce_precision(norms, 8, 7)
    trail = lax.reduce_precision(norms - lead, 8, 7)
    return lead.astype(BF16), trail.astype(BF16), lead + trail


def inverse(norms):
    return jnp.where(norms > 0, 1.0 / jnp.where(norms > 0, norms, 1.0), 0.0)


def encode_by(value, scale):
    ratio = value * inverse(scale) * 2.0**LIFT
    p2 = ratio * ratio
    p4 = p2 * p2
    return (p4 * p4 * (p4 * ratio)).astype(BF16)


def encode(value, rows, cols):
    ratio = value * inverse(rows)[:, None] * (inverse(cols) * 2.0**LIFT)[None, :]
    p2 = ratio * ratio
    p4 = p2 * p2
    return (p4 * p4 * (p4 * ratio)).astype(BF16)


def decode_by(code, scale):
    wide = code.astype(F32)
    size = jnp.exp2(jnp.log2(jnp.abs(wide)) * (1.0 / POWER) - LIFT)
    return jnp.where(wide < 0, -size, size) * scale


def decode(code, rows, cols):
    return decode_by(code, rows[:, None] * cols[None, :])


def pack(code, parts):
    width = code.shape[1]
    tail = []
    for part in parts:
        part = jnp.pad(part, (0, -part.size % width))
        tail.append(part.reshape(-1, width))
    count = sum(t.shape[0] for t in tail)
    tail.append(jnp.zeros((-count % 8, width), BF16))
    return jnp.concatenate([code, *tail])


def unpack(packed, rows, sizes):
    width = packed.shape[1]
    tail, norms = packed[rows:].astype(F32), []
    for size in sizes:
        count = -(-size // width)
        lead, trail = (tail[i * count : (i + 1) * count].reshape(-1)[:size] for i in (0, 1))
        norms.append(lead + trail)
        tail = tail[2 * count :]
    return packed[:rows], *norms


def dot(left, right, dim):
    return lax.dot_general(
        left, right, (((dim,), (dim,)), ((), ())), preferred_element_type=F32
    )


def cut(array, start, size, dim=0):
    return lax.dynamic_slice_in_dim(array, start, size, dim)


def shards(gradient):
    rows, width = gradient.shape
    row, col = lax.axis_index("row"), lax.axis_index("col")
    x, zh = row // 4, row % 4
    y, zl, core = col // 4, col // 2 % 2, col % 2
    total_rows, total_cols = rows * 16, width * 16

    half = width // 2
    near = send(
        cut(gradient, (zh + 1) % 2 * half, half, 1),
        lambda x, zh, y, zl, core: (x, 2 * core + (zh + 1) % 2, y, zl, zh // 2),
    )
    far = cut(gradient, zh % 2 * half, half, 1)

    block, chunk, quarter = width // 4, width // 16, width // 8
    turned = [cut(gradient, (x + s) % 4 * block, block, 1) for s in range(4)]
    upper = lambda s: (x + s) % 4 > 1

    def halves(array, dim=0):
        return [lax.slice_in_dim(array, q * quarter, (q + 1) * quarter, axis=dim) for q in (0, 1)]

    def crossed(array, s, dim=0):
        low, high = halves(array, dim)
        return jnp.where(upper(s), high, low), jnp.where(upper(s), low, high)

    def right_part(s):
        rows = turned[s]
        base = dot(rows, jnp.concatenate([rows, turned[(s + 1) % 4]], 1), 0)
        more = [dot(r, c, 0) for r, c in zip(halves(rows, 1), crossed(turned[(s + 2) % 4], s, 1))]
        return base, more

    def right_scales(norms, s):
        rows, after_1, after_2 = (cut(norms, (x + s + i) % 4 * block, block) for i in range(3))
        return rows, jnp.concatenate([rows, after_1]), halves(rows), crossed(after_2, s)

    def fold(more):
        return jnp.concatenate([m[i : i + chunk] for m in more for i in (0, chunk)], 1)

    def unfold(more):
        parts = [more[:, i * quarter : (i + 1) * quarter] for i in range(4)]
        return [jnp.concatenate(parts[:2]), jnp.concatenate(parts[2:])]

    lead, trail, norms = split(jnp.sqrt(jnp.sum(jnp.square(gradient.astype(F32)), 0)))
    packed = {}
    for s in (2, 1, 3):
        (base, more), (rows, cols, more_r, more_c) = right_part(s), right_scales(norms, s)
        code = [encode(base, rows, cols), fold([encode(*m) for m in zip(more, more_r, more_c)])]
        packed[s] = pack(jnp.concatenate(code), [lead, trail])
    over_x = lambda s: send(packed[s], lambda x, zh, y, zl, core: (x + s, zh, y, zl, core))
    right_in = [over_x(2)]
    near, far, right_in, packed = lax.optimization_barrier((near, far, right_in, packed))
    far = send(far, lambda x, zh, y, zl, core: (x, 2 * core + zh % 2, y, zl, zh // 2))
    right_in += [over_x(1), over_x(3)]
    (right_base, right_more), right_squares = right_part(0), norms**2
    near, far, right_in = lax.optimization_barrier((near, far, right_in))

    swap = lambda x, zh, y, zl, core: (x, zh, y, zl, 1 - core)
    swapped = [send(far, swap), send(near, swap)]

    for packed in right_in:
        code, norms = unpack(packed, block + chunk, [width])
        rows, cols, more_r, more_c = right_scales(norms, 0)
        right_base += decode(code[:block], rows, cols)
        more = [decode(*m) for m in zip(unfold(code[block:]), more_r, more_c)]
        right_more = [m + n for m, n in zip(right_more, more)]
        right_squares += norms**2
    right_base, swapped = lax.optimization_barrier((right_base, swapped))
    lead, trail, norms = split(jnp.sqrt(right_squares))
    rows, cols, more_r, more_c = right_scales(norms, 0)

    def spread(base, more):
        low, high = more
        images = [jnp.where(upper(0), high, low).T, jnp.where(upper(0), low, high).T]
        return jnp.concatenate([base, jnp.concatenate(more), base[:, block:].T, jnp.concatenate(images)], 1)

    code = spread(encode(right_base, rows, cols), [encode(*m) for m in zip(right_more, more_r, more_c)])
    packed_z = {s: pack(cut(code, (zh + s) % 4 * chunk, chunk), [lead, trail]) for s in STEPS}
    over_z = lambda s: send(packed_z[s], lambda x, zh, y, zl, core: (x, zh + s, y, zl, core))
    right_in = [over_z(1), over_z(3)]
    far, near, swapped, packed_z = lax.optimization_barrier((far, near, swapped, packed_z))
    right_own = cut(spread(right_base, right_more), zh * chunk, chunk)

    held = jnp.stack([far, near, *swapped])
    place = lambda j: 2 * ((j // 2) ^ core) + (j + zh) % 2
    left_norms = jnp.sqrt(jnp.sum(jnp.square(held.astype(F32)), 2))
    held, left_norms = (v.reshape(4, 2, 2, 128, *v.shape[2:]) for v in (held, left_norms))

    def at(array, *index):
        for i in index:
            array = lax.dynamic_index_in_dim(array, i, 0, False)
        return array

    def rows_for(array, b):
        tail = array.shape[4:]
        picked = []
        for a in range(4):
            parity = core ^ (a > b).astype(jnp.int32)
            part = lax.dynamic_slice(
                array, (place(a), 0, parity, 0, *(0 for _ in tail)), (1, 2, 1, 128, *tail)
            )
            picked.append(part.reshape(256, *tail))
        return jnp.concatenate(picked)

    def more_rows(array, b, zl):
        m = (2 * zl + core + 1) % 4
        return at(array, place(b), m // 2, m % 2)

    def cols_for(array, b):
        return lax.dynamic_index_in_dim(at(array, place(b)), core, 1, False)

    def left_part(b):
        cols = cols_for(held, b)
        base = dot(rows_for(held, b), cols.reshape(256, half), 1)
        more = [dot(more_rows(held, b, zl), cols[zl], 1) for zl in (0, 1)]
        return base, jnp.concatenate(more, 1)

    def left_scales(norms, b):
        cols = cols_for(norms, b)
        more = [more_rows(norms, b, zl)[:, None] * cols[zl][None, :] for zl in (0, 1)]
        return rows_for(norms, b), cols.reshape(256), jnp.concatenate(more, 1)

    lead, trail, norms = split(left_norms)
    packed = {}
    for s in STEPS:
        b = (y + s) % 4
        (base, more), (scale_r, scale_c, scale_m) = left_part(b), left_scales(norms, b)
        code = jnp.concatenate([encode(base, scale_r, scale_c), encode_by(more, scale_m)])
        packed[s] = pack(code, [lead.reshape(-1), trail.reshape(-1)])
    over_y = lambda s: send(packed[s], lambda x, zh, y, zl, core: (x, zh, y + s, zl, core))
    left_in = [over_y(1), over_y(3)]
    left_in, packed, right_in, packed_z = lax.optimization_barrier((left_in, packed, right_in, packed_z))
    left_in.append(over_y(2))
    right_in.append(over_z(2))
    left_base, left_more = left_part(y)
    left_squares = norms**2

    for packed in left_in:
        code, norms = unpack(packed, 1152, [2048])
        norms = norms.reshape(4, 2, 2, 128)
        scale_r, scale_c, scale_m = left_scales(norms, y)
        left_base += decode(code[:1024], scale_r, scale_c)
        left_more += decode_by(code[1024:], scale_m)
        left_squares += norms**2
    lead, trail, norms = split(jnp.sqrt(left_squares))
    scale_r, scale_c, scale_m = left_scales(norms, y)
    code_base, code_more = encode(left_base, scale_r, scale_c), encode_by(left_more, scale_m)
    tails = [(rows_for(v, y), cols_for(v, y), [more_rows(v, y, i) for i in (0, 1)]) for v in (lead, trail)]

    def final_piece(base, more, zh, zl):
        return jnp.concatenate([lax.dynamic_slice(base, (zh * 256, zl * 128), (256, 128)), cut(more, zl * 128, 128, 1)])

    arrived = []
    for s in (1, 7, 2, 6, 3, 5, 4):
        z = (2 * zh + zl + s) % 8
        parts = []
        for tail_r, tail_c, tail_m in tails:
            parts += [cut(tail_r, z // 2 * 256, 256), jnp.where(z % 2 == 0, *tail_m), at(tail_c, z % 2)]
        packed = pack(
            final_piece(code_base, code_more, z // 2, z % 2), [jnp.concatenate(parts[:3]), jnp.concatenate(parts[3:])]
        )

        def to(x, zh, y, zl, core):
            z = (2 * zh + zl + s) % 8
            return (x, z // 2, y, z % 2, core)

        arrived.append(send(packed, to))
        if len(arrived) == 5:
            right_in = lax.optimization_barrier((right_in, packed))[0]
    left_gram = final_piece(left_base, left_more, zh, zl)
    for packed in arrived:
        code, norms = unpack(packed, 384, [512])
        left_gram += decode(code, norms[:384], norms[384:])
    left_gram = left_gram * (1.0 / total_cols)

    first, second, more = left_gram[:128], left_gram[128:256], left_gram[256:]
    diagonal = zh == y
    same, other = jnp.where(zl == 0, first, second), jnp.where(zl == 0, second, first)

    def mirror(step):
        def to(x, zh, y, zl, core):
            if zh != y:
                return (x, y, zh, zl ^ step, core ^ (zh > y))
            n = (2 * zl + core + 1 - step) % 4
            return (x, zh, y, n // 2, n % 2)

        return to

    got_same = send(jnp.where(diagonal, more, same).T, mirror(0))
    got_other = send(other.T, mirror(1))
    n = 2 * zl + core
    parity = core ^ (zh > y).astype(jnp.int32)
    blocks = jnp.zeros((4, 128, 128), F32)
    blocks = lax.dynamic_update_index_in_dim(blocks, first, parity, 0)
    blocks = lax.dynamic_update_index_in_dim(blocks, second, parity + 2, 0)
    where_same = jnp.where(diagonal, (n + 3) % 4, 2 * zl + 1 - parity)
    where_other = jnp.where(diagonal, (n + 1) % 4, 2 * (1 - zl) + 1 - parity)
    blocks = lax.dynamic_update_index_in_dim(blocks, got_same, where_same, 0)
    blocks = lax.dynamic_update_index_in_dim(blocks, jnp.where(diagonal, more, got_other), where_other, 0)
    left_gram = blocks.reshape(512, 128)

    for packed in right_in:
        code, norms = unpack(packed, chunk, [width])
        blocks = [cut(norms, (x + i) % 4 * block, block) for i in range(3)]
        rows = [cut(v, zh * chunk, chunk) for v in blocks]
        pick = lambda v, s: jnp.where(zh > 1, *crossed(v, s)[::-1])
        regions = [
            rows[0][:, None] * jnp.concatenate([blocks[0], blocks[1], pick(blocks[2], 0)])[None, :],
            rows[1][:, None] * blocks[0][None, :],
            rows[2][:, None] * pick(blocks[0], 0)[None, :],
        ]
        right_own += decode_by(code, jnp.concatenate(regions, 1))
    right_own = right_own * (1.0 / total_rows)
    ends = [2 * block, 2 * block + quarter, 3 * block + quarter, width]
    base, more, image_1, image_2 = (right_own[:, i:j] for i, j in zip([0, *ends], ends))
    image_1 = send(image_1, lambda x, zh, y, zl, core: (x + 1, zh, y, zl, core))
    image_2 = send(image_2, lambda x, zh, y, zl, core: (x + 2, zh, y, zl, core))
    low_first = (zh > 1) == upper(0)
    opposite = [jnp.where(low_first, more, image_2), jnp.where(low_first, image_2, more)]
    turned = jnp.concatenate([base, *opposite, image_1], 1)
    return (left_gram, cut(jnp.concatenate([turned, turned], 1), (4 - x) % 4 * block, width, 1))


def solution(mesh):
    in_specs = (P("row", "col"),)
    out_specs = (P("row", "col"), P(("col", "row"), None))
    return jax.shard_map(shards, mesh=mesh, in_specs=in_specs, out_specs=out_specs, check_vma=False)
```

```python
import functools
import itertools

import jax
import jax.numpy as jnp
from jax import lax
from jax.experimental import pallas as pl
from jax.experimental.pallas import tpu as pltpu
from jax.sharding import PartitionSpec as P

F32, BF16 = jnp.float32, jnp.bfloat16

SIZES = (4, 4, 4, 2, 2)
PLACES = list(itertools.product(*(range(n) for n in SIZES)))
STEPS = (1, 3, 2)
Z_STEPS = (1, 7, 2, 6, 3, 5, 4)


def number(place):
    x, zh, y, zl, core = (p % n for p, n in zip(place, SIZES))
    return (4 * x + zh) * 16 + 4 * y + 2 * zl + core


def send(array, to):
    return lax.ppermute(array, ("row", "col"), [(number(p), number(to(*p))) for p in PLACES])


POWER = 13
LIFT = 120 / POWER
LOG_LIFT = LIFT * 0.6931471805599453


def split(norms):
    lead = norms.astype(BF16).astype(F32)
    trail = (norms - lead).astype(BF16).astype(F32)
    return lead, trail, lead + trail


def inverse(norms):
    return jnp.where(norms > 0, 1.0 / jnp.where(norms > 0, norms, 1.0), 0.0)


def raised(value, rows, cols):
    ratio = value * rows * (cols * 2.0**LIFT)
    p2 = ratio * ratio
    p4 = p2 * p2
    return p4 * p4 * (p4 * ratio)


def root(code, rows, cols):
    size = jnp.exp(jnp.log(jnp.abs(code)) * (1.0 / POWER) - LOG_LIFT)
    return jnp.where(code < 0, -size, size) * (rows * cols)


def upright(row):
    parts = [row[:, i : i + 128] for i in range(0, row.shape[1], 128)]
    return jnp.concatenate([jnp.broadcast_to(p, (128, 128)).T for p in parts], 0)


def dot(left, right, dim):
    return lax.dot_general(
        left, right, (((dim,), (dim,)), ((), ())), preferred_element_type=F32
    )


def run(body, outs, scratch, *args):
    smem, vmem = pl.BlockSpec(memory_space=pltpu.SMEM), pl.BlockSpec(memory_space=pltpu.VMEM)
    return pl.pallas_call(
        body,
        out_shape=[jax.ShapeDtypeStruct(shape, dtype) for shape, dtype in outs],
        in_specs=[smem] + [vmem] * (len(args) - 1),
        out_specs=[vmem] * len(outs),
        scratch_shapes=[pltpu.VMEM(shape, dtype) for shape, dtype in scratch],
        compiler_params=pltpu.CompilerParams(vmem_limit_bytes=48 * 1024 * 1024),
    )(*args)


BLOCK, CHUNK, TILES, WINDOW, IMAGE = 448, 112, 14, 1408, 512
PIECE = WINDOW + IMAGE


def first_tile(d):
    return 7 * (d // 2) + 3 * (d % 2)


def lead_in(d):
    return 64 * (d % 2)


def tile(i):
    return pl.ds(pl.multiple_of(i * 128, 128), 128)


def fill_window(g_ref, w_ref, d):
    for t in range(11):
        w_ref[:, t * 128 : (t + 1) * 128] = g_ref[:, tile(lax.rem(first_tile(d) + t, TILES))]


def block_rows(value, d):
    return jnp.where(d % 2 == 1, value[64:512], value[:448])


def column_norms(w_ref):
    return jnp.sqrt(jnp.sum(jnp.square(w_ref[...].astype(F32)), 0, keepdims=True))


def padded(rows, count):
    rows = jnp.concatenate(rows, 0)
    return jnp.concatenate([rows, jnp.zeros((count - rows.shape[0], rows.shape[1]), F32)], 0)


def right_first(step, at_ref, g_ref, out_ref, w_ref):
    d = lax.rem(at_ref[0] + step, 4)
    fill_window(g_ref, w_ref, d)
    lead, trail, norms = split(column_norms(w_ref))
    out_ref[BLOCK:, :] = padded([lead, trail], 16).astype(BF16)
    cols = inverse(norms)
    rows = block_rows(upright(cols[:, :512]), d)
    for t in range(11):
        lanes = slice(t * 128, (t + 1) * 128)
        part = block_rows(dot(w_ref[:, :512], w_ref[:, lanes], 0), d)
        out_ref[:BLOCK, lanes] = raised(part, rows, cols[:, lanes]).astype(BF16)


def right_second(at_ref, g_ref, in_1, in_3, in_2, out_1, out_3, out_2, own_ref, w_ref, e_ref, t_ref):
    d, zh = at_ref[0], at_ref[1]
    fill_window(g_ref, w_ref, d)
    own = column_norms(w_ref)
    squares, theirs = jnp.square(own), []
    for ref in (in_1, in_3, in_2):
        tail = ref[BLOCK:, :].astype(F32)
        norms = tail[0:1] + tail[1:2]
        squares += jnp.square(norms)
        theirs.append((ref, norms, block_rows(upright(norms[:, :512]), d)))
    lead, trail, norms = split(jnp.sqrt(squares))
    cols = inverse(norms)
    rows = block_rows(upright(cols[:, :512]), d)
    begin = pl.multiple_of(lead_in(d), 64)
    e_ref[:64, :] = jnp.zeros((64, WINDOW), F32)
    e_ref[BLOCK:, :] = jnp.zeros((64, WINDOW), F32)
    for t in range(11):
        lanes = slice(t * 128, (t + 1) * 128)
        part = block_rows(dot(w_ref[:, :512], w_ref[:, lanes], 0), d)
        for ref, their_cols, their_rows in theirs:
            part += root(ref[:BLOCK, lanes].astype(F32), their_rows, their_cols[:, lanes])
        e_ref[pl.ds(begin, BLOCK), lanes] = raised(part, rows, cols[:, lanes])
    for i in range(5):
        for j in range(4):
            t_ref[i * 128 : (i + 1) * 128, j * 128 : (j + 1) * 128] = e_ref[
                j * 128 : (j + 1) * 128, 384 + i * 128 : 512 + i * 128
            ].T
    blank = jnp.zeros((1, IMAGE), F32)
    tail = [jnp.concatenate([v, blank], 1) for v in (lead, trail, norms)]
    for step, ref in ((1, out_1), (3, out_3), (2, out_2), (0, own_ref)):
        chunk = lax.rem(zh + step, 4) * CHUNK
        piece = e_ref[pl.ds(pl.multiple_of(begin + chunk, 16), CHUNK), :]
        image = t_ref[pl.ds(pl.multiple_of(64 + begin + chunk, 16), CHUNK), :]
        ref[:CHUNK, :WINDOW] = piece.astype(ref.dtype)
        ref[:CHUNK, WINDOW:] = image.astype(ref.dtype)
        ref[CHUNK:, :] = padded(tail[:2] if step else tail[2:], 16).astype(ref.dtype)


def right_third(scale, at_ref, own_ref, in_1, in_3, in_2, out_ref, image_ref, r_ref):
    d, zh = at_ref[0], at_ref[1]
    begin = pl.multiple_of(lead_in(d) + zh * CHUNK, 16)
    for i, ref in enumerate((own_ref, in_1, in_3, in_2)):
        tail = ref[CHUNK:, :].astype(F32)
        norms = (tail[0:1] if i == 0 else tail[0:1] + tail[1:2])[:, :WINDOW]
        r_ref[...] = upright(norms[:, :1024])
        rows = r_ref[pl.ds(begin, CHUNK), :]
        image_rows = r_ref[pl.ds(pl.multiple_of(448 + begin, 16), CHUNK), :]
        for t in range(15):
            lanes = slice(t * 128, (t + 1) * 128)
            code = ref[:CHUNK, lanes].astype(F32)
            if t < 11:
                to, here, part = out_ref, lanes, root(code, rows, norms[:, lanes])
            else:
                here = slice((t - 11) * 128, (t - 10) * 128)
                to, part = image_ref, root(code, image_rows, norms[:, here])
            if i == 0:
                to[:, here] = part * scale
            else:
                to[:, here] += part * scale


def right_last(at_ref, base_ref, image_ref, out_ref):
    d = at_ref[0]
    for t in range(11):
        out_ref[:, tile(lax.rem(first_tile(d) + t, TILES))] = base_ref[:, t * 128 : (t + 1) * 128]
    even = d % 2 == 0
    for t in range(3):
        part = jnp.where(
            even, image_ref[:, (t + 1) * 128 : (t + 2) * 128], image_ref[:, t * 128 : (t + 1) * 128]
        )
        out_ref[:, tile(lax.rem(first_tile(d) + 11 + t, TILES))] = part


SUB, BASE, ROWS = 128, 1024, 1152


def sub(i):
    return pl.ds(pl.multiple_of(i * SUB, SUB), SUB)


def base_subs(core, b):
    return [4 * a + (core ^ (a > b).astype(jnp.int32)) + 2 * h for a in range(4) for h in (0, 1)]


def more_sub(core, b, zl):
    return 4 * b + lax.rem(2 * zl + core + 1, 4)


def two_cols(ref, core, b):
    return jnp.concatenate([ref[pl.ds(4 * b + core + 2 * zl, 1), :] for zl in (0, 1)], 1)


def left_first(at_ref, far, near, far_2, near_2, out_1, out_3, out_2, own_ref, norm_ref, a_ref, b_ref, i_ref, s_ref):
    zh, y, core = at_ref[1], at_ref[2], at_ref[4]
    for p, ref in enumerate((far, near, far_2, near_2)):
        j = 2 * ((p // 2) ^ core) + lax.rem(p + zh, 2)
        a_ref[pl.ds(pl.multiple_of(j * 512, 512), 512), :] = ref[...]
    leads, trails, lanes = [], [], []
    for i in range(16):
        rows = slice(i * SUB, (i + 1) * SUB)
        squares = jnp.sum(jnp.square(a_ref[rows, :].astype(F32)), 1, keepdims=True)
        row = jnp.broadcast_to(jnp.sqrt(squares), (SUB, SUB)).T[0:1]
        lead, trail, norms = split(row)
        leads.append(lead), trails.append(trail), lanes.append(norms)
        i_ref[rows, :] = upright(inverse(norms))
    tail = jnp.concatenate([jnp.concatenate(leads, 0), jnp.concatenate(trails, 0)], 1).astype(BF16)
    norm_ref[...] = jnp.concatenate(lanes, 0)
    s_ref[...] = inverse(norm_ref[...])
    for step, out in ((1, out_1), (3, out_3), (2, out_2), (0, own_ref)):
        b = lax.rem(y + step, 4)
        for zl in (0, 1):
            b_ref[zl * SUB : (zl + 1) * SUB, :] = a_ref[sub(4 * b + core + 2 * zl), :]
        cols = two_cols(s_ref, core, b)
        for k, i in enumerate(base_subs(core, b)):
            part = dot(a_ref[sub(i), :], b_ref[...], 1)
            if step:
                scale = i_ref[sub(i), :]
                part = raised(part, jnp.concatenate([scale, scale], 1), cols).astype(BF16)
            out[k * SUB : (k + 1) * SUB, :] = part
        for zl in (0, 1):
            here = slice(zl * SUB, (zl + 1) * SUB)
            i = more_sub(core, b, zl)
            part = dot(a_ref[sub(i), :], b_ref[here, :], 1)
            if step:
                part = raised(part, i_ref[sub(i), :], cols[:, here]).astype(BF16)
            out[BASE:ROWS, here] = part
        if step:
            out[ROWS:, :] = tail


def left_second(at_ref, own_ref, norm_ref, in_1, in_3, in_2, *refs):
    outs, (e_ref, s_ref, lead_ref, trail_ref, n_ref) = refs[:8], refs[8:]
    zh, y, zl, core = (at_ref[i] for i in (1, 2, 3, 4))
    squares = jnp.square(norm_ref[...])
    for k, ref in enumerate((in_1, in_3, in_2)):
        tail = ref[ROWS:, :].astype(F32)
        norms = tail[:, :SUB] + tail[:, SUB:]
        squares += jnp.square(norms)
        s_ref[k] = norms
    lead_ref[...], trail_ref[...], n_ref[...] = split(jnp.sqrt(squares))
    s_ref[3] = inverse(n_ref[...])
    sources = [(ref, k) for k, ref in enumerate((in_1, in_3, in_2))]
    cols = [two_cols(s_ref.at[k], core, y) for k in range(4)]
    r = lambda k, i: upright(s_ref.at[k][pl.ds(i, 1), :])
    for j, i in enumerate(base_subs(core, y)):
        rows = slice(j * SUB, (j + 1) * SUB)
        part = own_ref[rows, :]
        for ref, k in sources:
            scale = r(k, i)
            part += root(ref[rows, :].astype(F32), jnp.concatenate([scale, scale], 1), cols[k])
        scale = r(3, i)
        e_ref[rows, :] = raised(part, jnp.concatenate([scale, scale], 1), cols[3])
    for l in (0, 1):
        here = slice(l * SUB, (l + 1) * SUB)
        i = more_sub(core, y, l)
        part = own_ref[BASE:ROWS, here]
        for ref, k in sources:
            part += root(ref[BASE:ROWS, here].astype(F32), r(k, i), cols[k][:, here])
        e_ref[BASE:ROWS, here] = raised(part, r(3, i), cols[3][:, here])
    for step, out in zip((*Z_STEPS, 0), outs):
        z = lax.rem(2 * zh + zl + step, 8)
        to_h, to_l = z // 2, lax.rem(z, 2)
        lanes = tile(to_l)
        out[:256, :] = e_ref[pl.ds(pl.multiple_of(to_h * 256, 256), 256), lanes].astype(out.dtype)
        out[256:384, :] = e_ref[BASE:ROWS, lanes].astype(out.dtype)
        first = 4 * to_h + (core ^ (to_h > y).astype(jnp.int32))
        picks = [first, first + 2, more_sub(core, y, to_l), 4 * y + 2 * to_l + core]
        tail = [ref[pl.ds(i, 1), :] for ref in ((lead_ref, trail_ref) if step else (n_ref,)) for i in picks]
        out[384:, :] = padded(tail, 16).astype(out.dtype)


def left_third(scale, at_ref, *refs):
    sources, (base_ref, more_ref, same_ref, other_ref, sum_ref) = refs[:8], refs[8:]
    zh, y, zl = at_ref[1], at_ref[2], at_ref[3]
    for k, ref in enumerate(sources):
        tail = ref[384:, :].astype(F32)
        norms = tail[0:4] if k == 0 else tail[0:4] + tail[4:8]
        for j in range(3):
            rows = slice(j * SUB, (j + 1) * SUB)
            part = root(ref[rows, :].astype(F32), upright(norms[j : j + 1]), norms[3:4]) * scale
            if k == 0:
                sum_ref[rows, :] = part
            else:
                sum_ref[rows, :] += part
    first, second, more = (sum_ref[j * SUB : (j + 1) * SUB, :] for j in range(3))
    base_ref[...] = sum_ref[:256, :]
    more_ref[...] = more
    same_ref[...] = jnp.where(zh == y, more, jnp.where(zl == 0, first, second)).T
    other_ref[...] = jnp.where(zl == 0, second, first).T


def left_last(at_ref, base_ref, more_ref, same_ref, other_ref, out_ref):
    zh, y, zl, core = (at_ref[i] for i in (1, 2, 3, 4))
    n, parity, diagonal = 2 * zl + core, core ^ (zh > y).astype(jnp.int32), zh == y
    out_ref[sub(parity), :] = base_ref[:SUB, :]
    out_ref[sub(parity + 2), :] = base_ref[SUB:, :]
    out_ref[sub(jnp.where(diagonal, lax.rem(n + 3, 4), 2 * zl + 1 - parity)), :] = same_ref[...]
    out_ref[sub(jnp.where(diagonal, lax.rem(n + 1, 4), 2 * (1 - zl) + 1 - parity)), :] = jnp.where(
        diagonal, more_ref[...], other_ref[...]
    )


def mirror(step):
    def to(x, zh, y, zl, core):
        if zh != y:
            return (x, y, zh, zl ^ step, core ^ (zh > y))
        n = (2 * zl + core + 1 - step) % 4
        return (x, zh, y, n // 2, n % 2)

    return to


def along_z(step):
    def to(x, zh, y, zl, core):
        z = (2 * zh + zl + step) % 8
        return (x, z // 2, y, z % 2, core)

    return to


def shards(gradient):
    rows, width = gradient.shape
    row, col = lax.axis_index("row"), lax.axis_index("col")
    x, zh, y, zl, core = row // 4, row % 4, col // 4, col // 2 % 2, col % 2
    at = jnp.stack([x, zh, y, zl, core, x, x, x]).astype(jnp.int32)
    barrier = lax.optimization_barrier
    half = width // 2

    cut = lambda parity: lax.dynamic_slice_in_dim(gradient, parity * half, half, 1)
    near, far = cut((zh + 1) % 2), cut(zh % 2)
    near = send(near, lambda x, zh, y, zl, core: (x, 2 * core + (zh + 1) % 2, y, zl, zh // 2))
    first = lambda s: run(
        functools.partial(right_first, s),
        [((BLOCK + 16, WINDOW), BF16)],
        [((rows, WINDOW), BF16)],
        at,
        gradient,
    )[0]
    over_x = lambda s, v: send(v, lambda x, zh, y, zl, core: (x + s, zh, y, zl, core))
    right_2 = over_x(2, first(2))
    code_1, code_3 = first(1), first(3)
    near, far, right_2, code_1, code_3 = barrier((near, far, right_2, code_1, code_3))
    far = send(far, lambda x, zh, y, zl, core: (x, 2 * core + zh % 2, y, zl, zh // 2))
    right_1, right_3 = over_x(1, code_1), over_x(3, code_3)
    near, far, right_1, right_2, right_3 = barrier((near, far, right_1, right_2, right_3))

    swap = lambda x, zh, y, zl, core: (x, zh, y, zl, 1 - core)
    far_2, near_2 = send(far, swap), send(near, swap)
    piece = (CHUNK + 16, PIECE)
    code_1, code_3, code_2, right_own = run(
        right_second,
        [(piece, BF16)] * 3 + [(piece, F32)],
        [((rows, WINDOW), BF16), ((512, WINDOW), F32), ((640, IMAGE), F32)],
        at,
        gradient,
        right_1,
        right_3,
        right_2,
    )
    over_z = lambda s, v: send(v, lambda x, zh, y, zl, core: (x, zh + s, y, zl, core))
    right_1, right_3 = over_z(1, code_1), over_z(3, code_3)

    far, near, far_2, near_2, code_2 = barrier((far, near, far_2, near_2, code_2))
    packed = (ROWS + 16, 256)
    left_1, left_3, left_2, left_own, norms = run(
        left_first,
        [(packed, BF16)] * 3 + [((ROWS, 256), F32), ((16, SUB), F32)],
        [((2048, half), BF16), ((256, half), BF16), ((2048, SUB), F32), ((16, SUB), F32)],
        at,
        far,
        near,
        far_2,
        near_2,
    )
    over_y = lambda s, v: send(v, lambda x, zh, y, zl, core: (x, zh, y + s, zl, core))
    left_1, left_3 = over_y(1, left_1), over_y(3, left_3)
    left_1, left_3, left_2, right_1, right_3, code_2 = barrier((left_1, left_3, left_2, right_1, right_3, code_2))
    left_2, right_2 = over_y(2, left_2), over_z(2, code_2)

    piece = (400, SUB)
    codes = run(
        left_second,
        [(piece, BF16)] * 7 + [(piece, F32)],
        [((ROWS, 256), F32), ((4, 16, SUB), F32)] + [((16, SUB), F32)] * 3,
        at,
        left_own,
        norms,
        left_1,
        left_3,
        left_2,
    )
    right_2, codes = barrier((right_2, codes))
    arrived = [send(code, along_z(s)) for s, code in zip(Z_STEPS, codes)]

    right_base, image = run(
        functools.partial(right_third, 1.0 / (rows * 16)),
        [((CHUNK, WINDOW), F32), ((CHUNK, IMAGE), F32)],
        [((1024, 128), F32)],
        at,
        right_own,
        right_1,
        right_3,
        right_2,
    )
    image = over_x(1, image)
    right_gram = run(right_last, [((CHUNK, width), F32)], [], at, right_base, image)[0]

    square = ((SUB, SUB), F32)
    base, more, same, other = run(
        functools.partial(left_third, 1.0 / (width * 16)),
        [((256, SUB), F32), square, square, square],
        [((384, SUB), F32)],
        at,
        codes[7],
        *arrived,
    )
    same, other = send(same, mirror(0)), send(other, mirror(1))
    left_gram = run(left_last, [((512, SUB), F32)], [], at, base, more, same, other)[0]
    return (left_gram, right_gram)


def solution(mesh):
    in_specs = (P("row", "col"),)
    out_specs = (P("row", "col"), P(("col", "row"), None))
    return jax.shard_map(shards, mesh=mesh, in_specs=in_specs, out_specs=out_specs, check_vma=False)
```

```python
import functools
import itertools

import jax
import jax.numpy as jnp
from jax import lax
from jax.experimental import pallas as pl
from jax.experimental.pallas import tpu as pltpu
from jax.sharding import PartitionSpec as P

F32, BF16 = jnp.float32, jnp.bfloat16

SIZES = (4, 4, 4, 2, 2)
PLACES = list(itertools.product(*(range(n) for n in SIZES)))
STEPS = (1, 3, 2)
Z_STEPS = (1, 7, 2, 6, 3, 5, 4)
FLOPS = 4_000_000_000


def number(place):
    x, zh, y, zl, core = (p % n for p, n in zip(place, SIZES))
    return (4 * x + zh) * 16 + 4 * y + 2 * zl + core


def send(array, to):
    return lax.ppermute(array, ("row", "col"), [(number(p), number(to(*p))) for p in PLACES])


POWER = 13
LIFT = 120 / POWER
LOG_LIFT = LIFT * 0.6931471805599453


def split(norms):
    lead = norms.astype(BF16).astype(F32)
    trail = (norms - lead).astype(BF16).astype(F32)
    return lead, trail, lead + trail


def inverse(norms):
    return jnp.where(norms > 0, 1.0 / jnp.where(norms > 0, norms, 1.0), 0.0)


def raised(value, rows, cols):
    ratio = value * rows * (cols * 2.0**LIFT)
    p2 = ratio * ratio
    p4 = p2 * p2
    return p4 * p4 * (p4 * ratio)


def root(code, rows, cols):
    size = jnp.exp(jnp.log(jnp.abs(code)) * (1.0 / POWER) - LOG_LIFT)
    return jnp.where(code < 0, -size, size) * (rows * cols)


def upright(row):
    parts = [row[:, i : i + 128] for i in range(0, row.shape[1], 128)]
    return jnp.concatenate([jnp.broadcast_to(p, (128, 128)).T for p in parts], 0)


def dot(left, right, dim):
    return lax.dot_general(
        left, right, (((dim,), (dim,)), ((), ())), preferred_element_type=F32
    )


def run(body, outs, scratch, flops, *args):
    smem, vmem = pl.BlockSpec(memory_space=pltpu.SMEM), pl.BlockSpec(memory_space=pltpu.VMEM)
    return pl.pallas_call(
        body,
        out_shape=[jax.ShapeDtypeStruct(shape, dtype) for shape, dtype in outs],
        in_specs=[smem] + [vmem] * (len(args) - 1),
        out_specs=[vmem] * len(outs),
        scratch_shapes=[pltpu.VMEM(shape, dtype) for shape, dtype in scratch],
        cost_estimate=pl.CostEstimate(
            flops=flops, bytes_accessed=sum(a.size * a.dtype.itemsize for a in args), transcendentals=0
        ),
        compiler_params=pltpu.CompilerParams(vmem_limit_bytes=48 * 1024 * 1024),
    )(*args)


BLOCK, CHUNK, TILES, WINDOW, IMAGE = 448, 112, 14, 1408, 384
WIDTH = WINDOW + IMAGE


def first_tile(d):
    return 7 * (d // 2) + 3 * (d % 2)


def lead_in(d):
    return 64 * (d % 2)


def tile(i):
    return pl.ds(pl.multiple_of(i * 128, 128), 128)


def fill_window(g_ref, w_ref, d):
    for t in range(11):
        w_ref[:, t * 128 : (t + 1) * 128] = g_ref[:, tile(lax.rem(first_tile(d) + t, TILES))]


def tile_after(d):
    return pl.ds(pl.multiple_of(128 * (d % 2), 128), IMAGE)


def block_rows(value, d):
    return jnp.where(d % 2 == 1, value[64:512], value[:448])


def column_norms(w_ref):
    return jnp.sqrt(jnp.sum(jnp.square(w_ref[...].astype(F32)), 0, keepdims=True))


def padded(rows, count):
    rows = jnp.concatenate(rows, 0)
    return jnp.concatenate([rows, jnp.zeros((count - rows.shape[0], rows.shape[1]), F32)], 0)


def right_first(step, at_ref, g_ref, out_ref, w_ref):
    d = lax.rem(at_ref[0] + step, 4)
    fill_window(g_ref, w_ref, d)
    lead, trail, norms = split(column_norms(w_ref))
    out_ref[BLOCK:, :] = padded([lead, trail], 16).astype(BF16)
    cols = inverse(norms)
    rows = block_rows(upright(cols[:, :512]), d)
    for t in range(11):
        lanes = slice(t * 128, (t + 1) * 128)
        part = block_rows(dot(w_ref[:, :512], w_ref[:, lanes], 0), d)
        out_ref[:BLOCK, lanes] = raised(part, rows, cols[:, lanes]).astype(BF16)


def right_second(at_ref, g_ref, in_1, in_3, in_2, out_1, out_3, out_2, own_ref, w_ref, e_ref, t_ref):
    d, zh = at_ref[0], at_ref[1]
    fill_window(g_ref, w_ref, d)
    own = column_norms(w_ref)
    squares, theirs = jnp.square(own), []
    for ref in (in_1, in_3, in_2):
        tail = ref[BLOCK:, :].astype(F32)
        norms = tail[0:1] + tail[1:2]
        squares += jnp.square(norms)
        theirs.append((ref, norms, block_rows(upright(norms[:, :512]), d)))
    lead, trail, norms = split(jnp.sqrt(squares))
    cols = inverse(norms)
    rows = block_rows(upright(cols[:, :512]), d)
    begin = pl.multiple_of(lead_in(d), 64)
    e_ref[:64, :] = jnp.zeros((64, WINDOW), F32)
    e_ref[BLOCK:, :] = jnp.zeros((64, WINDOW), F32)
    for t in range(11):
        lanes = slice(t * 128, (t + 1) * 128)
        part = block_rows(dot(w_ref[:, :512], w_ref[:, lanes], 0), d)
        for ref, their_cols, their_rows in theirs:
            part += root(ref[:BLOCK, lanes].astype(F32), their_rows, their_cols[:, lanes])
        e_ref[pl.ds(begin, BLOCK), lanes] = raised(part, rows, cols[:, lanes])
    for i in range(5):
        for j in range(4):
            t_ref[i * 128 : (i + 1) * 128, j * 128 : (j + 1) * 128] = e_ref[
                j * 128 : (j + 1) * 128, 384 + i * 128 : 512 + i * 128
            ].T
    tails = [jnp.concatenate([v[:, t * 128 : (t + 1) * 128] for t in range(11)], 0) for v in (lead, trail, norms)]
    for step, ref in ((1, out_1), (3, out_3), (2, out_2), (0, own_ref)):
        chunk = lax.rem(zh + step, 4) * CHUNK
        piece = e_ref[pl.ds(pl.multiple_of(begin + chunk, 16), CHUNK), :]
        image = t_ref[pl.ds(pl.multiple_of(64 + begin + chunk, 16), CHUNK), tile_after(d)]
        ref[:, :WINDOW] = piece.astype(ref.dtype)
        ref[:, WINDOW:WIDTH] = image.astype(ref.dtype)
        ref[:, WIDTH:] = padded(tails[:2] if step else tails[2:], CHUNK).astype(ref.dtype)


def right_third(scale, at_ref, own_ref, in_1, in_3, in_2, out_ref, image_ref, r_ref, n_ref):
    d, zh = at_ref[0], at_ref[1]
    begin = pl.multiple_of(lead_in(d) + zh * CHUNK, 16)
    for i, ref in enumerate((own_ref, in_1, in_3, in_2)):
        tail = ref[:, WIDTH:].astype(F32)
        n_ref[...] = tail[:11] if i == 0 else tail[:11] + tail[11:22]
        for t in range(8):
            r_ref[t * 128 : (t + 1) * 128, :] = upright(n_ref[t : t + 1, :])
        rows = r_ref[pl.ds(begin, CHUNK), :]
        image_rows = r_ref[pl.ds(pl.multiple_of(448 + begin, 16), CHUNK), :]
        for t in range(14):
            lanes = slice(t * 128, (t + 1) * 128)
            code = ref[:, lanes].astype(F32)
            if t < 11:
                to, here, part = out_ref, lanes, root(code, rows, n_ref[t : t + 1, :])
            else:
                here = slice((t - 11) * 128, (t - 10) * 128)
                cols = n_ref[pl.ds(t - 11 + lax.rem(d, 2), 1), :]
                to, part = image_ref, root(code, image_rows, cols)
            if i == 0:
                to[:, here] = part * scale
            else:
                to[:, here] += part * scale


def right_last(at_ref, base_ref, image_ref, out_ref):
    d = at_ref[0]
    for t in range(14):
        ref, i = (base_ref, t) if t < 11 else (image_ref, t - 11)
        out_ref[:, tile(lax.rem(first_tile(d) + t, TILES))] = ref[:, i * 128 : (i + 1) * 128]


SUB, BASE, ROWS = 128, 1024, 1152


def sub(i):
    return pl.ds(pl.multiple_of(i * SUB, SUB), SUB)


def base_subs(core, b):
    return [4 * a + (core ^ (a > b).astype(jnp.int32)) + 2 * h for a in range(4) for h in (0, 1)]


def more_sub(core, b, zl):
    return 4 * b + lax.rem(2 * zl + core + 1, 4)


def two_cols(ref, core, b):
    return jnp.concatenate([ref[pl.ds(4 * b + core + 2 * zl, 1), :] for zl in (0, 1)], 1)


def left_first(at_ref, far, near, far_2, near_2, out_1, out_3, out_2, own_ref, norm_ref, a_ref, b_ref, i_ref, s_ref):
    zh, y, core = at_ref[1], at_ref[2], at_ref[4]
    for p, ref in enumerate((far, near, far_2, near_2)):
        j = 2 * ((p // 2) ^ core) + lax.rem(p + zh, 2)
        a_ref[pl.ds(pl.multiple_of(j * 512, 512), 512), :] = ref[...]
    leads, trails, lanes = [], [], []
    for i in range(16):
        rows = slice(i * SUB, (i + 1) * SUB)
        squares = jnp.sum(jnp.square(a_ref[rows, :].astype(F32)), 1, keepdims=True)
        row = jnp.broadcast_to(jnp.sqrt(squares), (SUB, SUB)).T[0:1]
        lead, trail, norms = split(row)
        leads.append(lead), trails.append(trail), lanes.append(norms)
        i_ref[rows, :] = upright(inverse(norms))
    tail = jnp.concatenate([jnp.concatenate(leads, 0), jnp.concatenate(trails, 0)], 1).astype(BF16)
    norm_ref[...] = jnp.concatenate(lanes, 0)
    s_ref[...] = inverse(norm_ref[...])
    for step, out in ((1, out_1), (3, out_3), (2, out_2), (0, own_ref)):
        b = lax.rem(y + step, 4)
        for zl in (0, 1):
            b_ref[zl * SUB : (zl + 1) * SUB, :] = a_ref[sub(4 * b + core + 2 * zl), :]
        cols = two_cols(s_ref, core, b)
        for k, i in enumerate(base_subs(core, b)):
            part = dot(a_ref[sub(i), :], b_ref[...], 1)
            if step:
                scale = i_ref[sub(i), :]
                part = raised(part, jnp.concatenate([scale, scale], 1), cols).astype(BF16)
            out[k * SUB : (k + 1) * SUB, :] = part
        for zl in (0, 1):
            here = slice(zl * SUB, (zl + 1) * SUB)
            i = more_sub(core, b, zl)
            part = dot(a_ref[sub(i), :], b_ref[here, :], 1)
            if step:
                part = raised(part, i_ref[sub(i), :], cols[:, here]).astype(BF16)
            out[BASE:ROWS, here] = part
        if step:
            out[ROWS:, :] = tail


def left_second(at_ref, own_ref, norm_ref, in_1, in_3, in_2, *refs):
    outs, (e_ref, s_ref, lead_ref, trail_ref, n_ref) = refs[:8], refs[8:]
    zh, y, zl, core = (at_ref[i] for i in (1, 2, 3, 4))
    squares = jnp.square(norm_ref[...])
    for k, ref in enumerate((in_1, in_3, in_2)):
        tail = ref[ROWS:, :].astype(F32)
        norms = tail[:, :SUB] + tail[:, SUB:]
        squares += jnp.square(norms)
        s_ref[k] = norms
    lead_ref[...], trail_ref[...], n_ref[...] = split(jnp.sqrt(squares))
    s_ref[3] = inverse(n_ref[...])
    sources = [(ref, k) for k, ref in enumerate((in_1, in_3, in_2))]
    cols = [two_cols(s_ref.at[k], core, y) for k in range(4)]
    r = lambda k, i: upright(s_ref.at[k][pl.ds(i, 1), :])
    for j, i in enumerate(base_subs(core, y)):
        rows = slice(j * SUB, (j + 1) * SUB)
        part = own_ref[rows, :]
        for ref, k in sources:
            scale = r(k, i)
            part += root(ref[rows, :].astype(F32), jnp.concatenate([scale, scale], 1), cols[k])
        scale = r(3, i)
        e_ref[rows, :] = raised(part, jnp.concatenate([scale, scale], 1), cols[3])
    for l in (0, 1):
        here = slice(l * SUB, (l + 1) * SUB)
        i = more_sub(core, y, l)
        part = own_ref[BASE:ROWS, here]
        for ref, k in sources:
            part += root(ref[BASE:ROWS, here].astype(F32), r(k, i), cols[k][:, here])
        e_ref[BASE:ROWS, here] = raised(part, r(3, i), cols[3][:, here])
    for step, out in zip((*Z_STEPS, 0), outs):
        z = lax.rem(2 * zh + zl + step, 8)
        to_h, to_l = z // 2, lax.rem(z, 2)
        lanes = tile(to_l)
        out[:256, :] = e_ref[pl.ds(pl.multiple_of(to_h * 256, 256), 256), lanes].astype(out.dtype)
        out[256:384, :] = e_ref[BASE:ROWS, lanes].astype(out.dtype)
        first = 4 * to_h + (core ^ (to_h > y).astype(jnp.int32))
        picks = [first, first + 2, more_sub(core, y, to_l), 4 * y + 2 * to_l + core]
        tail = [ref[pl.ds(i, 1), :] for ref in ((lead_ref, trail_ref) if step else (n_ref,)) for i in picks]
        out[384:, :] = padded(tail, 16).astype(out.dtype)


def left_third(scale, at_ref, *refs):
    sources, (base_ref, more_ref, same_ref, other_ref, sum_ref) = refs[:8], refs[8:]
    zh, y, zl = at_ref[1], at_ref[2], at_ref[3]
    for k, ref in enumerate(sources):
        tail = ref[384:, :].astype(F32)
        norms = tail[0:4] if k == 0 else tail[0:4] + tail[4:8]
        for j in range(3):
            rows = slice(j * SUB, (j + 1) * SUB)
            part = root(ref[rows, :].astype(F32), upright(norms[j : j + 1]), norms[3:4]) * scale
            if k == 0:
                sum_ref[rows, :] = part
            else:
                sum_ref[rows, :] += part
    first, second, more = (sum_ref[j * SUB : (j + 1) * SUB, :] for j in range(3))
    base_ref[...] = sum_ref[:256, :]
    more_ref[...] = more
    same_ref[...] = jnp.where(zh == y, more, jnp.where(zl == 0, first, second)).T
    other_ref[...] = jnp.where(zl == 0, second, first).T


def left_last(at_ref, base_ref, more_ref, same_ref, other_ref, out_ref):
    zh, y, zl, core = (at_ref[i] for i in (1, 2, 3, 4))
    n, parity, diagonal = 2 * zl + core, core ^ (zh > y).astype(jnp.int32), zh == y
    out_ref[sub(parity), :] = base_ref[:SUB, :]
    out_ref[sub(parity + 2), :] = base_ref[SUB:, :]
    out_ref[sub(jnp.where(diagonal, lax.rem(n + 3, 4), 2 * zl + 1 - parity)), :] = same_ref[...]
    out_ref[sub(jnp.where(diagonal, lax.rem(n + 1, 4), 2 * (1 - zl) + 1 - parity)), :] = jnp.where(
        diagonal, more_ref[...], other_ref[...]
    )


def mirror(step):
    def to(x, zh, y, zl, core):
        if zh != y:
            return (x, y, zh, zl ^ step, core ^ (zh > y))
        n = (2 * zl + core + 1 - step) % 4
        return (x, zh, y, n // 2, n % 2)

    return to


def along_z(step):
    def to(x, zh, y, zl, core):
        z = (2 * zh + zl + step) % 8
        return (x, z // 2, y, z % 2, core)

    return to


def shards(gradient):
    rows, width = gradient.shape
    row, col = lax.axis_index("row"), lax.axis_index("col")
    x, zh, y, zl, core = row // 4, row % 4, col // 4, col // 2 % 2, col % 2
    at = jnp.stack([x, zh, y, zl, core, x, x, x]).astype(jnp.int32)
    barrier = lax.optimization_barrier
    half = width // 2

    cut = lambda parity: lax.dynamic_slice_in_dim(gradient, parity * half, half, 1)
    near, far, gradient = barrier((cut((zh + 1) % 2), cut(zh % 2), gradient))
    near = send(near, lambda x, zh, y, zl, core: (x, 2 * core + (zh + 1) % 2, y, zl, zh // 2))
    far = send(far, lambda x, zh, y, zl, core: (x, 2 * core + zh % 2, y, zl, zh // 2))

    first = lambda s: run(
        functools.partial(right_first, s),
        [((BLOCK + 16, WINDOW), BF16)],
        [((rows, WINDOW), BF16)],
        FLOPS,
        at,
        gradient,
    )[0]
    over_x = lambda s, v: send(v, lambda x, zh, y, zl, core: (x + s, zh, y, zl, core))
    right_1, right_3, right_2 = (over_x(s, first(s)) for s in STEPS)

    swap = lambda x, zh, y, zl, core: (x, zh, y, zl, 1 - core)
    far_2, near_2 = send(far, swap), send(near, swap)
    packed = (ROWS + 16, 256)
    left_1, left_3, left_2, left_own, norms = run(
        left_first,
        [(packed, BF16)] * 3 + [((ROWS, 256), F32), ((16, SUB), F32)],
        [((2048, half), BF16), ((256, half), BF16), ((2048, SUB), F32), ((16, SUB), F32)],
        FLOPS,
        at,
        far,
        near,
        far_2,
        near_2,
    )
    right_1, right_3, right_2, _ = barrier((right_1, right_3, right_2, left_1))
    over_y = lambda s, v: send(v, lambda x, zh, y, zl, core: (x, zh, y + s, zl, core))
    left_1, left_3, left_2 = over_y(1, left_1), over_y(3, left_3), over_y(2, left_2)

    piece = (CHUNK, WIDTH + 128)
    code_1, code_3, code_2, right_own = run(
        right_second,
        [(piece, BF16)] * 3 + [(piece, F32)],
        [((rows, WINDOW), BF16), ((512, WINDOW), F32), ((640, 512), F32)],
        FLOPS,
        at,
        gradient,
        right_1,
        right_3,
        right_2,
    )
    over_z = lambda s, v: send(v, lambda x, zh, y, zl, core: (x, zh + s, y, zl, core))
    right_1, right_3 = over_z(1, code_1), over_z(3, code_3)
    left_1, left_3, left_2, right_1, right_3, code_2 = barrier((left_1, left_3, left_2, right_1, right_3, code_2))
    right_2 = over_z(2, code_2)

    piece = (400, SUB)
    codes = run(
        left_second,
        [(piece, BF16)] * 7 + [(piece, F32)],
        [((ROWS, 256), F32), ((4, 16, SUB), F32)] + [((16, SUB), F32)] * 3,
        FLOPS,
        at,
        left_own,
        norms,
        left_1,
        left_3,
        left_2,
    )
    right_2, _ = barrier((right_2, codes))
    arrived = [send(code, along_z(s)) for s, code in zip(Z_STEPS, codes)]

    right_base, image = run(
        functools.partial(right_third, 1.0 / (rows * 16)),
        [((CHUNK, WINDOW), F32), ((CHUNK, IMAGE), F32)],
        [((1024, 128), F32), ((11, 128), F32)],
        FLOPS,
        at,
        right_own,
        right_1,
        right_3,
        right_2,
    )
    image = over_x(1, image)
    right_gram = run(right_last, [((CHUNK, width), F32)], [], FLOPS, at, right_base, image)[0]

    square = ((SUB, SUB), F32)
    base, more, same, other = run(
        functools.partial(left_third, 1.0 / (width * 16)),
        [((256, SUB), F32), square, square, square],
        [((384, SUB), F32)],
        FLOPS,
        at,
        codes[7],
        *arrived,
    )
    same, other = send(same, mirror(0)), send(other, mirror(1))
    left_gram = run(left_last, [((512, SUB), F32)], [], FLOPS, at, base, more, same, other)[0]
    return (left_gram, right_gram)


def solution(mesh):
    in_specs = (P("row", "col"),)
    out_specs = (P("row", "col"), P(("col", "row"), None))
    return jax.shard_map(shards, mesh=mesh, in_specs=in_specs, out_specs=out_specs, check_vma=False)
```

```python
import functools
import itertools

import jax
import jax.numpy as jnp
from jax import lax
from jax.experimental import pallas as pl
from jax.experimental.pallas import tpu as pltpu
from jax.sharding import PartitionSpec as P

F32, BF16 = jnp.float32, jnp.bfloat16

SIZES = (4, 4, 4, 2, 2)
PLACES = list(itertools.product(*(range(n) for n in SIZES)))
STEPS = (1, 3, 2)
Z_STEPS = (1, 7, 2, 6, 3, 5, 4)
FLOPS = 4_000_000_000


def number(place):
    x, zh, y, zl, core = (p % n for p, n in zip(place, SIZES))
    return (4 * x + zh) * 16 + 4 * y + 2 * zl + core


def send(array, to):
    return lax.ppermute(array, ("row", "col"), [(number(p), number(to(*p))) for p in PLACES])


POWER = 13
LIFT = 120 / POWER
LOG_LIFT = LIFT * 0.6931471805599453


def split(norms):
    lead = norms.astype(BF16).astype(F32)
    trail = (norms - lead).astype(BF16).astype(F32)
    return lead, trail, lead + trail


def inverse(norms):
    return jnp.where(norms > 0, 1.0 / jnp.where(norms > 0, norms, 1.0), 0.0)


def raised(value, rows, cols):
    ratio = value * rows * (cols * 2.0**LIFT)
    p2 = ratio * ratio
    p4 = p2 * p2
    return p4 * p4 * (p4 * ratio)


def root(code, rows, cols):
    size = jnp.exp(jnp.log(jnp.abs(code)) * (1.0 / POWER) - LOG_LIFT)
    return jnp.where(code < 0, -size, size) * (rows * cols)


def upright(row):
    parts = [row[:, i : i + 128] for i in range(0, row.shape[1], 128)]
    return jnp.concatenate([jnp.broadcast_to(p, (128, 128)).T for p in parts], 0)


def dot(left, right, dim):
    return lax.dot_general(
        left, right, (((dim,), (dim,)), ((), ())), preferred_element_type=F32
    )


def run(body, outs, scratch, flops, *args):
    smem, vmem = pl.BlockSpec(memory_space=pltpu.SMEM), pl.BlockSpec(memory_space=pltpu.VMEM)
    return pl.pallas_call(
        body,
        out_shape=[jax.ShapeDtypeStruct(shape, dtype) for shape, dtype in outs],
        in_specs=[smem] + [vmem] * (len(args) - 1),
        out_specs=[vmem] * len(outs),
        scratch_shapes=[pltpu.VMEM(shape, dtype) for shape, dtype in scratch],
        cost_estimate=pl.CostEstimate(
            flops=flops, bytes_accessed=sum(a.size * a.dtype.itemsize for a in args), transcendentals=0
        ),
        compiler_params=pltpu.CompilerParams(vmem_limit_bytes=48 * 1024 * 1024),
    )(*args)


BLOCK, CHUNK, TILES, WINDOW, IMAGE = 448, 112, 14, 1408, 384
WIDTH = WINDOW + IMAGE


def first_tile(d):
    return 7 * (d // 2) + 3 * (d % 2)


def lead_in(d):
    return 64 * (d % 2)


def tile(i):
    return pl.ds(pl.multiple_of(i * 128, 128), 128)


HALF_ROWS = BLOCK // 2
PARTS = [slice(i, min(i + 256, WINDOW)) for i in range(0, WINDOW, 256)]


def fill_window(g_ref, w_ref, l_ref, d):
    for t in range(11):
        w_ref[:, t * 128 : (t + 1) * 128] = g_ref[:, tile(lax.rem(first_tile(d) + t, TILES))]
    l_ref[...] = w_ref[:, :512].T


def tile_after(d):
    return pl.ds(pl.multiple_of(128 * (d % 2), 128), IMAGE)


def column_norms(w_ref):
    return jnp.sqrt(jnp.sum(jnp.square(w_ref[...].astype(F32)), 0, keepdims=True))


def padded(rows, count):
    rows = jnp.concatenate(rows, 0)
    return jnp.concatenate([rows, jnp.zeros((count - rows.shape[0], rows.shape[1]), F32)], 0)


def rows_of(r_ref, norms, d, start=0, count=BLOCK):
    r_ref[...] = upright(norms[:, :512])
    return r_ref[pl.ds(pl.multiple_of(lead_in(d) + start, 16), count), :]


def wide(rows, lanes):
    return rows if lanes.stop - lanes.start == 128 else jnp.concatenate([rows, rows], 1)


def product(l_ref, w_ref, lanes, d):
    left = l_ref[pl.ds(pl.multiple_of(lead_in(d), 64), BLOCK), :]
    return jnp.dot(left, w_ref[:, lanes], preferred_element_type=F32)


def right_far(at_ref, g_ref, out_a, out_b, w_ref, l_ref, r_ref):
    d = lax.rem(at_ref[0] + 2, 4)
    fill_window(g_ref, w_ref, l_ref, d)
    lead, trail, norms = split(column_norms(w_ref))
    tail = padded([lead, trail], 16).astype(BF16)
    cols = inverse(norms)
    rows = rows_of(r_ref, cols, d)
    for ref in (out_a, out_b):
        ref[HALF_ROWS:, :] = tail
    for lanes in PARTS:
        code = raised(product(l_ref, w_ref, lanes, d), wide(rows, lanes), cols[:, lanes]).astype(BF16)
        out_a[:HALF_ROWS, lanes] = code[:HALF_ROWS]
        out_b[:HALF_ROWS, lanes] = code[HALF_ROWS:]


def right_near(step, at_ref, g_ref, in_ref, out_ref, w_ref, l_ref, r_ref, p_ref):
    d = lax.rem(at_ref[0] + step, 4)
    start = 0 if step == 1 else HALF_ROWS
    fill_window(g_ref, w_ref, l_ref, d)
    tail = in_ref[HALF_ROWS:, :].astype(F32)
    theirs = tail[0:1] + tail[1:2]
    their_rows = rows_of(r_ref, theirs, d, start, HALF_ROWS)
    lead, trail, norms = split(jnp.sqrt(jnp.square(column_norms(w_ref)) + jnp.square(theirs)))
    out_ref[BLOCK:, :] = padded([lead, trail], 16).astype(BF16)
    cols = inverse(norms)
    rows = rows_of(r_ref, cols, d)
    here = slice(start, start + HALF_ROWS)
    for lanes in PARTS:
        part = p_ref.at[:, : lanes.stop - lanes.start]
        part[...] = product(l_ref, w_ref, lanes, d)
        part[here, :] += root(in_ref[:HALF_ROWS, lanes].astype(F32), wide(their_rows, lanes), theirs[:, lanes])
        out_ref[:BLOCK, lanes] = raised(part[...], wide(rows, lanes), cols[:, lanes]).astype(BF16)


def right_second(at_ref, g_ref, in_1, in_3, out_1, out_3, out_2, own_ref, w_ref, l_ref, r_ref, e_ref, t_ref):
    d, zh = at_ref[0], at_ref[1]
    fill_window(g_ref, w_ref, l_ref, d)
    squares, theirs = jnp.square(column_norms(w_ref)), []
    for ref in (in_1, in_3):
        tail = ref[BLOCK:, :].astype(F32)
        norms = tail[0:1] + tail[1:2]
        squares += jnp.square(norms)
        theirs.append((ref, norms, rows_of(r_ref, norms, d)))
    lead, trail, norms = split(jnp.sqrt(squares))
    cols = inverse(norms)
    rows = rows_of(r_ref, cols, d)
    begin = pl.multiple_of(lead_in(d), 64)
    e_ref[:64, :] = jnp.zeros((64, WINDOW), F32)
    e_ref[BLOCK:, :] = jnp.zeros((64, WINDOW), F32)
    for lanes in PARTS:
        part = product(l_ref, w_ref, lanes, d)
        for ref, their_cols, their_rows in theirs:
            part += root(ref[:BLOCK, lanes].astype(F32), wide(their_rows, lanes), their_cols[:, lanes])
        e_ref[pl.ds(begin, BLOCK), lanes] = raised(part, wide(rows, lanes), cols[:, lanes])
    for i in range(5):
        for j in range(4):
            t_ref[i * 128 : (i + 1) * 128, j * 128 : (j + 1) * 128] = e_ref[
                j * 128 : (j + 1) * 128, 384 + i * 128 : 512 + i * 128
            ].T
    tails = [jnp.concatenate([v[:, t * 128 : (t + 1) * 128] for t in range(11)], 0) for v in (lead, trail, norms)]
    for step, ref in ((1, out_1), (3, out_3), (2, out_2), (0, own_ref)):
        chunk = lax.rem(zh + step, 4) * CHUNK
        piece = e_ref[pl.ds(pl.multiple_of(begin + chunk, 16), CHUNK), :]
        image = t_ref[pl.ds(pl.multiple_of(64 + begin + chunk, 16), CHUNK), tile_after(d)]
        ref[:, :WINDOW] = piece.astype(ref.dtype)
        ref[:, WINDOW:WIDTH] = image.astype(ref.dtype)
        ref[:, WIDTH:] = padded(tails[:2] if step else tails[2:], CHUNK).astype(ref.dtype)


def right_third(scale, at_ref, own_ref, in_1, in_3, in_2, out_ref, image_ref, r_ref, n_ref):
    d, zh = at_ref[0], at_ref[1]
    begin = pl.multiple_of(lead_in(d) + zh * CHUNK, 16)
    for i, ref in enumerate((own_ref, in_1, in_3, in_2)):
        tail = ref[:, WIDTH:].astype(F32)
        n_ref[...] = tail[:11] if i == 0 else tail[:11] + tail[11:22]
        for t in range(8):
            r_ref[t * 128 : (t + 1) * 128, :] = upright(n_ref[t : t + 1, :])
        rows = r_ref[pl.ds(begin, CHUNK), :]
        image_rows = r_ref[pl.ds(pl.multiple_of(448 + begin, 16), CHUNK), :]
        for t in range(14):
            lanes = slice(t * 128, (t + 1) * 128)
            code = ref[:, lanes].astype(F32)
            if t < 11:
                to, here, part = out_ref, lanes, root(code, rows, n_ref[t : t + 1, :])
            else:
                here = slice((t - 11) * 128, (t - 10) * 128)
                cols = n_ref[pl.ds(t - 11 + lax.rem(d, 2), 1), :]
                to, part = image_ref, root(code, image_rows, cols)
            if i == 0:
                to[:, here] = part * scale
            else:
                to[:, here] += part * scale


def right_last(at_ref, base_ref, image_ref, out_ref):
    d = at_ref[0]
    for t in range(14):
        ref, i = (base_ref, t) if t < 11 else (image_ref, t - 11)
        out_ref[:, tile(lax.rem(first_tile(d) + t, TILES))] = ref[:, i * 128 : (i + 1) * 128]


SUB, BASE, ROWS = 128, 1024, 1152


def sub(i):
    return pl.ds(pl.multiple_of(i * SUB, SUB), SUB)


def base_subs(core, b):
    return [4 * a + (core ^ (a > b).astype(jnp.int32)) + 2 * h for a in range(4) for h in (0, 1)]


def slot(i):
    return i // 4 * 4 + 2 * (i % 2) + i // 2 % 2


def more_sub(core, b, zl):
    return 4 * b + lax.rem(2 * zl + core + 1, 4)


def two_cols(ref, core, b):
    return jnp.concatenate([ref[pl.ds(4 * b + core + 2 * zl, 1), :] for zl in (0, 1)], 1)


def left_first(at_ref, far, near, far_2, near_2, out_1, out_3, out_2, own_ref, norm_ref, a_ref, b_ref, i_ref, s_ref):
    zh, y, core = at_ref[1], at_ref[2], at_ref[4]
    for p, ref in enumerate((far, near, far_2, near_2)):
        j = 2 * ((p // 2) ^ core) + lax.rem(p + zh, 2)
        for m in range(4):
            a_ref[sub(4 * j + slot(m)), :] = ref[m * SUB : (m + 1) * SUB, :]
    leads, trails, lanes = [], [], []
    for i in range(16):
        rows = slice(slot(i) * SUB, (slot(i) + 1) * SUB)
        squares = jnp.sum(jnp.square(a_ref[rows, :].astype(F32)), 1, keepdims=True)
        row = jnp.broadcast_to(jnp.sqrt(squares), (SUB, SUB)).T[0:1]
        lead, trail, norms = split(row)
        leads.append(lead), trails.append(trail), lanes.append(norms)
        i_ref[rows, :] = upright(inverse(norms))
    tail = jnp.concatenate([jnp.concatenate(leads, 0), jnp.concatenate(trails, 0)], 1).astype(BF16)
    norm_ref[...] = jnp.concatenate(lanes, 0)
    s_ref[...] = inverse(norm_ref[...])
    for step, out in ((1, out_1), (3, out_3), (2, out_2), (0, own_ref)):
        b = lax.rem(y + step, 4)
        for zl in (0, 1):
            b_ref[zl * SUB : (zl + 1) * SUB, :] = a_ref[sub(slot(4 * b + core + 2 * zl)), :]
        cols = two_cols(s_ref, core, b)
        for k, i in enumerate(base_subs(core, b)[::2]):
            pair = pl.ds(pl.multiple_of(slot(i) * SUB, 2 * SUB), 2 * SUB)
            part = dot(a_ref[pair, :], b_ref[...], 1)
            if step:
                scale = i_ref[pair, :]
                part = raised(part, jnp.concatenate([scale, scale], 1), cols).astype(BF16)
            out[k * 2 * SUB : (k + 1) * 2 * SUB, :] = part
        for zl in (0, 1):
            here = slice(zl * SUB, (zl + 1) * SUB)
            i = slot(more_sub(core, b, zl))
            part = dot(a_ref[sub(i), :], b_ref[here, :], 1)
            if step:
                part = raised(part, i_ref[sub(i), :], cols[:, here]).astype(BF16)
            out[BASE:ROWS, here] = part
        if step:
            out[ROWS:, :] = tail


def left_second(at_ref, own_ref, norm_ref, in_1, in_3, in_2, *refs):
    outs, (e_ref, s_ref, lead_ref, trail_ref, n_ref) = refs[:8], refs[8:]
    zh, y, zl, core = (at_ref[i] for i in (1, 2, 3, 4))
    squares = jnp.square(norm_ref[...])
    for k, ref in enumerate((in_1, in_3, in_2)):
        tail = ref[ROWS:, :].astype(F32)
        norms = tail[:, :SUB] + tail[:, SUB:]
        squares += jnp.square(norms)
        s_ref[k] = norms
    lead_ref[...], trail_ref[...], n_ref[...] = split(jnp.sqrt(squares))
    s_ref[3] = inverse(n_ref[...])
    sources = [(ref, k) for k, ref in enumerate((in_1, in_3, in_2))]
    cols = [two_cols(s_ref.at[k], core, y) for k in range(4)]
    r = lambda k, i: upright(s_ref.at[k][pl.ds(i, 1), :])
    for j, i in enumerate(base_subs(core, y)):
        rows = slice(j * SUB, (j + 1) * SUB)
        part = own_ref[rows, :]
        for ref, k in sources:
            scale = r(k, i)
            part += root(ref[rows, :].astype(F32), jnp.concatenate([scale, scale], 1), cols[k])
        scale = r(3, i)
        e_ref[rows, :] = raised(part, jnp.concatenate([scale, scale], 1), cols[3])
    for l in (0, 1):
        here = slice(l * SUB, (l + 1) * SUB)
        i = more_sub(core, y, l)
        part = own_ref[BASE:ROWS, here]
        for ref, k in sources:
            part += root(ref[BASE:ROWS, here].astype(F32), r(k, i), cols[k][:, here])
        e_ref[BASE:ROWS, here] = raised(part, r(3, i), cols[3][:, here])
    for step, out in zip((*Z_STEPS, 0), outs):
        z = lax.rem(2 * zh + zl + step, 8)
        to_h, to_l = z // 2, lax.rem(z, 2)
        lanes = tile(to_l)
        out[:256, :] = e_ref[pl.ds(pl.multiple_of(to_h * 256, 256), 256), lanes].astype(out.dtype)
        out[256:384, :] = e_ref[BASE:ROWS, lanes].astype(out.dtype)
        first = 4 * to_h + (core ^ (to_h > y).astype(jnp.int32))
        picks = [first, first + 2, more_sub(core, y, to_l), 4 * y + 2 * to_l + core]
        tail = [ref[pl.ds(i, 1), :] for ref in ((lead_ref, trail_ref) if step else (n_ref,)) for i in picks]
        out[384:, :] = padded(tail, 16).astype(out.dtype)


def left_third(scale, at_ref, *refs):
    sources, (base_ref, more_ref, same_ref, other_ref, sum_ref) = refs[:8], refs[8:]
    zh, y, zl = at_ref[1], at_ref[2], at_ref[3]
    for k, ref in enumerate(sources):
        tail = ref[384:, :].astype(F32)
        norms = tail[0:4] if k == 0 else tail[0:4] + tail[4:8]
        for j in range(3):
            rows = slice(j * SUB, (j + 1) * SUB)
            part = root(ref[rows, :].astype(F32), upright(norms[j : j + 1]), norms[3:4]) * scale
            if k == 0:
                sum_ref[rows, :] = part
            else:
                sum_ref[rows, :] += part
    first, second, more = (sum_ref[j * SUB : (j + 1) * SUB, :] for j in range(3))
    base_ref[...] = sum_ref[:256, :]
    more_ref[...] = more
    same_ref[...] = jnp.where(zh == y, more, jnp.where(zl == 0, first, second)).T
    other_ref[...] = jnp.where(zl == 0, second, first).T


def left_last(at_ref, base_ref, more_ref, same_ref, other_ref, out_ref):
    zh, y, zl, core = (at_ref[i] for i in (1, 2, 3, 4))
    n, parity, diagonal = 2 * zl + core, core ^ (zh > y).astype(jnp.int32), zh == y
    out_ref[sub(parity), :] = base_ref[:SUB, :]
    out_ref[sub(parity + 2), :] = base_ref[SUB:, :]
    out_ref[sub(jnp.where(diagonal, lax.rem(n + 3, 4), 2 * zl + 1 - parity)), :] = same_ref[...]
    out_ref[sub(jnp.where(diagonal, lax.rem(n + 1, 4), 2 * (1 - zl) + 1 - parity)), :] = jnp.where(
        diagonal, more_ref[...], other_ref[...]
    )


def mirror(step):
    def to(x, zh, y, zl, core):
        if zh != y:
            return (x, y, zh, zl ^ step, core ^ (zh > y))
        n = (2 * zl + core + 1 - step) % 4
        return (x, zh, y, n // 2, n % 2)

    return to


def along_z(step):
    def to(x, zh, y, zl, core):
        z = (2 * zh + zl + step) % 8
        return (x, z // 2, y, z % 2, core)

    return to


def shards(gradient):
    rows, width = gradient.shape
    row, col = lax.axis_index("row"), lax.axis_index("col")
    x, zh, y, zl, core = row // 4, row % 4, col // 4, col // 2 % 2, col % 2
    at = jnp.stack([x, zh, y, zl, core, x, x, x]).astype(jnp.int32)
    barrier = lax.optimization_barrier
    half = width // 2

    cut = lambda parity: lax.dynamic_slice_in_dim(gradient, parity * half, half, 1)
    near, far, gradient = barrier((cut((zh + 1) % 2), cut(zh % 2), gradient))
    near = send(near, lambda x, zh, y, zl, core: (x, 2 * core + (zh + 1) % 2, y, zl, zh // 2))
    far = send(far, lambda x, zh, y, zl, core: (x, 2 * core + zh % 2, y, zl, zh // 2))

    window = [((rows, WINDOW), BF16), ((512, 512), BF16), ((512, 128), F32)]
    half_part, whole_part = ((HALF_ROWS + 16, WINDOW), BF16), ((BLOCK + 16, WINDOW), BF16)
    over_x = lambda s, v: send(v, lambda x, zh, y, zl, core: (x + s, zh, y, zl, core))
    far_1, far_3 = run(right_far, [half_part] * 2, window, FLOPS, at, gradient)
    far_1, far_3 = over_x(1, far_1), over_x(3, far_3)
    add = lambda s, v: run(
        functools.partial(right_near, s), [whole_part], window + [((BLOCK, 256), F32)], FLOPS, at, gradient, v
    )[0]
    code_1, code_3 = add(1, far_1), add(3, far_3)
    right_1, right_3 = over_x(1, code_1), over_x(3, code_3)
    near, far, _ = barrier((near, far, (code_1, code_3)))

    swap = lambda x, zh, y, zl, core: (x, zh, y, zl, 1 - core)
    far_2, near_2 = send(far, swap), send(near, swap)
    packed = (ROWS + 16, 256)
    left_1, left_3, left_2, left_own, norms = run(
        left_first,
        [(packed, BF16)] * 3 + [((ROWS, 256), F32), ((16, SUB), F32)],
        [((2048, half), BF16), ((256, half), BF16), ((2048, SUB), F32), ((16, SUB), F32)],
        FLOPS,
        at,
        far,
        near,
        far_2,
        near_2,
    )
    right_1, right_3, _ = barrier((right_1, right_3, left_1))
    over_y = lambda s, v: send(v, lambda x, zh, y, zl, core: (x, zh, y + s, zl, core))
    left_1, left_3, left_2 = over_y(1, left_1), over_y(3, left_3), over_y(2, left_2)

    piece = (CHUNK, WIDTH + 128)
    code_1, code_3, code_2, right_own = run(
        right_second,
        [(piece, BF16)] * 3 + [(piece, F32)],
        window + [((512, WINDOW), F32), ((640, 512), F32)],
        FLOPS,
        at,
        gradient,
        right_1,
        right_3,
    )
    over_z = lambda s, v: send(v, lambda x, zh, y, zl, core: (x, zh + s, y, zl, core))
    right_2, right_1 = over_z(2, code_2), over_z(1, code_1)
    code_3, _ = barrier((code_3, left_3))
    right_3 = over_z(3, code_3)
    left_1, left_3, left_2, right_1, right_3, right_2 = barrier(
        (left_1, left_3, left_2, right_1, right_3, right_2)
    )

    piece = (400, SUB)
    codes = run(
        left_second,
        [(piece, BF16)] * 7 + [(piece, F32)],
        [((ROWS, 256), F32), ((4, 16, SUB), F32)] + [((16, SUB), F32)] * 3,
        FLOPS,
        at,
        left_own,
        norms,
        left_1,
        left_3,
        left_2,
    )
    right_1, right_3, _ = barrier((right_1, right_3, codes))
    arrived = [send(code, along_z(s)) for s, code in zip(Z_STEPS, codes)]

    right_base, image = run(
        functools.partial(right_third, 1.0 / (rows * 16)),
        [((CHUNK, WINDOW), F32), ((CHUNK, IMAGE), F32)],
        [((1024, 128), F32), ((11, 128), F32)],
        FLOPS,
        at,
        right_own,
        right_1,
        right_3,
        right_2,
    )
    image = over_x(1, image)
    right_gram = run(right_last, [((CHUNK, width), F32)], [], FLOPS, at, right_base, image)[0]

    square = ((SUB, SUB), F32)
    base, more, same, other = run(
        functools.partial(left_third, 1.0 / (width * 16)),
        [((256, SUB), F32), square, square, square],
        [((384, SUB), F32)],
        FLOPS,
        at,
        codes[7],
        *arrived,
    )
    same, other = send(same, mirror(0)), send(other, mirror(1))
    left_gram = run(left_last, [((512, SUB), F32)], [], FLOPS, at, base, more, same, other)[0]
    return (left_gram, right_gram)


def solution(mesh):
    in_specs = (P("row", "col"),)
    out_specs = (P("row", "col"), P(("col", "row"), None))
    return jax.shard_map(shards, mesh=mesh, in_specs=in_specs, out_specs=out_specs, check_vma=False)
```

```python
import functools
import itertools

import jax
import jax.numpy as jnp
from jax import lax
from jax.experimental import pallas as pl
from jax.experimental.pallas import tpu as pltpu
from jax.sharding import PartitionSpec as P

F32, BF16 = jnp.float32, jnp.bfloat16

SIZES = (4, 4, 4, 2, 2)
PLACES = list(itertools.product(*(range(n) for n in SIZES)))
STEPS = (1, 3, 2)
Z_STEPS = (1, 7, 2, 6, 3, 5, 4)
FLOPS = 4_000_000_000


def number(place):
    x, zh, y, zl, core = (p % n for p, n in zip(place, SIZES))
    return (4 * x + zh) * 16 + 4 * y + 2 * zl + core


def send(array, to):
    return lax.ppermute(array, ("row", "col"), [(number(p), number(to(*p))) for p in PLACES])


POWER = 13
LIFT = 120 / POWER
LOG_LIFT = LIFT * 0.6931471805599453


def split(norms):
    lead = norms.astype(BF16).astype(F32)
    trail = (norms - lead).astype(BF16).astype(F32)
    return lead, trail, lead + trail


def inverse(norms):
    return jnp.where(norms > 0, 1.0 / jnp.where(norms > 0, norms, 1.0), 0.0)


def raised(value, rows, cols):
    ratio = value * rows * (cols * 2.0**LIFT)
    p2 = ratio * ratio
    p4 = p2 * p2
    return p4 * p4 * (p4 * ratio)


def root(code, rows, cols):
    size = jnp.exp(jnp.log(jnp.abs(code)) * (1.0 / POWER) - LOG_LIFT)
    return jnp.where(code < 0, -size, size) * (rows * cols)


def upright(row):
    parts = [row[:, i : i + 128] for i in range(0, row.shape[1], 128)]
    return jnp.concatenate([jnp.broadcast_to(p, (128, 128)).T for p in parts], 0)


def dot(left, right, dim):
    return lax.dot_general(
        left, right, (((dim,), (dim,)), ((), ())), preferred_element_type=F32
    )


def run(body, outs, scratch, flops, *args):
    smem, vmem = pl.BlockSpec(memory_space=pltpu.SMEM), pl.BlockSpec(memory_space=pltpu.VMEM)
    return pl.pallas_call(
        body,
        out_shape=[jax.ShapeDtypeStruct(shape, dtype) for shape, dtype in outs],
        in_specs=[smem] + [vmem] * (len(args) - 1),
        out_specs=[vmem] * len(outs),
        scratch_shapes=[pltpu.VMEM(shape, dtype) for shape, dtype in scratch],
        cost_estimate=pl.CostEstimate(
            flops=flops, bytes_accessed=sum(a.size * a.dtype.itemsize for a in args), transcendentals=0
        ),
        compiler_params=pltpu.CompilerParams(vmem_limit_bytes=48 * 1024 * 1024),
    )(*args)


BLOCK, CHUNK, TILES, WINDOW, IMAGE = 448, 112, 14, 1408, 384
WIDTH = WINDOW + IMAGE


def first_tile(d):
    return 7 * (d // 2) + 3 * (d % 2)


def lead_in(d):
    return 64 * (d % 2)


def tile(i):
    return pl.ds(pl.multiple_of(i * 128, 128), 128)


HALF_ROWS = BLOCK // 2
PARTS = [slice(i, min(i + 256, WINDOW)) for i in range(0, WINDOW, 256)]


def fill_window(g_ref, w_ref, l_ref, d):
    for t in range(11):
        w_ref[:, t * 128 : (t + 1) * 128] = g_ref[:, tile(lax.rem(first_tile(d) + t, TILES))]
    l_ref[...] = w_ref[:, :512].T


def tile_after(d):
    return pl.ds(pl.multiple_of(128 * (d % 2), 128), IMAGE)


def column_norms(w_ref):
    return jnp.sqrt(jnp.sum(jnp.square(w_ref[...].astype(F32)), 0, keepdims=True))


def padded(rows, count):
    rows = jnp.concatenate(rows, 0)
    return jnp.concatenate([rows, jnp.zeros((count - rows.shape[0], rows.shape[1]), F32)], 0)


def rows_of(r_ref, norms, d, start=0, count=BLOCK):
    r_ref[...] = upright(norms[:, :512])
    return r_ref[pl.ds(pl.multiple_of(lead_in(d) + start, 16), count), :]


def wide(rows, lanes):
    return rows if lanes.stop - lanes.start == 128 else jnp.concatenate([rows, rows], 1)


def product(l_ref, w_ref, lanes, d):
    left = l_ref[pl.ds(pl.multiple_of(lead_in(d), 64), BLOCK), :]
    return jnp.dot(left, w_ref[:, lanes], preferred_element_type=F32)


def right_far(at_ref, g_ref, out_a, out_b, w_ref, l_ref, r_ref):
    d = lax.rem(at_ref[0] + 2, 4)
    fill_window(g_ref, w_ref, l_ref, d)
    lead, trail, norms = split(column_norms(w_ref))
    tail = padded([lead, trail], 16).astype(BF16)
    cols = inverse(norms)
    rows = rows_of(r_ref, cols, d)
    for ref in (out_a, out_b):
        ref[HALF_ROWS:, :] = tail
    for lanes in PARTS:
        code = raised(product(l_ref, w_ref, lanes, d), wide(rows, lanes), cols[:, lanes]).astype(BF16)
        out_a[:HALF_ROWS, lanes] = code[:HALF_ROWS]
        out_b[:HALF_ROWS, lanes] = code[HALF_ROWS:]


def right_near(step, at_ref, g_ref, in_ref, out_ref, w_ref, l_ref, r_ref, p_ref):
    d = lax.rem(at_ref[0] + step, 4)
    start = 0 if step == 1 else HALF_ROWS
    fill_window(g_ref, w_ref, l_ref, d)
    tail = in_ref[HALF_ROWS:, :].astype(F32)
    theirs = tail[0:1] + tail[1:2]
    their_rows = rows_of(r_ref, theirs, d, start, HALF_ROWS)
    lead, trail, norms = split(jnp.sqrt(jnp.square(column_norms(w_ref)) + jnp.square(theirs)))
    out_ref[BLOCK:, :] = padded([lead, trail], 16).astype(BF16)
    cols = inverse(norms)
    rows = rows_of(r_ref, cols, d)
    here = slice(start, start + HALF_ROWS)
    for lanes in PARTS:
        part = p_ref.at[:, : lanes.stop - lanes.start]
        part[...] = product(l_ref, w_ref, lanes, d)
        part[here, :] += root(in_ref[:HALF_ROWS, lanes].astype(F32), wide(their_rows, lanes), theirs[:, lanes])
        out_ref[:BLOCK, lanes] = raised(part[...], wide(rows, lanes), cols[:, lanes]).astype(BF16)


def right_second(at_ref, g_ref, in_1, in_3, out_1, out_3, out_2, own_ref, w_ref, l_ref, r_ref, e_ref, t_ref):
    d, zh = at_ref[0], at_ref[1]
    fill_window(g_ref, w_ref, l_ref, d)
    squares, theirs = jnp.square(column_norms(w_ref)), []
    for ref in (in_1, in_3):
        tail = ref[BLOCK:, :].astype(F32)
        norms = tail[0:1] + tail[1:2]
        squares += jnp.square(norms)
        theirs.append((ref, norms, rows_of(r_ref, norms, d)))
    lead, trail, norms = split(jnp.sqrt(squares))
    cols = inverse(norms)
    rows = rows_of(r_ref, cols, d)
    begin = pl.multiple_of(lead_in(d), 64)
    e_ref[:64, :] = jnp.zeros((64, WINDOW), F32)
    e_ref[BLOCK:, :] = jnp.zeros((64, WINDOW), F32)
    for lanes in PARTS:
        part = product(l_ref, w_ref, lanes, d)
        for ref, their_cols, their_rows in theirs:
            part += root(ref[:BLOCK, lanes].astype(F32), wide(their_rows, lanes), their_cols[:, lanes])
        e_ref[pl.ds(begin, BLOCK), lanes] = raised(part, wide(rows, lanes), cols[:, lanes])
    for i in range(5):
        for j in range(4):
            t_ref[i * 128 : (i + 1) * 128, j * 128 : (j + 1) * 128] = e_ref[
                j * 128 : (j + 1) * 128, 384 + i * 128 : 512 + i * 128
            ].T
    tails = [jnp.concatenate([v[:, t * 128 : (t + 1) * 128] for t in range(11)], 0) for v in (lead, trail, norms)]
    for step, ref in ((1, out_1), (3, out_3), (2, out_2), (0, own_ref)):
        chunk = lax.rem(zh + step, 4) * CHUNK
        piece = e_ref[pl.ds(pl.multiple_of(begin + chunk, 16), CHUNK), :]
        image = t_ref[pl.ds(pl.multiple_of(64 + begin + chunk, 16), CHUNK), tile_after(d)]
        ref[:, :WINDOW] = piece.astype(ref.dtype)
        ref[:, WINDOW:WIDTH] = image.astype(ref.dtype)
        ref[:, WIDTH:] = padded(tails[:2] if step else tails[2:], CHUNK).astype(ref.dtype)


def right_third(scale, at_ref, own_ref, in_1, in_3, in_2, out_ref, image_ref, r_ref, n_ref):
    d, zh = at_ref[0], at_ref[1]
    begin = pl.multiple_of(lead_in(d) + zh * CHUNK, 16)
    for i, ref in enumerate((own_ref, in_1, in_3, in_2)):
        tail = ref[:, WIDTH:].astype(F32)
        n_ref[...] = tail[:11] if i == 0 else tail[:11] + tail[11:22]
        for t in range(8):
            r_ref[t * 128 : (t + 1) * 128, :] = upright(n_ref[t : t + 1, :])
        rows = r_ref[pl.ds(begin, CHUNK), :]
        image_rows = r_ref[pl.ds(pl.multiple_of(448 + begin, 16), CHUNK), :]
        for t in range(14):
            lanes = slice(t * 128, (t + 1) * 128)
            code = ref[:, lanes].astype(F32)
            if t < 11:
                to, here, part = out_ref, lanes, root(code, rows, n_ref[t : t + 1, :])
            else:
                here = slice((t - 11) * 128, (t - 10) * 128)
                cols = n_ref[pl.ds(t - 11 + lax.rem(d, 2), 1), :]
                to, part = image_ref, root(code, image_rows, cols)
            if i == 0:
                to[:, here] = part * scale
            else:
                to[:, here] += part * scale


def right_last(at_ref, base_ref, image_ref, out_ref):
    d = at_ref[0]
    for t in range(14):
        ref, i = (base_ref, t) if t < 11 else (image_ref, t - 11)
        out_ref[:, tile(lax.rem(first_tile(d) + t, TILES))] = ref[:, i * 128 : (i + 1) * 128]


SUB, BASE, ROWS = 128, 1024, 1152


def sub(i):
    return pl.ds(pl.multiple_of(i * SUB, SUB), SUB)


def base_subs(core, b):
    return [4 * a + (core ^ (a > b).astype(jnp.int32)) + 2 * h for a in range(4) for h in (0, 1)]


def slot(i):
    return i // 4 * 4 + 2 * (i % 2) + i // 2 % 2


def more_sub(core, b, zl):
    return 4 * b + lax.rem(2 * zl + core + 1, 4)


def two_cols(ref, core, b):
    return jnp.concatenate([ref[pl.ds(4 * b + core + 2 * zl, 1), :] for zl in (0, 1)], 1)


def left_first(at_ref, far, near, far_2, near_2, out_1, out_3, out_2, own_ref, norm_ref, a_ref, b_ref, i_ref, s_ref):
    zh, y, core = at_ref[1], at_ref[2], at_ref[4]
    for p, ref in enumerate((far, near, far_2, near_2)):
        j = 2 * ((p // 2) ^ core) + lax.rem(p + zh, 2)
        for m in range(4):
            a_ref[sub(4 * j + slot(m)), :] = ref[m * SUB : (m + 1) * SUB, :]
    leads, trails, lanes = [], [], []
    for i in range(16):
        rows = slice(slot(i) * SUB, (slot(i) + 1) * SUB)
        squares = jnp.sum(jnp.square(a_ref[rows, :].astype(F32)), 1, keepdims=True)
        row = jnp.broadcast_to(jnp.sqrt(squares), (SUB, SUB)).T[0:1]
        lead, trail, norms = split(row)
        leads.append(lead), trails.append(trail), lanes.append(norms)
        i_ref[rows, :] = upright(inverse(norms))
    tail = jnp.concatenate([jnp.concatenate(leads, 0), jnp.concatenate(trails, 0)], 1).astype(BF16)
    norm_ref[...] = jnp.concatenate(lanes, 0)
    s_ref[...] = inverse(norm_ref[...])
    for step, out in ((1, out_1), (3, out_3), (2, out_2), (0, own_ref)):
        b = lax.rem(y + step, 4)
        for zl in (0, 1):
            b_ref[zl * SUB : (zl + 1) * SUB, :] = a_ref[sub(slot(4 * b + core + 2 * zl)), :]
        cols = two_cols(s_ref, core, b)
        for k, i in enumerate(base_subs(core, b)[::2]):
            pair = pl.ds(pl.multiple_of(slot(i) * SUB, 2 * SUB), 2 * SUB)
            part = dot(a_ref[pair, :], b_ref[...], 1)
            if step:
                scale = i_ref[pair, :]
                part = raised(part, jnp.concatenate([scale, scale], 1), cols).astype(BF16)
            out[k * 2 * SUB : (k + 1) * 2 * SUB, :] = part
        for zl in (0, 1):
            here = slice(zl * SUB, (zl + 1) * SUB)
            i = slot(more_sub(core, b, zl))
            part = dot(a_ref[sub(i), :], b_ref[here, :], 1)
            if step:
                part = raised(part, i_ref[sub(i), :], cols[:, here]).astype(BF16)
            out[BASE:ROWS, here] = part
        if step:
            out[ROWS:, :] = tail


def left_second(at_ref, own_ref, norm_ref, in_1, in_3, in_2, *refs):
    outs, (e_ref, s_ref, lead_ref, trail_ref, n_ref) = refs[:8], refs[8:]
    zh, y, zl, core = (at_ref[i] for i in (1, 2, 3, 4))
    squares = jnp.square(norm_ref[...])
    for k, ref in enumerate((in_1, in_3, in_2)):
        tail = ref[ROWS:, :].astype(F32)
        norms = tail[:, :SUB] + tail[:, SUB:]
        squares += jnp.square(norms)
        s_ref[k] = norms
    lead_ref[...], trail_ref[...], n_ref[...] = split(jnp.sqrt(squares))
    s_ref[3] = inverse(n_ref[...])
    sources = [(ref, k) for k, ref in enumerate((in_1, in_3, in_2))]
    cols = [two_cols(s_ref.at[k], core, y) for k in range(4)]
    r = lambda k, i: upright(s_ref.at[k][pl.ds(i, 1), :])
    for j, i in enumerate(base_subs(core, y)):
        rows = slice(j * SUB, (j + 1) * SUB)
        part = own_ref[rows, :]
        for ref, k in sources:
            scale = r(k, i)
            part += root(ref[rows, :].astype(F32), jnp.concatenate([scale, scale], 1), cols[k])
        scale = r(3, i)
        e_ref[rows, :] = raised(part, jnp.concatenate([scale, scale], 1), cols[3])
    for l in (0, 1):
        here = slice(l * SUB, (l + 1) * SUB)
        i = more_sub(core, y, l)
        part = own_ref[BASE:ROWS, here]
        for ref, k in sources:
            part += root(ref[BASE:ROWS, here].astype(F32), r(k, i), cols[k][:, here])
        e_ref[BASE:ROWS, here] = raised(part, r(3, i), cols[3][:, here])
    for step, out in zip((*Z_STEPS, 0), outs):
        z = lax.rem(2 * zh + zl + step, 8)
        to_h, to_l = z // 2, lax.rem(z, 2)
        lanes = tile(to_l)
        out[:256, :] = e_ref[pl.ds(pl.multiple_of(to_h * 256, 256), 256), lanes].astype(out.dtype)
        out[256:384, :] = e_ref[BASE:ROWS, lanes].astype(out.dtype)
        first = 4 * to_h + (core ^ (to_h > y).astype(jnp.int32))
        picks = [first, first + 2, more_sub(core, y, to_l), 4 * y + 2 * to_l + core]
        tail = [ref[pl.ds(i, 1), :] for ref in ((lead_ref, trail_ref) if step else (n_ref,)) for i in picks]
        out[384:, :] = padded(tail, 16).astype(out.dtype)


def left_third(scale, at_ref, *refs):
    sources, (base_ref, more_ref, same_ref, other_ref, sum_ref) = refs[:8], refs[8:]
    zh, y, zl = at_ref[1], at_ref[2], at_ref[3]
    for k, ref in enumerate(sources):
        tail = ref[384:, :].astype(F32)
        norms = tail[0:4] if k == 0 else tail[0:4] + tail[4:8]
        for j in range(3):
            rows = slice(j * SUB, (j + 1) * SUB)
            part = root(ref[rows, :].astype(F32), upright(norms[j : j + 1]), norms[3:4]) * scale
            if k == 0:
                sum_ref[rows, :] = part
            else:
                sum_ref[rows, :] += part
    first, second, more = (sum_ref[j * SUB : (j + 1) * SUB, :] for j in range(3))
    base_ref[...] = sum_ref[:256, :]
    more_ref[...] = more
    same_ref[...] = jnp.where(zh == y, more, jnp.where(zl == 0, first, second)).T
    other_ref[...] = jnp.where(zl == 0, second, first).T


def left_last(at_ref, base_ref, more_ref, same_ref, other_ref, out_ref):
    zh, y, zl, core = (at_ref[i] for i in (1, 2, 3, 4))
    n, parity, diagonal = 2 * zl + core, core ^ (zh > y).astype(jnp.int32), zh == y
    out_ref[sub(parity), :] = base_ref[:SUB, :]
    out_ref[sub(parity + 2), :] = base_ref[SUB:, :]
    out_ref[sub(jnp.where(diagonal, lax.rem(n + 3, 4), 2 * zl + 1 - parity)), :] = same_ref[...]
    out_ref[sub(jnp.where(diagonal, lax.rem(n + 1, 4), 2 * (1 - zl) + 1 - parity)), :] = jnp.where(
        diagonal, more_ref[...], other_ref[...]
    )


def mirror(step):
    def to(x, zh, y, zl, core):
        if zh != y:
            return (x, y, zh, zl ^ step, core ^ (zh > y))
        n = (2 * zl + core + 1 - step) % 4
        return (x, zh, y, n // 2, n % 2)

    return to


def along_z(step):
    def to(x, zh, y, zl, core):
        z = (2 * zh + zl + step) % 8
        return (x, z // 2, y, z % 2, core)

    return to


def shards(gradient):
    rows, width = gradient.shape
    row, col = lax.axis_index("row"), lax.axis_index("col")
    x, zh, y, zl, core = row // 4, row % 4, col // 4, col // 2 % 2, col % 2
    at = jnp.stack([x, zh, y, zl, core, x, x, x]).astype(jnp.int32)
    barrier = lax.optimization_barrier
    half = width // 2

    cut = lambda parity: lax.dynamic_slice_in_dim(gradient, parity * half, half, 1)
    near, far, gradient = barrier((cut((zh + 1) % 2), cut(zh % 2), gradient))
    near = send(near, lambda x, zh, y, zl, core: (x, 2 * core + (zh + 1) % 2, y, zl, zh // 2))

    window = [((rows, WINDOW), BF16), ((512, 512), BF16), ((512, 128), F32)]
    half_part, whole_part = ((HALF_ROWS + 16, WINDOW), BF16), ((BLOCK + 16, WINDOW), BF16)
    over_x = lambda s, v: send(v, lambda x, zh, y, zl, core: (x + s, zh, y, zl, core))
    far_1, far_3 = run(right_far, [half_part] * 2, window, FLOPS, at, gradient)
    far_1, far_3 = over_x(1, far_1), over_x(3, far_3)
    near, far, far_1, far_3 = barrier((near, far, far_1, far_3))
    far = send(far, lambda x, zh, y, zl, core: (x, 2 * core + zh % 2, y, zl, zh // 2))
    add = lambda s, v: run(
        functools.partial(right_near, s), [whole_part], window + [((BLOCK, 256), F32)], FLOPS, at, gradient, v
    )[0]
    code_1, code_3 = add(1, far_1), add(3, far_3)
    right_1, right_3 = over_x(1, code_1), over_x(3, code_3)
    near, far, right_1, right_3 = barrier((near, far, right_1, right_3))

    swap = lambda x, zh, y, zl, core: (x, zh, y, zl, 1 - core)
    far_2, near_2 = send(far, swap), send(near, swap)

    piece = (CHUNK, WIDTH + 128)
    code_1, code_3, code_2, right_own = run(
        right_second,
        [(piece, BF16)] * 3 + [(piece, F32)],
        window + [((512, WINDOW), F32), ((640, 512), F32)],
        FLOPS,
        at,
        gradient,
        right_1,
        right_3,
    )
    over_z = lambda s, v: send(v, lambda x, zh, y, zl, core: (x, zh + s, y, zl, core))
    right_2 = over_z(2, code_2)

    far, near, far_2, near_2, _ = barrier((far, near, far_2, near_2, code_1))
    packed = (ROWS + 16, 256)
    left_1, left_3, left_2, left_own, norms = run(
        left_first,
        [(packed, BF16)] * 3 + [((ROWS, 256), F32), ((16, SUB), F32)],
        [((2048, half), BF16), ((256, half), BF16), ((2048, SUB), F32), ((16, SUB), F32)],
        FLOPS,
        at,
        far,
        near,
        far_2,
        near_2,
    )
    over_y = lambda s, v: send(v, lambda x, zh, y, zl, core: (x, zh, y + s, zl, core))
    left_1, left_3 = over_y(1, left_1), over_y(3, left_3)
    left_1, left_3, left_2, right_2, code_1, code_3 = barrier((left_1, left_3, left_2, right_2, code_1, code_3))
    left_2, right_1, right_3 = over_y(2, left_2), over_z(1, code_1), over_z(3, code_3)
    left_2, right_1, right_3 = barrier((left_2, right_1, right_3))

    piece = (400, SUB)
    codes = run(
        left_second,
        [(piece, BF16)] * 7 + [(piece, F32)],
        [((ROWS, 256), F32), ((4, 16, SUB), F32)] + [((16, SUB), F32)] * 3,
        FLOPS,
        at,
        left_own,
        norms,
        left_1,
        left_3,
        left_2,
    )
    arrived = [send(code, along_z(s)) for s, code in zip(Z_STEPS, codes)]
    right_1, right_3, _ = barrier((right_1, right_3, arrived[0]))

    right_base, image = run(
        functools.partial(right_third, 1.0 / (rows * 16)),
        [((CHUNK, WINDOW), F32), ((CHUNK, IMAGE), F32)],
        [((1024, 128), F32), ((11, 128), F32)],
        FLOPS,
        at,
        right_own,
        right_1,
        right_3,
        right_2,
    )
    image = over_x(1, image)
    right_gram = run(right_last, [((CHUNK, width), F32)], [], FLOPS, at, right_base, image)[0]

    arrived, right_gram = barrier((arrived, right_gram))
    square = ((SUB, SUB), F32)
    base, more, same, other = run(
        functools.partial(left_third, 1.0 / (width * 16)),
        [((256, SUB), F32), square, square, square],
        [((384, SUB), F32)],
        FLOPS,
        at,
        codes[7],
        *arrived,
    )
    same, other = send(same, mirror(0)), send(other, mirror(1))
    left_gram = run(left_last, [((512, SUB), F32)], [], FLOPS, at, base, more, same, other)[0]
    return (left_gram, right_gram)


def solution(mesh):
    in_specs = (P("row", "col"),)
    out_specs = (P("row", "col"), P(("col", "row"), None))
    return jax.shard_map(shards, mesh=mesh, in_specs=in_specs, out_specs=out_specs, check_vma=False)
```

```python
import functools
import itertools

import jax
import jax.numpy as jnp
from jax import lax
from jax.experimental import pallas as pl
from jax.experimental.pallas import tpu as pltpu
from jax.sharding import PartitionSpec as P

F32, BF16 = jnp.float32, jnp.bfloat16

SIZES = (4, 4, 4, 2, 2)
PLACES = list(itertools.product(*(range(n) for n in SIZES)))
STEPS = (1, 3, 2)
Z_STEPS = (1, 7, 2, 6, 3, 5, 4)


def number(place):
    x, zh, y, zl, core = (p % n for p, n in zip(place, SIZES))
    return (4 * x + zh) * 16 + 4 * y + 2 * zl + core


def send(array, to):
    return lax.ppermute(array, ("row", "col"), [(number(p), number(to(*p))) for p in PLACES])


POWER = 13
LIFT = 120 / POWER
LOG_LIFT = LIFT * 0.6931471805599453


def split(norms):
    lead = norms.astype(BF16).astype(F32)
    trail = (norms - lead).astype(BF16).astype(F32)
    return lead, trail, lead + trail


def inverse(norms):
    return jnp.where(norms > 0, 1.0 / jnp.where(norms > 0, norms, 1.0), 0.0)


def raised(value, rows, cols):
    ratio = value * rows * (cols * 2.0**LIFT)
    p2 = ratio * ratio
    p4 = p2 * p2
    return p4 * p4 * (p4 * ratio)


def root(code, rows, cols):
    size = jnp.exp(jnp.log(jnp.abs(code)) * (1.0 / POWER) - LOG_LIFT)
    return jnp.where(code < 0, -size, size) * (rows * cols)


def upright(row):
    parts = [row[:, i : i + 128] for i in range(0, row.shape[1], 128)]
    return jnp.concatenate([jnp.broadcast_to(p, (128, 128)).T for p in parts], 0)


def dot(left, right, dim):
    return lax.dot_general(
        left, right, (((dim,), (dim,)), ((), ())), preferred_element_type=F32
    )


def run(body, outs, scratch, *args):
    smem, vmem = pl.BlockSpec(memory_space=pltpu.SMEM), pl.BlockSpec(memory_space=pltpu.VMEM)
    return pl.pallas_call(
        body,
        out_shape=[jax.ShapeDtypeStruct(shape, dtype) for shape, dtype in outs],
        in_specs=[smem] + [vmem] * (len(args) - 1),
        out_specs=[vmem] * len(outs),
        scratch_shapes=[pltpu.VMEM(shape, dtype) for shape, dtype in scratch],
        cost_estimate=pl.CostEstimate(flops=1000, bytes_accessed=1000, transcendentals=0),
        compiler_params=pltpu.CompilerParams(vmem_limit_bytes=48 * 1024 * 1024),
    )(*args)


BLOCK, CHUNK, TILES, WINDOW, IMAGE = 448, 112, 14, 1408, 384
WIDTH = WINDOW + IMAGE


def first_tile(d):
    return 7 * (d // 2) + 3 * (d % 2)


def lead_in(d):
    return 64 * (d % 2)


def tile(i):
    return pl.ds(pl.multiple_of(i * 128, 128), 128)


HALF_ROWS = BLOCK // 2
PARTS = [slice(i, min(i + 256, WINDOW)) for i in range(0, WINDOW, 256)]


def fill_window(g_ref, w_ref, l_ref, d):
    for t in range(11):
        w_ref[:, t * 128 : (t + 1) * 128] = g_ref[:, tile(lax.rem(first_tile(d) + t, TILES))]
    l_ref[...] = w_ref[:, :512].T


def tile_after(d):
    return pl.ds(pl.multiple_of(128 * (d % 2), 128), IMAGE)


def column_norms(w_ref):
    return jnp.sqrt(jnp.sum(jnp.square(w_ref[...].astype(F32)), 0, keepdims=True))


def padded(rows, count):
    rows = jnp.concatenate(rows, 0)
    return jnp.concatenate([rows, jnp.zeros((count - rows.shape[0], rows.shape[1]), F32)], 0)


def rows_of(r_ref, norms, d, start=0, count=BLOCK):
    r_ref[...] = upright(norms[:, :512])
    return r_ref[pl.ds(pl.multiple_of(lead_in(d) + start, 16), count), :]


def wide(rows, lanes):
    return rows if lanes.stop - lanes.start == 128 else jnp.concatenate([rows, rows], 1)


def product(l_ref, w_ref, lanes, d):
    left = l_ref[pl.ds(pl.multiple_of(lead_in(d), 64), BLOCK), :]
    return jnp.dot(left, w_ref[:, lanes], preferred_element_type=F32)


def right_far(at_ref, g_ref, out_a, out_b, w_ref, l_ref, r_ref):
    d = lax.rem(at_ref[0] + 2, 4)
    fill_window(g_ref, w_ref, l_ref, d)
    lead, trail, norms = split(column_norms(w_ref))
    tail = padded([lead, trail], 16).astype(BF16)
    cols = inverse(norms)
    rows = rows_of(r_ref, cols, d)
    for ref in (out_a, out_b):
        ref[HALF_ROWS:, :] = tail
    for lanes in PARTS:
        code = raised(product(l_ref, w_ref, lanes, d), wide(rows, lanes), cols[:, lanes]).astype(BF16)
        out_a[:HALF_ROWS, lanes] = code[:HALF_ROWS]
        out_b[:HALF_ROWS, lanes] = code[HALF_ROWS:]


def right_near(step, at_ref, g_ref, in_ref, out_ref, w_ref, l_ref, r_ref, p_ref):
    d = lax.rem(at_ref[0] + step, 4)
    start = 0 if step == 1 else HALF_ROWS
    fill_window(g_ref, w_ref, l_ref, d)
    tail = in_ref[HALF_ROWS:, :].astype(F32)
    theirs = tail[0:1] + tail[1:2]
    their_rows = rows_of(r_ref, theirs, d, start, HALF_ROWS)
    lead, trail, norms = split(jnp.sqrt(jnp.square(column_norms(w_ref)) + jnp.square(theirs)))
    out_ref[BLOCK:, :] = padded([lead, trail], 16).astype(BF16)
    cols = inverse(norms)
    rows = rows_of(r_ref, cols, d)
    here = slice(start, start + HALF_ROWS)
    for lanes in PARTS:
        part = p_ref.at[:, : lanes.stop - lanes.start]
        part[...] = product(l_ref, w_ref, lanes, d)
        part[here, :] += root(in_ref[:HALF_ROWS, lanes].astype(F32), wide(their_rows, lanes), theirs[:, lanes])
        out_ref[:BLOCK, lanes] = raised(part[...], wide(rows, lanes), cols[:, lanes]).astype(BF16)


def right_second(at_ref, g_ref, in_1, in_3, out_1, out_3, out_2, own_ref, w_ref, l_ref, r_ref, e_ref, t_ref):
    d, zh = at_ref[0], at_ref[1]
    fill_window(g_ref, w_ref, l_ref, d)
    squares, theirs = jnp.square(column_norms(w_ref)), []
    for ref in (in_1, in_3):
        tail = ref[BLOCK:, :].astype(F32)
        norms = tail[0:1] + tail[1:2]
        squares += jnp.square(norms)
        theirs.append((ref, norms, rows_of(r_ref, norms, d)))
    lead, trail, norms = split(jnp.sqrt(squares))
    cols = inverse(norms)
    rows = rows_of(r_ref, cols, d)
    begin = pl.multiple_of(lead_in(d), 64)
    e_ref[:64, :] = jnp.zeros((64, WINDOW), F32)
    e_ref[BLOCK:, :] = jnp.zeros((64, WINDOW), F32)
    for lanes in PARTS:
        part = product(l_ref, w_ref, lanes, d)
        for ref, their_cols, their_rows in theirs:
            part += root(ref[:BLOCK, lanes].astype(F32), wide(their_rows, lanes), their_cols[:, lanes])
        e_ref[pl.ds(begin, BLOCK), lanes] = raised(part, wide(rows, lanes), cols[:, lanes])
    for i in range(5):
        for j in range(4):
            t_ref[i * 128 : (i + 1) * 128, j * 128 : (j + 1) * 128] = e_ref[
                j * 128 : (j + 1) * 128, 384 + i * 128 : 512 + i * 128
            ].T
    tails = [jnp.concatenate([v[:, t * 128 : (t + 1) * 128] for t in range(11)], 0) for v in (lead, trail, norms)]
    for step, ref in ((1, out_1), (3, out_3), (2, out_2), (0, own_ref)):
        chunk = lax.rem(zh + step, 4) * CHUNK
        piece = e_ref[pl.ds(pl.multiple_of(begin + chunk, 16), CHUNK), :]
        image = t_ref[pl.ds(pl.multiple_of(64 + begin + chunk, 16), CHUNK), tile_after(d)]
        ref[:, :WINDOW] = piece.astype(ref.dtype)
        ref[:, WINDOW:WIDTH] = image.astype(ref.dtype)
        ref[:, WIDTH:] = padded(tails[:2] if step else tails[2:], CHUNK).astype(ref.dtype)


def right_third(scale, at_ref, own_ref, in_1, in_3, in_2, out_ref, image_ref, r_ref, n_ref):
    d, zh = at_ref[0], at_ref[1]
    begin = pl.multiple_of(lead_in(d) + zh * CHUNK, 16)
    for i, ref in enumerate((own_ref, in_1, in_3, in_2)):
        tail = ref[:, WIDTH:].astype(F32)
        n_ref[...] = tail[:11] if i == 0 else tail[:11] + tail[11:22]
        for t in range(8):
            r_ref[t * 128 : (t + 1) * 128, :] = upright(n_ref[t : t + 1, :])
        rows = r_ref[pl.ds(begin, CHUNK), :]
        image_rows = r_ref[pl.ds(pl.multiple_of(448 + begin, 16), CHUNK), :]
        for t in range(14):
            lanes = slice(t * 128, (t + 1) * 128)
            code = ref[:, lanes].astype(F32)
            if t < 11:
                to, here, part = out_ref, lanes, root(code, rows, n_ref[t : t + 1, :])
            else:
                here = slice((t - 11) * 128, (t - 10) * 128)
                cols = n_ref[pl.ds(t - 11 + lax.rem(d, 2), 1), :]
                to, part = image_ref, root(code, image_rows, cols)
            if i == 0:
                to[:, here] = part * scale
            else:
                to[:, here] += part * scale


def right_last(at_ref, base_ref, image_ref, out_ref):
    d = at_ref[0]
    for t in range(14):
        ref, i = (base_ref, t) if t < 11 else (image_ref, t - 11)
        out_ref[:, tile(lax.rem(first_tile(d) + t, TILES))] = ref[:, i * 128 : (i + 1) * 128]


SUB, BASE, ROWS = 128, 1024, 1152


def sub(i):
    return pl.ds(pl.multiple_of(i * SUB, SUB), SUB)


def base_subs(core, b):
    return [4 * a + (core ^ (a > b).astype(jnp.int32)) + 2 * h for a in range(4) for h in (0, 1)]


def slot(i):
    return i // 4 * 4 + 2 * (i % 2) + i // 2 % 2


def more_sub(core, b, zl):
    return 4 * b + lax.rem(2 * zl + core + 1, 4)


def two_cols(ref, core, b):
    return jnp.concatenate([ref[pl.ds(4 * b + core + 2 * zl, 1), :] for zl in (0, 1)], 1)


def left_first(at_ref, far, near, far_2, near_2, out_1, out_3, out_2, own_ref, norm_ref, a_ref, b_ref, i_ref, s_ref):
    zh, y, core = at_ref[1], at_ref[2], at_ref[4]
    for p, ref in enumerate((far, near, far_2, near_2)):
        j = 2 * ((p // 2) ^ core) + lax.rem(p + zh, 2)
        for m in range(4):
            a_ref[sub(4 * j + slot(m)), :] = ref[m * SUB : (m + 1) * SUB, :]
    leads, trails, lanes = [], [], []
    for i in range(16):
        rows = slice(slot(i) * SUB, (slot(i) + 1) * SUB)
        squares = jnp.sum(jnp.square(a_ref[rows, :].astype(F32)), 1, keepdims=True)
        row = jnp.broadcast_to(jnp.sqrt(squares), (SUB, SUB)).T[0:1]
        lead, trail, norms = split(row)
        leads.append(lead), trails.append(trail), lanes.append(norms)
        i_ref[rows, :] = upright(inverse(norms))
    tail = jnp.concatenate([jnp.concatenate(leads, 0), jnp.concatenate(trails, 0)], 1).astype(BF16)
    norm_ref[...] = jnp.concatenate(lanes, 0)
    s_ref[...] = inverse(norm_ref[...])
    for step, out in ((1, out_1), (3, out_3), (2, out_2), (0, own_ref)):
        b = lax.rem(y + step, 4)
        for zl in (0, 1):
            b_ref[zl * SUB : (zl + 1) * SUB, :] = a_ref[sub(slot(4 * b + core + 2 * zl)), :]
        cols = two_cols(s_ref, core, b)
        for k, i in enumerate(base_subs(core, b)[::2]):
            pair = pl.ds(pl.multiple_of(slot(i) * SUB, 2 * SUB), 2 * SUB)
            part = dot(a_ref[pair, :], b_ref[...], 1)
            if step:
                scale = i_ref[pair, :]
                part = raised(part, jnp.concatenate([scale, scale], 1), cols).astype(BF16)
            out[k * 2 * SUB : (k + 1) * 2 * SUB, :] = part
        for zl in (0, 1):
            here = slice(zl * SUB, (zl + 1) * SUB)
            i = slot(more_sub(core, b, zl))
            part = dot(a_ref[sub(i), :], b_ref[here, :], 1)
            if step:
                part = raised(part, i_ref[sub(i), :], cols[:, here]).astype(BF16)
            out[BASE:ROWS, here] = part
        if step:
            out[ROWS:, :] = tail


def left_second(at_ref, own_ref, norm_ref, in_1, in_3, in_2, *refs):
    outs, (e_ref, s_ref, lead_ref, trail_ref, n_ref) = refs[:8], refs[8:]
    zh, y, zl, core = (at_ref[i] for i in (1, 2, 3, 4))
    squares = jnp.square(norm_ref[...])
    for k, ref in enumerate((in_1, in_3, in_2)):
        tail = ref[ROWS:, :].astype(F32)
        norms = tail[:, :SUB] + tail[:, SUB:]
        squares += jnp.square(norms)
        s_ref[k] = norms
    lead_ref[...], trail_ref[...], n_ref[...] = split(jnp.sqrt(squares))
    s_ref[3] = inverse(n_ref[...])
    sources = [(ref, k) for k, ref in enumerate((in_1, in_3, in_2))]
    cols = [two_cols(s_ref.at[k], core, y) for k in range(4)]
    r = lambda k, i: upright(s_ref.at[k][pl.ds(i, 1), :])
    for j, i in enumerate(base_subs(core, y)):
        rows = slice(j * SUB, (j + 1) * SUB)
        part = own_ref[rows, :]
        for ref, k in sources:
            scale = r(k, i)
            part += root(ref[rows, :].astype(F32), jnp.concatenate([scale, scale], 1), cols[k])
        scale = r(3, i)
        e_ref[rows, :] = raised(part, jnp.concatenate([scale, scale], 1), cols[3])
    for l in (0, 1):
        here = slice(l * SUB, (l + 1) * SUB)
        i = more_sub(core, y, l)
        part = own_ref[BASE:ROWS, here]
        for ref, k in sources:
            part += root(ref[BASE:ROWS, here].astype(F32), r(k, i), cols[k][:, here])
        e_ref[BASE:ROWS, here] = raised(part, r(3, i), cols[3][:, here])
    for step, out in zip((*Z_STEPS, 0), outs):
        z = lax.rem(2 * zh + zl + step, 8)
        to_h, to_l = z // 2, lax.rem(z, 2)
        lanes = tile(to_l)
        out[:256, :] = e_ref[pl.ds(pl.multiple_of(to_h * 256, 256), 256), lanes].astype(out.dtype)
        out[256:384, :] = e_ref[BASE:ROWS, lanes].astype(out.dtype)
        first = 4 * to_h + (core ^ (to_h > y).astype(jnp.int32))
        picks = [first, first + 2, more_sub(core, y, to_l), 4 * y + 2 * to_l + core]
        tail = [ref[pl.ds(i, 1), :] for ref in ((lead_ref, trail_ref) if step else (n_ref,)) for i in picks]
        out[384:, :] = padded(tail, 16).astype(out.dtype)


def left_third(scale, at_ref, *refs):
    sources, (base_ref, more_ref, same_ref, other_ref, sum_ref) = refs[:8], refs[8:]
    zh, y, zl = at_ref[1], at_ref[2], at_ref[3]
    for k, ref in enumerate(sources):
        tail = ref[384:, :].astype(F32)
        norms = tail[0:4] if k == 0 else tail[0:4] + tail[4:8]
        for j in range(3):
            rows = slice(j * SUB, (j + 1) * SUB)
            part = root(ref[rows, :].astype(F32), upright(norms[j : j + 1]), norms[3:4]) * scale
            if k == 0:
                sum_ref[rows, :] = part
            else:
                sum_ref[rows, :] += part
    first, second, more = (sum_ref[j * SUB : (j + 1) * SUB, :] for j in range(3))
    base_ref[...] = sum_ref[:256, :]
    more_ref[...] = more
    same_ref[...] = jnp.where(zh == y, more, jnp.where(zl == 0, first, second)).T
    other_ref[...] = jnp.where(zl == 0, second, first).T


def left_last(at_ref, base_ref, more_ref, same_ref, other_ref, out_ref):
    zh, y, zl, core = (at_ref[i] for i in (1, 2, 3, 4))
    n, parity, diagonal = 2 * zl + core, core ^ (zh > y).astype(jnp.int32), zh == y
    out_ref[sub(parity), :] = base_ref[:SUB, :]
    out_ref[sub(parity + 2), :] = base_ref[SUB:, :]
    out_ref[sub(jnp.where(diagonal, lax.rem(n + 3, 4), 2 * zl + 1 - parity)), :] = same_ref[...]
    out_ref[sub(jnp.where(diagonal, lax.rem(n + 1, 4), 2 * (1 - zl) + 1 - parity)), :] = jnp.where(
        diagonal, more_ref[...], other_ref[...]
    )


def mirror(step):
    def to(x, zh, y, zl, core):
        if zh != y:
            return (x, y, zh, zl ^ step, core ^ (zh > y))
        n = (2 * zl + core + 1 - step) % 4
        return (x, zh, y, n // 2, n % 2)

    return to


def along_z(step):
    def to(x, zh, y, zl, core):
        z = (2 * zh + zl + step) % 8
        return (x, z // 2, y, z % 2, core)

    return to


def shards(gradient):
    rows, width = gradient.shape
    row, col = lax.axis_index("row"), lax.axis_index("col")
    x, zh, y, zl, core = row // 4, row % 4, col // 4, col // 2 % 2, col % 2
    at = jnp.stack([x, zh, y, zl, core, x, x, x]).astype(jnp.int32)
    barrier = lax.optimization_barrier
    half = width // 2

    cut = lambda parity: lax.dynamic_slice_in_dim(gradient, parity * half, half, 1)
    near, far, gradient = barrier((cut((zh + 1) % 2), cut(zh % 2), gradient))
    near = send(near, lambda x, zh, y, zl, core: (x, 2 * core + (zh + 1) % 2, y, zl, zh // 2))

    window = [((rows, WINDOW), BF16), ((512, 512), BF16), ((512, 128), F32)]
    half_part, whole_part = ((HALF_ROWS + 16, WINDOW), BF16), ((BLOCK + 16, WINDOW), BF16)
    over_x = lambda s, v: send(v, lambda x, zh, y, zl, core: (x + s, zh, y, zl, core))
    far_1, far_3 = run(right_far, [half_part] * 2, window, at, gradient)
    far_1, far_3 = over_x(1, far_1), over_x(3, far_3)
    near, far, far_1, far_3 = barrier((near, far, far_1, far_3))
    far = send(far, lambda x, zh, y, zl, core: (x, 2 * core + zh % 2, y, zl, zh // 2))
    add = lambda s, v: run(
        functools.partial(right_near, s), [whole_part], window + [((BLOCK, 256), F32)], at, gradient, v
    )[0]
    code_1, code_3 = add(1, far_1), add(3, far_3)
    right_1, right_3 = over_x(1, code_1), over_x(3, code_3)

    swap = lambda x, zh, y, zl, core: (x, zh, y, zl, 1 - core)
    far_2, near_2 = send(far, swap), send(near, swap)

    far, near, far_2, near_2, right_1, right_3 = barrier((far, near, far_2, near_2, right_1, right_3))
    packed = (ROWS + 16, 256)
    left_1, left_3, left_2, left_own, norms = run(
        left_first,
        [(packed, BF16)] * 3 + [((ROWS, 256), F32), ((16, SUB), F32)],
        [((2048, half), BF16), ((256, half), BF16), ((2048, SUB), F32), ((16, SUB), F32)],
        at,
        far,
        near,
        far_2,
        near_2,
    )
    over_y = lambda s, v: send(v, lambda x, zh, y, zl, core: (x, zh, y + s, zl, core))
    right_1, right_3, _ = barrier((right_1, right_3, left_2))
    left_1, left_3, left_2 = over_y(1, left_1), over_y(3, left_3), over_y(2, left_2)

    piece = (CHUNK, WIDTH + 128)
    code_1, code_3, code_2, right_own = run(
        right_second,
        [(piece, BF16)] * 3 + [(piece, F32)],
        window + [((512, WINDOW), F32), ((640, 512), F32)],
        at,
        gradient,
        right_1,
        right_3,
    )
    over_z = lambda s, v: send(v, lambda x, zh, y, zl, core: (x, zh + s, y, zl, core))
    right_1, right_3, right_2 = over_z(1, code_1), over_z(3, code_3), over_z(2, code_2)

    piece = (400, SUB)
    codes = run(
        left_second,
        [(piece, BF16)] * 7 + [(piece, F32)],
        [((ROWS, 256), F32), ((4, 16, SUB), F32)] + [((16, SUB), F32)] * 3,
        at,
        left_own,
        norms,
        left_1,
        left_3,
        left_2,
    )
    arrived = [send(code, along_z(s)) for s, code in zip(Z_STEPS, codes)]
    right_1, right_3, _ = barrier((right_1, right_3, codes))

    right_base, image = run(
        functools.partial(right_third, 1.0 / (rows * 16)),
        [((CHUNK, WINDOW), F32), ((CHUNK, IMAGE), F32)],
        [((1024, 128), F32), ((11, 128), F32)],
        at,
        right_own,
        right_1,
        right_3,
        right_2,
    )
    arrived, image = barrier((arrived, image))
    image = over_x(1, image)
    right_gram = run(right_last, [((CHUNK, width), F32)], [], at, right_base, image)[0]

    square = ((SUB, SUB), F32)
    base, more, same, other = run(
        functools.partial(left_third, 1.0 / (width * 16)),
        [((256, SUB), F32), square, square, square],
        [((384, SUB), F32)],
        at,
        codes[7],
        *arrived,
    )
    same, other = send(same, mirror(0)), send(other, mirror(1))
    left_gram = run(left_last, [((512, SUB), F32)], [], at, base, more, same, other)[0]
    return (left_gram, right_gram)


def solution(mesh):
    in_specs = (P("row", "col"),)
    out_specs = (P("row", "col"), P(("col", "row"), None))
    return jax.shard_map(shards, mesh=mesh, in_specs=in_specs, out_specs=out_specs, check_vma=False)
```

```python
import functools
import itertools

import jax
import jax.numpy as jnp
from jax import lax
from jax.experimental import pallas as pl
from jax.experimental.pallas import tpu as pltpu
from jax.sharding import PartitionSpec as P

F32, BF16 = jnp.float32, jnp.bfloat16

SIZES = (4, 4, 4, 2, 2)
PLACES = list(itertools.product(*(range(n) for n in SIZES)))
STEPS = (1, 3, 2)
Z_STEPS = (1, 7, 2, 6, 3, 5, 4)


def number(place):
    x, zh, y, zl, core = (p % n for p, n in zip(place, SIZES))
    return (4 * x + zh) * 16 + 4 * y + 2 * zl + core


def send(array, to):
    return lax.ppermute(array, ("row", "col"), [(number(p), number(to(*p))) for p in PLACES])


POWER = 13
LIFT = 120 / POWER
LOG_LIFT = LIFT * 0.6931471805599453


def split(norms):
    lead = norms.astype(BF16).astype(F32)
    trail = (norms - lead).astype(BF16).astype(F32)
    return lead, trail, lead + trail


def inverse(norms):
    return jnp.where(norms > 0, 1.0 / jnp.where(norms > 0, norms, 1.0), 0.0)


def raised(value, rows, cols):
    ratio = value * rows * (cols * 2.0**LIFT)
    p2 = ratio * ratio
    p4 = p2 * p2
    return p4 * p4 * (p4 * ratio)


def root(code, rows, cols):
    size = jnp.exp(jnp.log(jnp.abs(code)) * (1.0 / POWER) - LOG_LIFT)
    return jnp.where(code < 0, -size, size) * (rows * cols)


def upright(row):
    parts = [row[:, i : i + 128] for i in range(0, row.shape[1], 128)]
    return jnp.concatenate([jnp.broadcast_to(p, (128, 128)).T for p in parts], 0)


def dot(left, right, dim):
    return lax.dot_general(
        left, right, (((dim,), (dim,)), ((), ())), preferred_element_type=F32
    )


def run(body, outs, scratch, *args):
    smem, vmem = pl.BlockSpec(memory_space=pltpu.SMEM), pl.BlockSpec(memory_space=pltpu.VMEM)
    return pl.pallas_call(
        body,
        out_shape=[jax.ShapeDtypeStruct(shape, dtype) for shape, dtype in outs],
        in_specs=[smem] + [vmem] * (len(args) - 1),
        out_specs=[vmem] * len(outs),
        scratch_shapes=[pltpu.VMEM(shape, dtype) for shape, dtype in scratch],
        cost_estimate=pl.CostEstimate(flops=1000, bytes_accessed=1000, transcendentals=0),
        compiler_params=pltpu.CompilerParams(vmem_limit_bytes=48 * 1024 * 1024),
    )(*args)


BLOCK, CHUNK, TILES, WINDOW, IMAGE = 448, 112, 14, 1408, 384
WIDTH = WINDOW + IMAGE


def first_tile(d):
    return 7 * (d // 2) + 3 * (d % 2)


def lead_in(d):
    return 64 * (d % 2)


def tile(i):
    return pl.ds(pl.multiple_of(i * 128, 128), 128)


HALF_ROWS = BLOCK // 2
PARTS = [slice(i, min(i + 256, WINDOW)) for i in range(0, WINDOW, 256)]


def fill_window(g_ref, w_ref, l_ref, d):
    for t in range(11):
        w_ref[:, t * 128 : (t + 1) * 128] = g_ref[:, tile(lax.rem(first_tile(d) + t, TILES))]
    l_ref[...] = w_ref[:, :512].T


def tile_after(d):
    return pl.ds(pl.multiple_of(128 * (d % 2), 128), IMAGE)


def column_norms(w_ref):
    return jnp.sqrt(jnp.sum(jnp.square(w_ref[...].astype(F32)), 0, keepdims=True))


def padded(rows, count):
    rows = jnp.concatenate(rows, 0)
    return jnp.concatenate([rows, jnp.zeros((count - rows.shape[0], rows.shape[1]), F32)], 0)


def rows_of(r_ref, norms, d, start=0, count=BLOCK):
    r_ref[...] = upright(norms[:, :512])
    return r_ref[pl.ds(pl.multiple_of(lead_in(d) + start, 16), count), :]


def wide(rows, lanes):
    return rows if lanes.stop - lanes.start == 128 else jnp.concatenate([rows, rows], 1)


def product(l_ref, w_ref, lanes, d):
    left = l_ref[pl.ds(pl.multiple_of(lead_in(d), 64), BLOCK), :]
    return jnp.dot(left, w_ref[:, lanes], preferred_element_type=F32)


def right_far(at_ref, g_ref, out_a, out_b, w_ref, l_ref, r_ref):
    d = lax.rem(at_ref[0] + 2, 4)
    fill_window(g_ref, w_ref, l_ref, d)
    lead, trail, norms = split(column_norms(w_ref))
    tail = padded([lead, trail], 16).astype(BF16)
    cols = inverse(norms)
    rows = rows_of(r_ref, cols, d)
    for ref in (out_a, out_b):
        ref[HALF_ROWS:, :] = tail
    for lanes in PARTS:
        code = raised(product(l_ref, w_ref, lanes, d), wide(rows, lanes), cols[:, lanes]).astype(BF16)
        out_a[:HALF_ROWS, lanes] = code[:HALF_ROWS]
        out_b[:HALF_ROWS, lanes] = code[HALF_ROWS:]


def right_near(step, at_ref, g_ref, in_ref, out_ref, w_ref, l_ref, r_ref, p_ref):
    d = lax.rem(at_ref[0] + step, 4)
    start = 0 if step == 1 else HALF_ROWS
    fill_window(g_ref, w_ref, l_ref, d)
    tail = in_ref[HALF_ROWS:, :].astype(F32)
    theirs = tail[0:1] + tail[1:2]
    their_rows = rows_of(r_ref, theirs, d, start, HALF_ROWS)
    lead, trail, norms = split(jnp.sqrt(jnp.square(column_norms(w_ref)) + jnp.square(theirs)))
    out_ref[BLOCK:, :] = padded([lead, trail], 16).astype(BF16)
    cols = inverse(norms)
    rows = rows_of(r_ref, cols, d)
    here = slice(start, start + HALF_ROWS)
    for lanes in PARTS:
        part = p_ref.at[:, : lanes.stop - lanes.start]
        part[...] = product(l_ref, w_ref, lanes, d)
        part[here, :] += root(in_ref[:HALF_ROWS, lanes].astype(F32), wide(their_rows, lanes), theirs[:, lanes])
        out_ref[:BLOCK, lanes] = raised(part[...], wide(rows, lanes), cols[:, lanes]).astype(BF16)


def right_second(at_ref, g_ref, in_1, in_3, out_1, out_3, out_2, own_ref, w_ref, l_ref, r_ref, e_ref, t_ref):
    d, zh = at_ref[0], at_ref[1]
    fill_window(g_ref, w_ref, l_ref, d)
    squares, theirs = jnp.square(column_norms(w_ref)), []
    for ref in (in_1, in_3):
        tail = ref[BLOCK:, :].astype(F32)
        norms = tail[0:1] + tail[1:2]
        squares += jnp.square(norms)
        theirs.append((ref, norms, rows_of(r_ref, norms, d)))
    lead, trail, norms = split(jnp.sqrt(squares))
    cols = inverse(norms)
    rows = rows_of(r_ref, cols, d)
    begin = pl.multiple_of(lead_in(d), 64)
    e_ref[:64, :] = jnp.zeros((64, WINDOW), F32)
    e_ref[BLOCK:, :] = jnp.zeros((64, WINDOW), F32)
    for lanes in PARTS:
        part = product(l_ref, w_ref, lanes, d)
        for ref, their_cols, their_rows in theirs:
            part += root(ref[:BLOCK, lanes].astype(F32), wide(their_rows, lanes), their_cols[:, lanes])
        e_ref[pl.ds(begin, BLOCK), lanes] = raised(part, wide(rows, lanes), cols[:, lanes])
    for i in range(5):
        for j in range(4):
            t_ref[i * 128 : (i + 1) * 128, j * 128 : (j + 1) * 128] = e_ref[
                j * 128 : (j + 1) * 128, 384 + i * 128 : 512 + i * 128
            ].T
    tails = [jnp.concatenate([v[:, t * 128 : (t + 1) * 128] for t in range(11)], 0) for v in (lead, trail, norms)]
    for step, ref in ((1, out_1), (3, out_3), (2, out_2), (0, own_ref)):
        chunk = lax.rem(zh + step, 4) * CHUNK
        piece = e_ref[pl.ds(pl.multiple_of(begin + chunk, 16), CHUNK), :]
        image = t_ref[pl.ds(pl.multiple_of(64 + begin + chunk, 16), CHUNK), tile_after(d)]
        ref[:, :WINDOW] = piece.astype(ref.dtype)
        ref[:, WINDOW:WIDTH] = image.astype(ref.dtype)
        ref[:, WIDTH:] = padded(tails[:2] if step else tails[2:], CHUNK).astype(ref.dtype)


def right_third(scale, at_ref, own_ref, in_1, in_3, in_2, out_ref, image_ref, r_ref, n_ref):
    d, zh = at_ref[0], at_ref[1]
    begin = pl.multiple_of(lead_in(d) + zh * CHUNK, 16)
    for i, ref in enumerate((own_ref, in_1, in_3, in_2)):
        tail = ref[:, WIDTH:].astype(F32)
        n_ref[...] = tail[:11] if i == 0 else tail[:11] + tail[11:22]
        for t in range(8):
            r_ref[t * 128 : (t + 1) * 128, :] = upright(n_ref[t : t + 1, :])
        rows = r_ref[pl.ds(begin, CHUNK), :]
        image_rows = r_ref[pl.ds(pl.multiple_of(448 + begin, 16), CHUNK), :]
        for t in range(14):
            lanes = slice(t * 128, (t + 1) * 128)
            code = ref[:, lanes].astype(F32)
            if t < 11:
                to, here, part = out_ref, lanes, root(code, rows, n_ref[t : t + 1, :])
            else:
                here = slice((t - 11) * 128, (t - 10) * 128)
                cols = n_ref[pl.ds(t - 11 + lax.rem(d, 2), 1), :]
                to, part = image_ref, root(code, image_rows, cols)
            if i == 0:
                to[:, here] = part * scale
            else:
                to[:, here] += part * scale


def right_last(at_ref, base_ref, image_ref, out_ref):
    d = at_ref[0]
    for t in range(14):
        ref, i = (base_ref, t) if t < 11 else (image_ref, t - 11)
        out_ref[:, tile(lax.rem(first_tile(d) + t, TILES))] = ref[:, i * 128 : (i + 1) * 128]


SUB, ROWS = 128, 2048


def sub(i):
    return pl.ds(pl.multiple_of(i * SUB, SUB), SUB)


def two_cols(ref, core, b):
    return jnp.concatenate([ref[pl.ds(4 * b + core + 2 * zl, 1), :] for zl in (0, 1)], 1)


def left_first(at_ref, far, near, far_2, near_2, out_1, out_3, out_2, own_ref, norm_ref, a_ref, b_ref, i_ref, s_ref):
    zh, y, core = at_ref[1], at_ref[2], at_ref[4]
    for p, ref in enumerate((far, near, far_2, near_2)):
        j = 2 * ((p // 2) ^ core) + lax.rem(p + zh, 2)
        a_ref[pl.ds(pl.multiple_of(j * 512, 512), 512), :] = ref[...]
    leads, trails, lanes = [], [], []
    for i in range(16):
        rows = slice(i * SUB, (i + 1) * SUB)
        squares = jnp.sum(jnp.square(a_ref[rows, :].astype(F32)), 1, keepdims=True)
        row = jnp.broadcast_to(jnp.sqrt(squares), (SUB, SUB)).T[0:1]
        lead, trail, norms = split(row)
        leads.append(lead), trails.append(trail), lanes.append(norms)
        i_ref[rows, :] = upright(inverse(norms))
    tail = jnp.concatenate([jnp.concatenate(leads, 0), jnp.concatenate(trails, 0)], 1).astype(BF16)
    norm_ref[...] = jnp.concatenate(lanes, 0)
    s_ref[...] = inverse(norm_ref[...])
    for step, out in ((1, out_1), (3, out_3), (2, out_2), (0, own_ref)):
        b = lax.rem(y + step, 4)
        for zl in (0, 1):
            b_ref[zl * SUB : (zl + 1) * SUB, :] = a_ref[sub(4 * b + core + 2 * zl), :]
        cols = two_cols(s_ref, core, b)
        for k in range(0, ROWS, 512):
            rows = slice(k, k + 512)
            part = dot(a_ref[rows, :], b_ref[...], 1)
            if step:
                scale = i_ref[rows, :]
                part = raised(part, jnp.concatenate([scale, scale], 1), cols).astype(BF16)
            out[rows, :] = part
        if step:
            out[ROWS:, :] = tail


def left_second(at_ref, own_ref, norm_ref, in_1, in_3, in_2, *refs):
    outs, (e_ref, s_ref, lead_ref, trail_ref, n_ref) = refs[:8], refs[8:]
    zh, y, zl, core = (at_ref[i] for i in (1, 2, 3, 4))
    squares = jnp.square(norm_ref[...])
    for k, ref in enumerate((in_1, in_3, in_2)):
        tail = ref[ROWS:, :].astype(F32)
        norms = tail[:, :SUB] + tail[:, SUB:]
        squares += jnp.square(norms)
        s_ref[k] = norms
    lead_ref[...], trail_ref[...], n_ref[...] = split(jnp.sqrt(squares))
    s_ref[3] = inverse(n_ref[...])
    cols = [two_cols(s_ref.at[k], core, y) for k in range(4)]
    for i in range(16):
        rows = slice(i * SUB, (i + 1) * SUB)
        scales = [upright(s_ref[k, i : i + 1, :]) for k in range(4)]
        scales = [jnp.concatenate([scale, scale], 1) for scale in scales]
        part = own_ref[rows, :]
        for k, ref in enumerate((in_1, in_3, in_2)):
            part += root(ref[rows, :].astype(F32), scales[k], cols[k])
        e_ref[rows, :] = raised(part, scales[3], cols[3])
    for step, out in zip((*Z_STEPS, 0), outs):
        z = lax.rem(2 * zh + zl + step, 8)
        to_h, to_l = z // 2, lax.rem(z, 2)
        out[:512, :] = e_ref[pl.ds(pl.multiple_of(to_h * 512, 512), 512), tile(to_l)].astype(out.dtype)
        picks = [4 * to_h + m for m in range(4)] + [4 * y + 2 * to_l + core]
        tail = [ref[pl.ds(i, 1), :] for ref in ((lead_ref, trail_ref) if step else (n_ref,)) for i in picks]
        out[512:, :] = padded(tail, 16).astype(out.dtype)


def left_third(scale, *refs):
    out_ref = refs[9]
    for k, ref in enumerate(refs[1:9]):
        tail = ref[512:, :].astype(F32)
        norms = tail[0:5] if k == 0 else tail[0:5] + tail[5:10]
        for j in range(4):
            rows = slice(j * SUB, (j + 1) * SUB)
            part = root(ref[rows, :].astype(F32), upright(norms[j : j + 1]), norms[4:5]) * scale
            if k == 0:
                out_ref[rows, :] = part
            else:
                out_ref[rows, :] += part


def along_z(step):
    def to(x, zh, y, zl, core):
        z = (2 * zh + zl + step) % 8
        return (x, z // 2, y, z % 2, core)

    return to


def shards(gradient):
    rows, width = gradient.shape
    row, col = lax.axis_index("row"), lax.axis_index("col")
    x, zh, y, zl, core = row // 4, row % 4, col // 4, col // 2 % 2, col % 2
    at = jnp.stack([x, zh, y, zl, core, x, x, x]).astype(jnp.int32)
    barrier = lax.optimization_barrier
    half = width // 2

    cut = lambda parity: lax.dynamic_slice_in_dim(gradient, parity * half, half, 1)
    near, far, gradient = barrier((cut((zh + 1) % 2), cut(zh % 2), gradient))
    near = send(near, lambda x, zh, y, zl, core: (x, 2 * core + (zh + 1) % 2, y, zl, zh // 2))

    window = [((rows, WINDOW), BF16), ((512, 512), BF16), ((512, 128), F32)]
    half_part, whole_part = ((HALF_ROWS + 16, WINDOW), BF16), ((BLOCK + 16, WINDOW), BF16)
    over_x = lambda s, v: send(v, lambda x, zh, y, zl, core: (x + s, zh, y, zl, core))
    far_1, far_3 = run(right_far, [half_part] * 2, window, at, gradient)
    far_1, far_3 = over_x(1, far_1), over_x(3, far_3)
    near, far, far_1, far_3 = barrier((near, far, far_1, far_3))
    far = send(far, lambda x, zh, y, zl, core: (x, 2 * core + zh % 2, y, zl, zh // 2))
    add = lambda s, v: run(
        functools.partial(right_near, s), [whole_part], window + [((BLOCK, 256), F32)], at, gradient, v
    )[0]
    code_1, code_3 = add(1, far_1), add(3, far_3)
    right_1, right_3 = over_x(1, code_1), over_x(3, code_3)

    swap = lambda x, zh, y, zl, core: (x, zh, y, zl, 1 - core)
    far_2, near_2 = send(far, swap), send(near, swap)

    far, near, far_2, near_2, right_1, right_3 = barrier((far, near, far_2, near_2, right_1, right_3))
    packed = (ROWS + 16, 256)
    left_1, left_3, left_2, left_own, norms = run(
        left_first,
        [(packed, BF16)] * 3 + [((ROWS, 256), F32), ((16, SUB), F32)],
        [((2048, half), BF16), ((256, half), BF16), ((2048, SUB), F32), ((16, SUB), F32)],
        at,
        far,
        near,
        far_2,
        near_2,
    )
    over_y = lambda s, v: send(v, lambda x, zh, y, zl, core: (x, zh, y + s, zl, core))
    right_1, right_3, _ = barrier((right_1, right_3, left_2))
    left_1, left_3, left_2 = over_y(1, left_1), over_y(3, left_3), over_y(2, left_2)

    piece = (CHUNK, WIDTH + 128)
    code_1, code_3, code_2, right_own = run(
        right_second,
        [(piece, BF16)] * 3 + [(piece, F32)],
        window + [((512, WINDOW), F32), ((640, 512), F32)],
        at,
        gradient,
        right_1,
        right_3,
    )
    over_z = lambda s, v: send(v, lambda x, zh, y, zl, core: (x, zh + s, y, zl, core))
    right_1, right_3, right_2 = over_z(1, code_1), over_z(3, code_3), over_z(2, code_2)

    piece = (512 + 16, SUB)
    codes = run(
        left_second,
        [(piece, BF16)] * 7 + [(piece, F32)],
        [((ROWS, 256), F32), ((4, 16, SUB), F32)] + [((16, SUB), F32)] * 3,
        at,
        left_own,
        norms,
        left_1,
        left_3,
        left_2,
    )
    arrived = [send(code, along_z(s)) for s, code in zip(Z_STEPS, codes)]
    right_1, right_3, _ = barrier((right_1, right_3, codes))

    right_base, image = run(
        functools.partial(right_third, 1.0 / (rows * 16)),
        [((CHUNK, WINDOW), F32), ((CHUNK, IMAGE), F32)],
        [((1024, 128), F32), ((11, 128), F32)],
        at,
        right_own,
        right_1,
        right_3,
        right_2,
    )
    image = over_x(1, image)
    arrived, image = barrier((arrived, image))
    right_gram = run(right_last, [((CHUNK, width), F32)], [], at, right_base, image)[0]

    left_gram = run(
        functools.partial(left_third, 1.0 / (width * 16)), [((512, SUB), F32)], [], at, codes[7], *arrived
    )[0]
    return (left_gram, right_gram)


def solution(mesh):
    in_specs = (P("row", "col"),)
    out_specs = (P("row", "col"), P(("col", "row"), None))
    return jax.shard_map(shards, mesh=mesh, in_specs=in_specs, out_specs=out_specs, check_vma=False)
```

```python
import functools
import itertools

import jax
import jax.numpy as jnp
from jax import lax
from jax.experimental import pallas as pl
from jax.experimental.pallas import tpu as pltpu
from jax.sharding import PartitionSpec as P

F32, BF16 = jnp.float32, jnp.bfloat16

SIZES = (4, 4, 4, 2, 2)
PLACES = list(itertools.product(*(range(n) for n in SIZES)))
STEPS = (1, 3, 2)
Z_STEPS = (1, 7, 2, 6, 3, 5, 4)


def number(place):
    x, zh, y, zl, core = (p % n for p, n in zip(place, SIZES))
    return (4 * x + zh) * 16 + 4 * y + 2 * zl + core


def send(array, to):
    return lax.ppermute(array, ("row", "col"), [(number(p), number(to(*p))) for p in PLACES])


POWER = 13
LIFT = 120 / POWER
LOG_LIFT = LIFT * 0.6931471805599453


def split(norms):
    lead = norms.astype(BF16).astype(F32)
    trail = (norms - lead).astype(BF16).astype(F32)
    return lead, trail, lead + trail


def inverse(norms):
    return jnp.where(norms > 0, 1.0 / jnp.where(norms > 0, norms, 1.0), 0.0)


def raised(value, rows, cols):
    ratio = value * rows * (cols * 2.0**LIFT)
    p2 = ratio * ratio
    p4 = p2 * p2
    return p4 * p4 * (p4 * ratio)


def root(code, rows, cols):
    size = jnp.exp(jnp.log(jnp.abs(code)) * (1.0 / POWER) - LOG_LIFT)
    return jnp.where(code < 0, -size, size) * (rows * cols)


def upright(row):
    parts = [row[:, i : i + 128] for i in range(0, row.shape[1], 128)]
    return jnp.concatenate([jnp.broadcast_to(p, (128, 128)).T for p in parts], 0)


def dot(left, right, dim):
    return lax.dot_general(
        left, right, (((dim,), (dim,)), ((), ())), preferred_element_type=F32
    )


def run(body, outs, scratch, *args):
    smem, vmem = pl.BlockSpec(memory_space=pltpu.SMEM), pl.BlockSpec(memory_space=pltpu.VMEM)
    return pl.pallas_call(
        body,
        out_shape=[jax.ShapeDtypeStruct(shape, dtype) for shape, dtype in outs],
        in_specs=[smem] + [vmem] * (len(args) - 1),
        out_specs=[vmem] * len(outs),
        scratch_shapes=[pltpu.VMEM(shape, dtype) for shape, dtype in scratch],
        cost_estimate=pl.CostEstimate(flops=1000, bytes_accessed=1000, transcendentals=0),
        compiler_params=pltpu.CompilerParams(vmem_limit_bytes=48 * 1024 * 1024),
    )(*args)


BLOCK, CHUNK, TILES, WINDOW, IMAGE = 448, 112, 14, 1408, 384
WIDTH = WINDOW + IMAGE


def first_tile(d):
    return 7 * (d // 2) + 3 * (d % 2)


def lead_in(d):
    return 64 * (d % 2)


def tile(i):
    return pl.ds(pl.multiple_of(i * 128, 128), 128)


HALF_ROWS = BLOCK // 2
PARTS = [slice(i, min(i + 256, WINDOW)) for i in range(0, WINDOW, 256)]


def fill_window(g_ref, w_ref, l_ref, d):
    for t in range(11):
        w_ref[:, t * 128 : (t + 1) * 128] = g_ref[:, tile(lax.rem(first_tile(d) + t, TILES))]
    l_ref[...] = w_ref[:, :512].T


def tile_after(d):
    return pl.ds(pl.multiple_of(128 * (d % 2), 128), IMAGE)


def column_norms(w_ref):
    return jnp.sqrt(jnp.sum(jnp.square(w_ref[...].astype(F32)), 0, keepdims=True))


def padded(rows, count):
    rows = jnp.concatenate(rows, 0)
    return jnp.concatenate([rows, jnp.zeros((count - rows.shape[0], rows.shape[1]), F32)], 0)


def rows_of(r_ref, norms, d, start=0, count=BLOCK):
    r_ref[...] = upright(norms[:, :512])
    return r_ref[pl.ds(pl.multiple_of(lead_in(d) + start, 16), count), :]


def wide(rows, lanes):
    return rows if lanes.stop - lanes.start == 128 else jnp.concatenate([rows, rows], 1)


def product(l_ref, w_ref, lanes, d):
    left = l_ref[pl.ds(pl.multiple_of(lead_in(d), 64), BLOCK), :]
    return jnp.dot(left, w_ref[:, lanes], preferred_element_type=F32)


def right_far(at_ref, g_ref, out_a, out_b, w_ref, l_ref, r_ref):
    d = lax.rem(at_ref[0] + 2, 4)
    fill_window(g_ref, w_ref, l_ref, d)
    lead, trail, norms = split(column_norms(w_ref))
    tail = padded([lead, trail], 16).astype(BF16)
    cols = inverse(norms)
    rows = rows_of(r_ref, cols, d)
    for ref in (out_a, out_b):
        ref[HALF_ROWS:, :] = tail
    for lanes in PARTS:
        code = raised(product(l_ref, w_ref, lanes, d), wide(rows, lanes), cols[:, lanes]).astype(BF16)
        out_a[:HALF_ROWS, lanes] = code[:HALF_ROWS]
        out_b[:HALF_ROWS, lanes] = code[HALF_ROWS:]


def right_near(step, at_ref, g_ref, in_ref, out_ref, w_ref, l_ref, r_ref, p_ref):
    d = lax.rem(at_ref[0] + step, 4)
    start = 0 if step == 1 else HALF_ROWS
    fill_window(g_ref, w_ref, l_ref, d)
    tail = in_ref[HALF_ROWS:, :].astype(F32)
    theirs = tail[0:1] + tail[1:2]
    their_rows = rows_of(r_ref, theirs, d, start, HALF_ROWS)
    lead, trail, norms = split(jnp.sqrt(jnp.square(column_norms(w_ref)) + jnp.square(theirs)))
    out_ref[BLOCK:, :] = padded([lead, trail], 16).astype(BF16)
    cols = inverse(norms)
    rows = rows_of(r_ref, cols, d)
    here = slice(start, start + HALF_ROWS)
    for lanes in PARTS:
        part = p_ref.at[:, : lanes.stop - lanes.start]
        part[...] = product(l_ref, w_ref, lanes, d)
        part[here, :] += root(in_ref[:HALF_ROWS, lanes].astype(F32), wide(their_rows, lanes), theirs[:, lanes])
        out_ref[:BLOCK, lanes] = raised(part[...], wide(rows, lanes), cols[:, lanes]).astype(BF16)


def right_second(at_ref, g_ref, in_1, in_3, out_1, out_3, out_2, own_ref, w_ref, l_ref, r_ref, e_ref, t_ref):
    d, zh = at_ref[0], at_ref[1]
    fill_window(g_ref, w_ref, l_ref, d)
    squares, theirs = jnp.square(column_norms(w_ref)), []
    for ref in (in_1, in_3):
        tail = ref[BLOCK:, :].astype(F32)
        norms = tail[0:1] + tail[1:2]
        squares += jnp.square(norms)
        theirs.append((ref, norms, rows_of(r_ref, norms, d)))
    lead, trail, norms = split(jnp.sqrt(squares))
    cols = inverse(norms)
    rows = rows_of(r_ref, cols, d)
    begin = pl.multiple_of(lead_in(d), 64)
    e_ref[:64, :] = jnp.zeros((64, WINDOW), F32)
    e_ref[BLOCK:, :] = jnp.zeros((64, WINDOW), F32)
    for lanes in PARTS:
        part = product(l_ref, w_ref, lanes, d)
        for ref, their_cols, their_rows in theirs:
            part += root(ref[:BLOCK, lanes].astype(F32), wide(their_rows, lanes), their_cols[:, lanes])
        e_ref[pl.ds(begin, BLOCK), lanes] = raised(part, wide(rows, lanes), cols[:, lanes])
    for i in range(5):
        for j in range(4):
            t_ref[i * 128 : (i + 1) * 128, j * 128 : (j + 1) * 128] = e_ref[
                j * 128 : (j + 1) * 128, 384 + i * 128 : 512 + i * 128
            ].T
    tails = [jnp.concatenate([v[:, t * 128 : (t + 1) * 128] for t in range(11)], 0) for v in (lead, trail, norms)]
    for step, ref in ((1, out_1), (3, out_3), (2, out_2), (0, own_ref)):
        chunk = lax.rem(zh + step, 4) * CHUNK
        piece = e_ref[pl.ds(pl.multiple_of(begin + chunk, 16), CHUNK), :]
        image = t_ref[pl.ds(pl.multiple_of(64 + begin + chunk, 16), CHUNK), tile_after(d)]
        ref[:, :WINDOW] = piece.astype(ref.dtype)
        ref[:, WINDOW:WIDTH] = image.astype(ref.dtype)
        ref[:, WIDTH:] = padded(tails[:2] if step else tails[2:], CHUNK).astype(ref.dtype)


def right_third(scale, at_ref, own_ref, in_1, in_3, in_2, out_ref, image_ref, r_ref, n_ref):
    d, zh = at_ref[0], at_ref[1]
    begin = pl.multiple_of(lead_in(d) + zh * CHUNK, 16)
    for i, ref in enumerate((own_ref, in_1, in_3, in_2)):
        tail = ref[:, WIDTH:].astype(F32)
        n_ref[...] = tail[:11] if i == 0 else tail[:11] + tail[11:22]
        for t in range(8):
            r_ref[t * 128 : (t + 1) * 128, :] = upright(n_ref[t : t + 1, :])
        rows = r_ref[pl.ds(begin, CHUNK), :]
        image_rows = r_ref[pl.ds(pl.multiple_of(448 + begin, 16), CHUNK), :]
        for t in range(14):
            lanes = slice(t * 128, (t + 1) * 128)
            code = ref[:, lanes].astype(F32)
            if t < 11:
                to, here, part = out_ref, lanes, root(code, rows, n_ref[t : t + 1, :])
            else:
                here = slice((t - 11) * 128, (t - 10) * 128)
                cols = n_ref[pl.ds(t - 11 + lax.rem(d, 2), 1), :]
                to, part = image_ref, root(code, image_rows, cols)
            if i == 0:
                to[:, here] = part * scale
            else:
                to[:, here] += part * scale


def right_last(at_ref, base_ref, image_ref, out_ref):
    d = at_ref[0]
    for t in range(14):
        ref, i = (base_ref, t) if t < 11 else (image_ref, t - 11)
        out_ref[:, tile(lax.rem(first_tile(d) + t, TILES))] = ref[:, i * 128 : (i + 1) * 128]


SUB, BASE, ROWS = 128, 1024, 1152


def sub(i):
    return pl.ds(pl.multiple_of(i * SUB, SUB), SUB)


def base_subs(core, b):
    return [4 * a + (core ^ (a > b).astype(jnp.int32)) + 2 * h for a in range(4) for h in (0, 1)]


def slot(i):
    return i // 4 * 4 + 2 * (i % 2) + i // 2 % 2


def more_sub(core, b, zl):
    return 4 * b + lax.rem(2 * zl + core + 1, 4)


def two_cols(ref, core, b):
    return jnp.concatenate([ref[pl.ds(4 * b + core + 2 * zl, 1), :] for zl in (0, 1)], 1)


def left_first(at_ref, far, near, far_2, near_2, out_1, out_3, out_2, own_ref, norm_ref, a_ref, b_ref, i_ref, s_ref):
    zh, y, core = at_ref[1], at_ref[2], at_ref[4]
    for p, ref in enumerate((far, near, far_2, near_2)):
        j = 2 * ((p // 2) ^ core) + lax.rem(p + zh, 2)
        for m in range(4):
            a_ref[sub(4 * j + slot(m)), :] = ref[m * SUB : (m + 1) * SUB, :]
    leads, trails, lanes = [], [], []
    for i in range(16):
        rows = slice(slot(i) * SUB, (slot(i) + 1) * SUB)
        squares = jnp.sum(jnp.square(a_ref[rows, :].astype(F32)), 1, keepdims=True)
        row = jnp.broadcast_to(jnp.sqrt(squares), (SUB, SUB)).T[0:1]
        lead, trail, norms = split(row)
        leads.append(lead), trails.append(trail), lanes.append(norms)
        i_ref[rows, :] = upright(inverse(norms))
    tail = jnp.concatenate([jnp.concatenate(leads, 0), jnp.concatenate(trails, 0)], 1).astype(BF16)
    norm_ref[...] = jnp.concatenate(lanes, 0)
    s_ref[...] = inverse(norm_ref[...])
    for step, out in ((1, out_1), (3, out_3), (2, out_2), (0, own_ref)):
        b = lax.rem(y + step, 4)
        for zl in (0, 1):
            b_ref[zl * SUB : (zl + 1) * SUB, :] = a_ref[sub(slot(4 * b + core + 2 * zl)), :]
        cols = two_cols(s_ref, core, b)
        for k, i in enumerate(base_subs(core, b)[::2]):
            pair = pl.ds(pl.multiple_of(slot(i) * SUB, 2 * SUB), 2 * SUB)
            part = dot(a_ref[pair, :], b_ref[...], 1)
            if step:
                scale = i_ref[pair, :]
                part = raised(part, jnp.concatenate([scale, scale], 1), cols).astype(BF16)
            out[k * 2 * SUB : (k + 1) * 2 * SUB, :] = part
        for zl in (0, 1):
            here = slice(zl * SUB, (zl + 1) * SUB)
            i = slot(more_sub(core, b, zl))
            part = dot(a_ref[sub(i), :], b_ref[here, :], 1)
            if step:
                part = raised(part, i_ref[sub(i), :], cols[:, here]).astype(BF16)
            out[BASE:ROWS, here] = part
        if step:
            out[ROWS:, :] = tail


def left_second(at_ref, own_ref, norm_ref, in_1, in_3, in_2, *refs):
    outs, (e_ref, s_ref, lead_ref, trail_ref, n_ref) = refs[:8], refs[8:]
    zh, y, zl, core = (at_ref[i] for i in (1, 2, 3, 4))
    squares = jnp.square(norm_ref[...])
    for k, ref in enumerate((in_1, in_3, in_2)):
        tail = ref[ROWS:, :].astype(F32)
        norms = tail[:, :SUB] + tail[:, SUB:]
        squares += jnp.square(norms)
        s_ref[k] = norms
    lead_ref[...], trail_ref[...], n_ref[...] = split(jnp.sqrt(squares))
    s_ref[3] = inverse(n_ref[...])
    sources = [(ref, k) for k, ref in enumerate((in_1, in_3, in_2))]
    cols = [two_cols(s_ref.at[k], core, y) for k in range(4)]
    r = lambda k, i: upright(s_ref.at[k][pl.ds(i, 1), :])
    for j, i in enumerate(base_subs(core, y)):
        rows = slice(j * SUB, (j + 1) * SUB)
        part = own_ref[rows, :]
        for ref, k in sources:
            scale = r(k, i)
            part += root(ref[rows, :].astype(F32), jnp.concatenate([scale, scale], 1), cols[k])
        scale = r(3, i)
        e_ref[rows, :] = raised(part, jnp.concatenate([scale, scale], 1), cols[3])
    for l in (0, 1):
        here = slice(l * SUB, (l + 1) * SUB)
        i = more_sub(core, y, l)
        part = own_ref[BASE:ROWS, here]
        for ref, k in sources:
            part += root(ref[BASE:ROWS, here].astype(F32), r(k, i), cols[k][:, here])
        e_ref[BASE:ROWS, here] = raised(part, r(3, i), cols[3][:, here])
    for step, out in zip((*Z_STEPS, 0), outs):
        z = lax.rem(2 * zh + zl + step, 8)
        to_h, to_l = z // 2, lax.rem(z, 2)
        lanes = tile(to_l)
        out[:256, :] = e_ref[pl.ds(pl.multiple_of(to_h * 256, 256), 256), lanes].astype(out.dtype)
        out[256:384, :] = e_ref[BASE:ROWS, lanes].astype(out.dtype)
        first = 4 * to_h + (core ^ (to_h > y).astype(jnp.int32))
        picks = [first, first + 2, more_sub(core, y, to_l), 4 * y + 2 * to_l + core]
        tail = [ref[pl.ds(i, 1), :] for ref in ((lead_ref, trail_ref) if step else (n_ref,)) for i in picks]
        out[384:, :] = padded(tail, 16).astype(out.dtype)


def left_third(scale, at_ref, *refs):
    sources, (base_ref, more_ref, same_ref, other_ref, sum_ref) = refs[:8], refs[8:]
    zh, y, zl = at_ref[1], at_ref[2], at_ref[3]
    for k, ref in enumerate(sources):
        tail = ref[384:, :].astype(F32)
        norms = tail[0:4] if k == 0 else tail[0:4] + tail[4:8]
        for j in range(3):
            rows = slice(j * SUB, (j + 1) * SUB)
            part = root(ref[rows, :].astype(F32), upright(norms[j : j + 1]), norms[3:4]) * scale
            if k == 0:
                sum_ref[rows, :] = part
            else:
                sum_ref[rows, :] += part
    first, second, more = (sum_ref[j * SUB : (j + 1) * SUB, :] for j in range(3))
    base_ref[...] = sum_ref[:256, :]
    more_ref[...] = more
    same_ref[...] = jnp.where(zh == y, more, jnp.where(zl == 0, first, second)).T
    other_ref[...] = jnp.where(zl == 0, second, first).T


def left_last(at_ref, base_ref, more_ref, same_ref, other_ref, out_ref):
    zh, y, zl, core = (at_ref[i] for i in (1, 2, 3, 4))
    n, parity, diagonal = 2 * zl + core, core ^ (zh > y).astype(jnp.int32), zh == y
    out_ref[sub(parity), :] = base_ref[:SUB, :]
    out_ref[sub(parity + 2), :] = base_ref[SUB:, :]
    out_ref[sub(jnp.where(diagonal, lax.rem(n + 3, 4), 2 * zl + 1 - parity)), :] = same_ref[...]
    out_ref[sub(jnp.where(diagonal, lax.rem(n + 1, 4), 2 * (1 - zl) + 1 - parity)), :] = jnp.where(
        diagonal, more_ref[...], other_ref[...]
    )


def mirror(step):
    def to(x, zh, y, zl, core):
        if zh != y:
            return (x, y, zh, zl ^ step, core ^ (zh > y))
        n = (2 * zl + core + 1 - step) % 4
        return (x, zh, y, n // 2, n % 2)

    return to


def along_z(step):
    def to(x, zh, y, zl, core):
        z = (2 * zh + zl + step) % 8
        return (x, z // 2, y, z % 2, core)

    return to


def shards(gradient):
    rows, width = gradient.shape
    row, col = lax.axis_index("row"), lax.axis_index("col")
    x, zh, y, zl, core = row // 4, row % 4, col // 4, col // 2 % 2, col % 2
    at = jnp.stack([x, zh, y, zl, core, x, x, x]).astype(jnp.int32)
    barrier = lax.optimization_barrier
    half = width // 2

    cut = lambda parity: lax.dynamic_slice_in_dim(gradient, parity * half, half, 1)
    near, far, gradient = barrier((cut((zh + 1) % 2), cut(zh % 2), gradient))
    near = send(near, lambda x, zh, y, zl, core: (x, 2 * core + (zh + 1) % 2, y, zl, zh // 2))

    window = [((rows, WINDOW), BF16), ((512, 512), BF16), ((512, 128), F32)]
    half_part, whole_part = ((HALF_ROWS + 16, WINDOW), BF16), ((BLOCK + 16, WINDOW), BF16)
    over_x = lambda s, v: send(v, lambda x, zh, y, zl, core: (x + s, zh, y, zl, core))
    far_1, far_3 = run(right_far, [half_part] * 2, window, at, gradient)
    far_1, far_3 = over_x(1, far_1), over_x(3, far_3)
    near, far, far_1, far_3 = barrier((near, far, far_1, far_3))
    far = send(far, lambda x, zh, y, zl, core: (x, 2 * core + zh % 2, y, zl, zh // 2))
    add = lambda s, v: run(
        functools.partial(right_near, s), [whole_part], window + [((BLOCK, 256), F32)], at, gradient, v
    )[0]
    code_1, code_3 = add(1, far_1), add(3, far_3)
    right_1, right_3 = over_x(1, code_1), over_x(3, code_3)

    swap = lambda x, zh, y, zl, core: (x, zh, y, zl, 1 - core)
    far_2, near_2 = send(far, swap), send(near, swap)

    piece = (CHUNK, WIDTH + 128)
    code_1, code_3, code_2, right_own = run(
        right_second,
        [(piece, BF16)] * 3 + [(piece, F32)],
        window + [((512, WINDOW), F32), ((640, 512), F32)],
        at,
        gradient,
        right_1,
        right_3,
    )
    over_z = lambda s, v: send(v, lambda x, zh, y, zl, core: (x, zh + s, y, zl, core))
    right_1, right_3 = over_z(1, code_1), over_z(3, code_3)

    far, near, far_2, near_2, _ = barrier((far, near, far_2, near_2, code_1))
    packed = (ROWS + 16, 256)
    left_1, left_3, left_2, left_own, norms = run(
        left_first,
        [(packed, BF16)] * 3 + [((ROWS, 256), F32), ((16, SUB), F32)],
        [((2048, half), BF16), ((256, half), BF16), ((2048, SUB), F32), ((16, SUB), F32)],
        at,
        far,
        near,
        far_2,
        near_2,
    )
    over_y = lambda s, v: send(v, lambda x, zh, y, zl, core: (x, zh, y + s, zl, core))
    left_1, left_3 = over_y(1, left_1), over_y(3, left_3)
    left_2, right_1, right_3 = barrier((left_2, right_1, right_3))
    left_1, left_3, code_2, right_1, right_3 = barrier((left_1, left_3, code_2, right_1, right_3))
    left_2, right_2 = over_y(2, left_2), over_z(2, code_2)

    piece = (400, SUB)
    codes = run(
        left_second,
        [(piece, BF16)] * 7 + [(piece, F32)],
        [((ROWS, 256), F32), ((4, 16, SUB), F32)] + [((16, SUB), F32)] * 3,
        at,
        left_own,
        norms,
        left_1,
        left_3,
        left_2,
    )
    arrived = [send(code, along_z(s)) for s, code in zip(Z_STEPS, codes)]
    right_1, right_3, _ = barrier((right_1, right_3, codes))

    right_base, image = run(
        functools.partial(right_third, 1.0 / (rows * 16)),
        [((CHUNK, WINDOW), F32), ((CHUNK, IMAGE), F32)],
        [((1024, 128), F32), ((11, 128), F32)],
        at,
        right_own,
        right_1,
        right_3,
        right_2,
    )
    arrived, image = barrier((arrived, image))
    image = over_x(1, image)
    right_gram = run(right_last, [((CHUNK, width), F32)], [], at, right_base, image)[0]

    square = ((SUB, SUB), F32)
    base, more, same, other = run(
        functools.partial(left_third, 1.0 / (width * 16)),
        [((256, SUB), F32), square, square, square],
        [((384, SUB), F32)],
        at,
        codes[7],
        *arrived,
    )
    same, other = send(same, mirror(0)), send(other, mirror(1))
    left_gram = run(left_last, [((512, SUB), F32)], [], at, base, more, same, other)[0]
    return (left_gram, right_gram)


def solution(mesh):
    in_specs = (P("row", "col"),)
    out_specs = (P("row", "col"), P(("col", "row"), None))
    return jax.shard_map(shards, mesh=mesh, in_specs=in_specs, out_specs=out_specs, check_vma=False)
```

```python
import functools
import itertools

import jax
import jax.numpy as jnp
from jax import lax
from jax.experimental import pallas as pl
from jax.experimental.pallas import tpu as pltpu
from jax.sharding import PartitionSpec as P

F32, BF16 = jnp.float32, jnp.bfloat16

SIZES = (4, 4, 4, 2, 2)
PLACES = list(itertools.product(*(range(n) for n in SIZES)))
STEPS = (1, 3, 2)
Z_STEPS = (4, 3, 5, 2, 6, 1, 7)


def number(place):
    x, zh, y, zl, core = (p % n for p, n in zip(place, SIZES))
    return (4 * x + zh) * 16 + 4 * y + 2 * zl + core


def send(array, to):
    return lax.ppermute(array, ("row", "col"), [(number(p), number(to(*p))) for p in PLACES])


POWER = 13
LIFT = 120 / POWER
LOG_LIFT = LIFT * 0.6931471805599453


def split(norms):
    lead = norms.astype(BF16).astype(F32)
    trail = (norms - lead).astype(BF16).astype(F32)
    return lead, trail, lead + trail


def inverse(norms):
    return jnp.where(norms > 0, 1.0 / jnp.where(norms > 0, norms, 1.0), 0.0)


def raised(value, rows, cols):
    ratio = value * rows * (cols * 2.0**LIFT)
    p2 = ratio * ratio
    p4 = p2 * p2
    return p4 * p4 * (p4 * ratio)


def root(code, rows, cols):
    size = jnp.exp(jnp.log(jnp.abs(code)) * (1.0 / POWER) - LOG_LIFT)
    return jnp.where(code < 0, -size, size) * (rows * cols)


def upright(row):
    parts = [row[:, i : i + 128] for i in range(0, row.shape[1], 128)]
    return jnp.concatenate([jnp.broadcast_to(p, (128, 128)).T for p in parts], 0)


def dot(left, right, dim):
    return lax.dot_general(
        left, right, (((dim,), (dim,)), ((), ())), preferred_element_type=F32
    )


def run(body, outs, scratch, *args):
    smem, vmem = pl.BlockSpec(memory_space=pltpu.SMEM), pl.BlockSpec(memory_space=pltpu.VMEM)
    return pl.pallas_call(
        body,
        out_shape=[jax.ShapeDtypeStruct(shape, dtype) for shape, dtype in outs],
        in_specs=[smem] + [vmem] * (len(args) - 1),
        out_specs=[vmem] * len(outs),
        scratch_shapes=[pltpu.VMEM(shape, dtype) for shape, dtype in scratch],
        cost_estimate=pl.CostEstimate(flops=1000, bytes_accessed=1000, transcendentals=0),
        compiler_params=pltpu.CompilerParams(vmem_limit_bytes=48 * 1024 * 1024),
    )(*args)


BLOCK, CHUNK, TILES, WINDOW, IMAGE = 448, 112, 14, 1408, 384
WIDTH = WINDOW + IMAGE


def first_tile(d):
    return 7 * (d // 2) + 3 * (d % 2)


def lead_in(d):
    return 64 * (d % 2)


def tile(i):
    return pl.ds(pl.multiple_of(i * 128, 128), 128)


HALF_ROWS = BLOCK // 2
PARTS = [slice(i, min(i + 256, WINDOW)) for i in range(0, WINDOW, 256)]


def fill_window(g_ref, w_ref, l_ref, d):
    for t in range(11):
        w_ref[:, t * 128 : (t + 1) * 128] = g_ref[:, tile(lax.rem(first_tile(d) + t, TILES))]
    l_ref[...] = w_ref[:, :512].T


def tile_after(d):
    return pl.ds(pl.multiple_of(128 * (d % 2), 128), IMAGE)


def column_norms(w_ref):
    return jnp.sqrt(jnp.sum(jnp.square(w_ref[...].astype(F32)), 0, keepdims=True))


def padded(rows, count):
    rows = jnp.concatenate(rows, 0)
    return jnp.concatenate([rows, jnp.zeros((count - rows.shape[0], rows.shape[1]), F32)], 0)


def rows_of(r_ref, norms, d, start=0, count=BLOCK):
    r_ref[...] = upright(norms[:, :512])
    return r_ref[pl.ds(pl.multiple_of(lead_in(d) + start, 16), count), :]


def wide(rows, lanes):
    return rows if lanes.stop - lanes.start == 128 else jnp.concatenate([rows, rows], 1)


def product(l_ref, w_ref, lanes, d):
    left = l_ref[pl.ds(pl.multiple_of(lead_in(d), 64), BLOCK), :]
    return jnp.dot(left, w_ref[:, lanes], preferred_element_type=F32)


def right_far(at_ref, g_ref, out_a, out_b, w_ref, l_ref, r_ref):
    d = lax.rem(at_ref[0] + 2, 4)
    fill_window(g_ref, w_ref, l_ref, d)
    lead, trail, norms = split(column_norms(w_ref))
    tail = padded([lead, trail], 16).astype(BF16)
    cols = inverse(norms)
    rows = rows_of(r_ref, cols, d)
    for ref in (out_a, out_b):
        ref[HALF_ROWS:, :] = tail
    for lanes in PARTS:
        code = raised(product(l_ref, w_ref, lanes, d), wide(rows, lanes), cols[:, lanes]).astype(BF16)
        out_a[:HALF_ROWS, lanes] = code[:HALF_ROWS]
        out_b[:HALF_ROWS, lanes] = code[HALF_ROWS:]


def right_near(step, at_ref, g_ref, in_ref, out_ref, w_ref, l_ref, r_ref, p_ref):
    d = lax.rem(at_ref[0] + step, 4)
    start = 0 if step == 1 else HALF_ROWS
    fill_window(g_ref, w_ref, l_ref, d)
    tail = in_ref[HALF_ROWS:, :].astype(F32)
    theirs = tail[0:1] + tail[1:2]
    their_rows = rows_of(r_ref, theirs, d, start, HALF_ROWS)
    lead, trail, norms = split(jnp.sqrt(jnp.square(column_norms(w_ref)) + jnp.square(theirs)))
    out_ref[BLOCK:, :] = padded([lead, trail], 16).astype(BF16)
    cols = inverse(norms)
    rows = rows_of(r_ref, cols, d)
    here = slice(start, start + HALF_ROWS)
    for lanes in PARTS:
        part = p_ref.at[:, : lanes.stop - lanes.start]
        part[...] = product(l_ref, w_ref, lanes, d)
        part[here, :] += root(in_ref[:HALF_ROWS, lanes].astype(F32), wide(their_rows, lanes), theirs[:, lanes])
        out_ref[:BLOCK, lanes] = raised(part[...], wide(rows, lanes), cols[:, lanes]).astype(BF16)


def right_product(at_ref, g_ref, out_ref, norm_ref, w_ref, l_ref, r_ref):
    d = at_ref[0]
    fill_window(g_ref, w_ref, l_ref, d)
    norm_ref[...] = jnp.broadcast_to(column_norms(w_ref), (8, WINDOW))
    for lanes in PARTS:
        out_ref[:, lanes] = product(l_ref, w_ref, lanes, d)


def right_second(at_ref, p_ref, norm_ref, in_1, in_3, out_1, out_3, out_2, own_ref, r_ref, e_ref, t_ref):
    d, zh = at_ref[0], at_ref[1]
    squares, theirs = jnp.square(norm_ref[0:1, :]), []
    for ref in (in_1, in_3):
        tail = ref[BLOCK:, :].astype(F32)
        norms = tail[0:1] + tail[1:2]
        squares += jnp.square(norms)
        theirs.append((ref, norms, rows_of(r_ref, norms, d)))
    lead, trail, norms = split(jnp.sqrt(squares))
    cols = inverse(norms)
    rows = rows_of(r_ref, cols, d)
    begin = pl.multiple_of(lead_in(d), 64)
    e_ref[:64, :] = jnp.zeros((64, WINDOW), F32)
    e_ref[BLOCK:, :] = jnp.zeros((64, WINDOW), F32)
    for lanes in PARTS:
        part = p_ref[:, lanes]
        for ref, their_cols, their_rows in theirs:
            part += root(ref[:BLOCK, lanes].astype(F32), wide(their_rows, lanes), their_cols[:, lanes])
        e_ref[pl.ds(begin, BLOCK), lanes] = raised(part, wide(rows, lanes), cols[:, lanes])
    for i in range(5):
        for j in range(4):
            t_ref[i * 128 : (i + 1) * 128, j * 128 : (j + 1) * 128] = e_ref[
                j * 128 : (j + 1) * 128, 384 + i * 128 : 512 + i * 128
            ].T
    tails = [jnp.concatenate([v[:, t * 128 : (t + 1) * 128] for t in range(11)], 0) for v in (lead, trail, norms)]
    for step, ref in ((1, out_1), (3, out_3), (2, out_2), (0, own_ref)):
        chunk = lax.rem(zh + step, 4) * CHUNK
        piece = e_ref[pl.ds(pl.multiple_of(begin + chunk, 16), CHUNK), :]
        image = t_ref[pl.ds(pl.multiple_of(64 + begin + chunk, 16), CHUNK), tile_after(d)]
        ref[:, :WINDOW] = piece.astype(ref.dtype)
        ref[:, WINDOW:WIDTH] = image.astype(ref.dtype)
        ref[:, WIDTH:] = padded(tails[:2] if step else tails[2:], CHUNK).astype(ref.dtype)


def right_third(scale, at_ref, own_ref, in_1, in_3, in_2, out_ref, image_ref, r_ref, n_ref):
    d, zh = at_ref[0], at_ref[1]
    begin = pl.multiple_of(lead_in(d) + zh * CHUNK, 16)
    for i, ref in enumerate((own_ref, in_1, in_3, in_2)):
        tail = ref[:, WIDTH:].astype(F32)
        n_ref[...] = tail[:11] if i == 0 else tail[:11] + tail[11:22]
        for t in range(8):
            r_ref[t * 128 : (t + 1) * 128, :] = upright(n_ref[t : t + 1, :])
        rows = r_ref[pl.ds(begin, CHUNK), :]
        image_rows = r_ref[pl.ds(pl.multiple_of(448 + begin, 16), CHUNK), :]
        for t in range(14):
            lanes = slice(t * 128, (t + 1) * 128)
            code = ref[:, lanes].astype(F32)
            if t < 11:
                to, here, part = out_ref, lanes, root(code, rows, n_ref[t : t + 1, :])
            else:
                here = slice((t - 11) * 128, (t - 10) * 128)
                cols = n_ref[pl.ds(t - 11 + lax.rem(d, 2), 1), :]
                to, part = image_ref, root(code, image_rows, cols)
            if i == 0:
                to[:, here] = part * scale
            else:
                to[:, here] += part * scale


def right_last(at_ref, base_ref, image_ref, out_ref):
    d = at_ref[0]
    for t in range(14):
        ref, i = (base_ref, t) if t < 11 else (image_ref, t - 11)
        out_ref[:, tile(lax.rem(first_tile(d) + t, TILES))] = ref[:, i * 128 : (i + 1) * 128]


SUB, BASE, ROWS = 128, 1024, 1152


def sub(i):
    return pl.ds(pl.multiple_of(i * SUB, SUB), SUB)


def base_subs(core, b):
    return [4 * a + (core ^ (a > b).astype(jnp.int32)) + 2 * h for a in range(4) for h in (0, 1)]


def slot(i):
    return i // 4 * 4 + 2 * (i % 2) + i // 2 % 2


def more_sub(core, b, zl):
    return 4 * b + lax.rem(2 * zl + core + 1, 4)


def two_cols(ref, core, b):
    return jnp.concatenate([ref[pl.ds(4 * b + core + 2 * zl, 1), :] for zl in (0, 1)], 1)


def left_first(at_ref, far, near, far_2, near_2, out_1, out_3, out_2, own_ref, norm_ref, a_ref, b_ref, i_ref, s_ref):
    zh, y, core = at_ref[1], at_ref[2], at_ref[4]
    for p, ref in enumerate((far, near, far_2, near_2)):
        j = 2 * ((p // 2) ^ core) + lax.rem(p + zh, 2)
        for m in range(4):
            a_ref[sub(4 * j + slot(m)), :] = ref[m * SUB : (m + 1) * SUB, :]
    leads, trails, lanes = [], [], []
    for i in range(16):
        rows = slice(slot(i) * SUB, (slot(i) + 1) * SUB)
        squares = jnp.sum(jnp.square(a_ref[rows, :].astype(F32)), 1, keepdims=True)
        row = jnp.broadcast_to(jnp.sqrt(squares), (SUB, SUB)).T[0:1]
        lead, trail, norms = split(row)
        leads.append(lead), trails.append(trail), lanes.append(norms)
        i_ref[rows, :] = upright(inverse(norms))
    tail = jnp.concatenate([jnp.concatenate(leads, 0), jnp.concatenate(trails, 0)], 1).astype(BF16)
    norm_ref[...] = jnp.concatenate(lanes, 0)
    s_ref[...] = inverse(norm_ref[...])
    for step, out in ((1, out_1), (3, out_3), (2, out_2), (0, own_ref)):
        b = lax.rem(y + step, 4)
        for zl in (0, 1):
            b_ref[zl * SUB : (zl + 1) * SUB, :] = a_ref[sub(slot(4 * b + core + 2 * zl)), :]
        cols = two_cols(s_ref, core, b)
        for k, i in enumerate(base_subs(core, b)[::2]):
            pair = pl.ds(pl.multiple_of(slot(i) * SUB, 2 * SUB), 2 * SUB)
            part = dot(a_ref[pair, :], b_ref[...], 1)
            if step:
                scale = i_ref[pair, :]
                part = raised(part, jnp.concatenate([scale, scale], 1), cols).astype(BF16)
            out[k * 2 * SUB : (k + 1) * 2 * SUB, :] = part
        for zl in (0, 1):
            here = slice(zl * SUB, (zl + 1) * SUB)
            i = slot(more_sub(core, b, zl))
            part = dot(a_ref[sub(i), :], b_ref[here, :], 1)
            if step:
                part = raised(part, i_ref[sub(i), :], cols[:, here]).astype(BF16)
            out[BASE:ROWS, here] = part
        if step:
            out[ROWS:, :] = tail


def left_second(at_ref, own_ref, norm_ref, in_1, in_3, in_2, *refs):
    outs, (e_ref, s_ref, lead_ref, trail_ref, n_ref) = refs[:8], refs[8:]
    zh, y, zl, core = (at_ref[i] for i in (1, 2, 3, 4))
    squares = jnp.square(norm_ref[...])
    for k, ref in enumerate((in_1, in_3, in_2)):
        tail = ref[ROWS:, :].astype(F32)
        norms = tail[:, :SUB] + tail[:, SUB:]
        squares += jnp.square(norms)
        s_ref[k] = norms
    lead_ref[...], trail_ref[...], n_ref[...] = split(jnp.sqrt(squares))
    s_ref[3] = inverse(n_ref[...])
    sources = [(ref, k) for k, ref in enumerate((in_1, in_3, in_2))]
    cols = [two_cols(s_ref.at[k], core, y) for k in range(4)]
    r = lambda k, i: upright(s_ref.at[k][pl.ds(i, 1), :])
    for j, i in enumerate(base_subs(core, y)):
        rows = slice(j * SUB, (j + 1) * SUB)
        part = own_ref[rows, :]
        for ref, k in sources:
            scale = r(k, i)
            part += root(ref[rows, :].astype(F32), jnp.concatenate([scale, scale], 1), cols[k])
        scale = r(3, i)
        e_ref[rows, :] = raised(part, jnp.concatenate([scale, scale], 1), cols[3])
    for l in (0, 1):
        here = slice(l * SUB, (l + 1) * SUB)
        i = more_sub(core, y, l)
        part = own_ref[BASE:ROWS, here]
        for ref, k in sources:
            part += root(ref[BASE:ROWS, here].astype(F32), r(k, i), cols[k][:, here])
        e_ref[BASE:ROWS, here] = raised(part, r(3, i), cols[3][:, here])
    for step, out in zip((*Z_STEPS, 0), outs):
        z = lax.rem(2 * zh + zl + step, 8)
        to_h, to_l = z // 2, lax.rem(z, 2)
        lanes = tile(to_l)
        out[:256, :] = e_ref[pl.ds(pl.multiple_of(to_h * 256, 256), 256), lanes].astype(out.dtype)
        out[256:384, :] = e_ref[BASE:ROWS, lanes].astype(out.dtype)
        first = 4 * to_h + (core ^ (to_h > y).astype(jnp.int32))
        picks = [first, first + 2, more_sub(core, y, to_l), 4 * y + 2 * to_l + core]
        tail = [ref[pl.ds(i, 1), :] for ref in ((lead_ref, trail_ref) if step else (n_ref,)) for i in picks]
        out[384:, :] = padded(tail, 16).astype(out.dtype)


def left_third(scale, at_ref, *refs):
    sources, (base_ref, more_ref, same_ref, other_ref, sum_ref) = refs[:8], refs[8:]
    zh, y, zl = at_ref[1], at_ref[2], at_ref[3]
    for k, ref in enumerate(sources):
        tail = ref[384:, :].astype(F32)
        norms = tail[0:4] if k == 0 else tail[0:4] + tail[4:8]
        for j in range(3):
            rows = slice(j * SUB, (j + 1) * SUB)
            part = root(ref[rows, :].astype(F32), upright(norms[j : j + 1]), norms[3:4]) * scale
            if k == 0:
                sum_ref[rows, :] = part
            else:
                sum_ref[rows, :] += part
    first, second, more = (sum_ref[j * SUB : (j + 1) * SUB, :] for j in range(3))
    base_ref[...] = sum_ref[:256, :]
    more_ref[...] = more
    same_ref[...] = jnp.where(zh == y, more, jnp.where(zl == 0, first, second)).T
    other_ref[...] = jnp.where(zl == 0, second, first).T


def left_last(at_ref, base_ref, more_ref, same_ref, other_ref, out_ref):
    zh, y, zl, core = (at_ref[i] for i in (1, 2, 3, 4))
    n, parity, diagonal = 2 * zl + core, core ^ (zh > y).astype(jnp.int32), zh == y
    out_ref[sub(parity), :] = base_ref[:SUB, :]
    out_ref[sub(parity + 2), :] = base_ref[SUB:, :]
    out_ref[sub(jnp.where(diagonal, lax.rem(n + 3, 4), 2 * zl + 1 - parity)), :] = same_ref[...]
    out_ref[sub(jnp.where(diagonal, lax.rem(n + 1, 4), 2 * (1 - zl) + 1 - parity)), :] = jnp.where(
        diagonal, more_ref[...], other_ref[...]
    )


def mirror(step):
    def to(x, zh, y, zl, core):
        if zh != y:
            return (x, y, zh, zl ^ step, core ^ (zh > y))
        n = (2 * zl + core + 1 - step) % 4
        return (x, zh, y, n // 2, n % 2)

    return to


def along_z(step):
    def to(x, zh, y, zl, core):
        z = (2 * zh + zl + step) % 8
        return (x, z // 2, y, z % 2, core)

    return to


def shards(gradient):
    rows, width = gradient.shape
    row, col = lax.axis_index("row"), lax.axis_index("col")
    x, zh, y, zl, core = row // 4, row % 4, col // 4, col // 2 % 2, col % 2
    at = jnp.stack([x, zh, y, zl, core, x, x, x]).astype(jnp.int32)
    barrier = lax.optimization_barrier
    half = width // 2

    cut = lambda parity: lax.dynamic_slice_in_dim(gradient, parity * half, half, 1)
    near, far, gradient = barrier((cut((zh + 1) % 2), cut(zh % 2), gradient))
    near = send(near, lambda x, zh, y, zl, core: (x, 2 * core + (zh + 1) % 2, y, zl, zh // 2))

    window = [((rows, WINDOW), BF16), ((512, 512), BF16), ((512, 128), F32)]
    half_part, whole_part = ((HALF_ROWS + 16, WINDOW), BF16), ((BLOCK + 16, WINDOW), BF16)
    over_x = lambda s, v: send(v, lambda x, zh, y, zl, core: (x + s, zh, y, zl, core))
    far_1, far_3 = run(right_far, [half_part] * 2, window, at, gradient)
    far_1, far_3 = over_x(1, far_1), over_x(3, far_3)
    add = lambda s, v: run(
        functools.partial(right_near, s), [whole_part], window + [((BLOCK, 256), F32)], at, gradient, v
    )[0]
    code_1, code_3 = add(1, far_1), add(3, far_3)
    right_1, right_3 = over_x(1, code_1), over_x(3, code_3)
    near, far, _ = barrier((near, far, code_3))
    far = send(far, lambda x, zh, y, zl, core: (x, 2 * core + zh % 2, y, zl, zh // 2))

    gradient, _ = barrier((gradient, (code_1, code_3)))
    product_own, norms_own = run(
        right_product, [((BLOCK, WINDOW), F32), ((8, WINDOW), F32)], window, at, gradient
    )

    near, far, product_own = barrier((near, far, product_own))
    swap = lambda x, zh, y, zl, core: (x, zh, y, zl, 1 - core)
    far_2, near_2 = send(far, swap), send(near, swap)

    piece = (CHUNK, WIDTH + 128)
    code_1, code_3, code_2, right_own = run(
        right_second,
        [(piece, BF16)] * 3 + [(piece, F32)],
        [((512, 128), F32), ((512, WINDOW), F32), ((640, 512), F32)],
        at,
        product_own,
        norms_own,
        right_1,
        right_3,
    )
    over_z = lambda s, v: send(v, lambda x, zh, y, zl, core: (x, zh + s, y, zl, core))
    right_1, right_3 = over_z(1, code_1), over_z(3, code_3)

    far, near, far_2, near_2, _ = barrier((far, near, far_2, near_2, code_1))
    packed = (ROWS + 16, 256)
    left_1, left_3, left_2, left_own, norms = run(
        left_first,
        [(packed, BF16)] * 3 + [((ROWS, 256), F32), ((16, SUB), F32)],
        [((2048, half), BF16), ((256, half), BF16), ((2048, SUB), F32), ((16, SUB), F32)],
        at,
        far,
        near,
        far_2,
        near_2,
    )
    over_y = lambda s, v: send(v, lambda x, zh, y, zl, core: (x, zh, y + s, zl, core))
    left_1, left_3 = over_y(1, left_1), over_y(3, left_3)
    left_2, right_1, right_3 = barrier((left_2, right_1, right_3))
    left_1, left_3, code_2, right_1, right_3 = barrier((left_1, left_3, code_2, right_1, right_3))
    left_2, right_2 = over_y(2, left_2), over_z(2, code_2)

    piece = (400, SUB)
    codes = run(
        left_second,
        [(piece, BF16)] * 7 + [(piece, F32)],
        [((ROWS, 256), F32), ((4, 16, SUB), F32)] + [((16, SUB), F32)] * 3,
        at,
        left_own,
        norms,
        left_1,
        left_3,
        left_2,
    )
    arrived = [send(code, along_z(s)) for s, code in zip(Z_STEPS, codes)]
    right_1, right_3, _ = barrier((right_1, right_3, codes))

    right_base, image = run(
        functools.partial(right_third, 1.0 / (rows * 16)),
        [((CHUNK, WINDOW), F32), ((CHUNK, IMAGE), F32)],
        [((1024, 128), F32), ((11, 128), F32)],
        at,
        right_own,
        right_1,
        right_3,
        right_2,
    )
    arrived, image = barrier((arrived, image))
    image = over_x(1, image)
    right_gram = run(right_last, [((CHUNK, width), F32)], [], at, right_base, image)[0]

    square = ((SUB, SUB), F32)
    base, more, same, other = run(
        functools.partial(left_third, 1.0 / (width * 16)),
        [((256, SUB), F32), square, square, square],
        [((384, SUB), F32)],
        at,
        codes[7],
        *arrived,
    )
    same, other = send(same, mirror(0)), send(other, mirror(1))
    left_gram = run(left_last, [((512, SUB), F32)], [], at, base, more, same, other)[0]
    return (left_gram, right_gram)


def solution(mesh):
    in_specs = (P("row", "col"),)
    out_specs = (P("row", "col"), P(("col", "row"), None))
    return jax.shard_map(shards, mesh=mesh, in_specs=in_specs, out_specs=out_specs, check_vma=False)
```

```python
import functools
import itertools

import jax
import jax.numpy as jnp
from jax import lax
from jax.experimental import pallas as pl
from jax.experimental.pallas import tpu as pltpu
from jax.sharding import PartitionSpec as P

F32, BF16 = jnp.float32, jnp.bfloat16

SIZES = (4, 4, 4, 2, 2)
PLACES = list(itertools.product(*(range(n) for n in SIZES)))
STEPS = (1, 3, 2)
Z_STEPS = (4, 3, 5, 2, 6, 1, 7)


def number(place):
    x, zh, y, zl, core = (p % n for p, n in zip(place, SIZES))
    return (4 * x + zh) * 16 + 4 * y + 2 * zl + core


def send(array, to):
    return lax.ppermute(array, ("row", "col"), [(number(p), number(to(*p))) for p in PLACES])


POWER = 13
LIFT = 120 / POWER
LOG_LIFT = LIFT * 0.6931471805599453


def split(norms):
    lead = norms.astype(BF16).astype(F32)
    trail = (norms - lead).astype(BF16).astype(F32)
    return lead, trail, lead + trail


def inverse(norms):
    return jnp.where(norms > 0, 1.0 / jnp.where(norms > 0, norms, 1.0), 0.0)


def raised(value, rows, cols):
    ratio = value * rows * (cols * 2.0**LIFT)
    p2 = ratio * ratio
    p4 = p2 * p2
    return p4 * p4 * (p4 * ratio)


def root(code, rows, cols):
    size = jnp.exp(jnp.log(jnp.abs(code)) * (1.0 / POWER) - LOG_LIFT)
    return jnp.where(code < 0, -size, size) * (rows * cols)


def upright(row):
    parts = [row[:, i : i + 128] for i in range(0, row.shape[1], 128)]
    return jnp.concatenate([jnp.broadcast_to(p, (128, 128)).T for p in parts], 0)


def dot(left, right, dim):
    return lax.dot_general(
        left, right, (((dim,), (dim,)), ((), ())), preferred_element_type=F32
    )


def run(body, outs, scratch, *args):
    smem, vmem = pl.BlockSpec(memory_space=pltpu.SMEM), pl.BlockSpec(memory_space=pltpu.VMEM)
    return pl.pallas_call(
        body,
        out_shape=[jax.ShapeDtypeStruct(shape, dtype) for shape, dtype in outs],
        in_specs=[smem] + [vmem] * (len(args) - 1),
        out_specs=[vmem] * len(outs),
        scratch_shapes=[pltpu.VMEM(shape, dtype) for shape, dtype in scratch],
        cost_estimate=pl.CostEstimate(flops=1000, bytes_accessed=1000, transcendentals=0),
        compiler_params=pltpu.CompilerParams(vmem_limit_bytes=48 * 1024 * 1024),
    )(*args)


BLOCK, CHUNK, TILES, WINDOW, IMAGE = 448, 112, 14, 1408, 384
WIDTH = WINDOW + IMAGE


def first_tile(d):
    return 7 * (d // 2) + 3 * (d % 2)


def lead_in(d):
    return 64 * (d % 2)


def tile(i):
    return pl.ds(pl.multiple_of(i * 128, 128), 128)


HALF_ROWS = BLOCK // 2
PARTS = [slice(i, min(i + 256, WINDOW)) for i in range(0, WINDOW, 256)]


def fill_window(g_ref, w_ref, l_ref, d):
    for t in range(11):
        w_ref[:, t * 128 : (t + 1) * 128] = g_ref[:, tile(lax.rem(first_tile(d) + t, TILES))]
    l_ref[...] = w_ref[:, :512].T


def tile_after(d):
    return pl.ds(pl.multiple_of(128 * (d % 2), 128), IMAGE)


def column_norms(w_ref):
    return jnp.sqrt(jnp.sum(jnp.square(w_ref[...].astype(F32)), 0, keepdims=True))


def padded(rows, count):
    rows = jnp.concatenate(rows, 0)
    return jnp.concatenate([rows, jnp.zeros((count - rows.shape[0], rows.shape[1]), F32)], 0)


def rows_of(r_ref, norms, d, start=0, count=BLOCK):
    r_ref[...] = upright(norms[:, :512])
    return r_ref[pl.ds(pl.multiple_of(lead_in(d) + start, 16), count), :]


def wide(rows, lanes):
    return rows if lanes.stop - lanes.start == 128 else jnp.concatenate([rows, rows], 1)


def product(l_ref, w_ref, lanes, d):
    left = l_ref[pl.ds(pl.multiple_of(lead_in(d), 64), BLOCK), :]
    return jnp.dot(left, w_ref[:, lanes], preferred_element_type=F32)


def right_far(at_ref, g_ref, out_a, out_b, w_ref, l_ref, r_ref):
    d = lax.rem(at_ref[0] + 2, 4)
    fill_window(g_ref, w_ref, l_ref, d)
    lead, trail, norms = split(column_norms(w_ref))
    tail = padded([lead, trail], 16).astype(BF16)
    cols = inverse(norms)
    rows = rows_of(r_ref, cols, d)
    for ref in (out_a, out_b):
        ref[HALF_ROWS:, :] = tail
    for lanes in PARTS:
        code = raised(product(l_ref, w_ref, lanes, d), wide(rows, lanes), cols[:, lanes]).astype(BF16)
        out_a[:HALF_ROWS, lanes] = code[:HALF_ROWS]
        out_b[:HALF_ROWS, lanes] = code[HALF_ROWS:]


def right_near(step, at_ref, g_ref, in_ref, out_ref, w_ref, l_ref, r_ref, p_ref):
    d = lax.rem(at_ref[0] + step, 4)
    start = 0 if step == 1 else HALF_ROWS
    fill_window(g_ref, w_ref, l_ref, d)
    tail = in_ref[HALF_ROWS:, :].astype(F32)
    theirs = tail[0:1] + tail[1:2]
    their_rows = rows_of(r_ref, theirs, d, start, HALF_ROWS)
    lead, trail, norms = split(jnp.sqrt(jnp.square(column_norms(w_ref)) + jnp.square(theirs)))
    out_ref[BLOCK:, :] = padded([lead, trail], 16).astype(BF16)
    cols = inverse(norms)
    rows = rows_of(r_ref, cols, d)
    here = slice(start, start + HALF_ROWS)
    for lanes in PARTS:
        part = p_ref.at[:, : lanes.stop - lanes.start]
        part[...] = product(l_ref, w_ref, lanes, d)
        part[here, :] += root(in_ref[:HALF_ROWS, lanes].astype(F32), wide(their_rows, lanes), theirs[:, lanes])
        out_ref[:BLOCK, lanes] = raised(part[...], wide(rows, lanes), cols[:, lanes]).astype(BF16)


def right_product(at_ref, g_ref, out_ref, norm_ref, w_ref, l_ref, r_ref):
    d = at_ref[0]
    fill_window(g_ref, w_ref, l_ref, d)
    norm_ref[...] = jnp.broadcast_to(column_norms(w_ref), (8, WINDOW))
    for lanes in PARTS:
        out_ref[:, lanes] = product(l_ref, w_ref, lanes, d)


def right_second(at_ref, p_ref, norm_ref, in_1, in_3, out_1, out_3, out_2, own_ref, r_ref, e_ref, t_ref):
    d, zh = at_ref[0], at_ref[1]
    squares, theirs = jnp.square(norm_ref[0:1, :]), []
    for ref in (in_1, in_3):
        tail = ref[BLOCK:, :].astype(F32)
        norms = tail[0:1] + tail[1:2]
        squares += jnp.square(norms)
        theirs.append((ref, norms, rows_of(r_ref, norms, d)))
    lead, trail, norms = split(jnp.sqrt(squares))
    cols = inverse(norms)
    rows = rows_of(r_ref, cols, d)
    begin = pl.multiple_of(lead_in(d), 64)
    e_ref[:64, :] = jnp.zeros((64, WINDOW), F32)
    e_ref[BLOCK:, :] = jnp.zeros((64, WINDOW), F32)
    for lanes in PARTS:
        part = p_ref[:, lanes]
        for ref, their_cols, their_rows in theirs:
            part += root(ref[:BLOCK, lanes].astype(F32), wide(their_rows, lanes), their_cols[:, lanes])
        e_ref[pl.ds(begin, BLOCK), lanes] = raised(part, wide(rows, lanes), cols[:, lanes])
    for i in range(5):
        for j in range(4):
            t_ref[i * 128 : (i + 1) * 128, j * 128 : (j + 1) * 128] = e_ref[
                j * 128 : (j + 1) * 128, 384 + i * 128 : 512 + i * 128
            ].T
    tails = [jnp.concatenate([v[:, t * 128 : (t + 1) * 128] for t in range(11)], 0) for v in (lead, trail, norms)]
    for step, ref in ((1, out_1), (3, out_3), (2, out_2), (0, own_ref)):
        chunk = lax.rem(zh + step, 4) * CHUNK
        piece = e_ref[pl.ds(pl.multiple_of(begin + chunk, 16), CHUNK), :]
        image = t_ref[pl.ds(pl.multiple_of(64 + begin + chunk, 16), CHUNK), tile_after(d)]
        ref[:, :WINDOW] = piece.astype(ref.dtype)
        ref[:, WINDOW:WIDTH] = image.astype(ref.dtype)
        ref[:, WIDTH:] = padded(tails[:2] if step else tails[2:], CHUNK).astype(ref.dtype)


def right_third(scale, at_ref, own_ref, in_1, in_3, in_2, out_ref, image_ref, r_ref, n_ref):
    d, zh = at_ref[0], at_ref[1]
    begin = pl.multiple_of(lead_in(d) + zh * CHUNK, 16)
    for i, ref in enumerate((own_ref, in_1, in_3, in_2)):
        tail = ref[:, WIDTH:].astype(F32)
        n_ref[...] = tail[:11] if i == 0 else tail[:11] + tail[11:22]
        for t in range(8):
            r_ref[t * 128 : (t + 1) * 128, :] = upright(n_ref[t : t + 1, :])
        rows = r_ref[pl.ds(begin, CHUNK), :]
        image_rows = r_ref[pl.ds(pl.multiple_of(448 + begin, 16), CHUNK), :]
        for t in range(14):
            lanes = slice(t * 128, (t + 1) * 128)
            code = ref[:, lanes].astype(F32)
            if t < 11:
                to, here, part = out_ref, lanes, root(code, rows, n_ref[t : t + 1, :])
            else:
                here = slice((t - 11) * 128, (t - 10) * 128)
                cols = n_ref[pl.ds(t - 11 + lax.rem(d, 2), 1), :]
                to, part = image_ref, root(code, image_rows, cols)
            if i == 0:
                to[:, here] = part * scale
            else:
                to[:, here] += part * scale


def right_last(at_ref, base_ref, image_ref, out_ref):
    d = at_ref[0]
    for t in range(14):
        ref, i = (base_ref, t) if t < 11 else (image_ref, t - 11)
        out_ref[:, tile(lax.rem(first_tile(d) + t, TILES))] = ref[:, i * 128 : (i + 1) * 128]


SUB, BASE, ROWS = 128, 1024, 1152


def sub(i):
    return pl.ds(pl.multiple_of(i * SUB, SUB), SUB)


def base_subs(core, b):
    return [4 * a + (core ^ (a > b).astype(jnp.int32)) + 2 * h for a in range(4) for h in (0, 1)]


def slot(i):
    return i // 4 * 4 + 2 * (i % 2) + i // 2 % 2


def more_sub(core, b, zl):
    return 4 * b + lax.rem(2 * zl + core + 1, 4)


def two_cols(ref, core, b):
    return jnp.concatenate([ref[pl.ds(4 * b + core + 2 * zl, 1), :] for zl in (0, 1)], 1)


def left_first(at_ref, far, near, far_2, near_2, out_1, out_3, out_2, own_ref, norm_ref, a_ref, b_ref, i_ref, s_ref):
    zh, y, core = at_ref[1], at_ref[2], at_ref[4]
    for p, ref in enumerate((far, near, far_2, near_2)):
        j = 2 * ((p // 2) ^ core) + lax.rem(p + zh, 2)
        for m in range(4):
            a_ref[sub(4 * j + slot(m)), :] = ref[m * SUB : (m + 1) * SUB, :]
    leads, trails, lanes = [], [], []
    for i in range(16):
        rows = slice(slot(i) * SUB, (slot(i) + 1) * SUB)
        squares = jnp.sum(jnp.square(a_ref[rows, :].astype(F32)), 1, keepdims=True)
        row = jnp.broadcast_to(jnp.sqrt(squares), (SUB, SUB)).T[0:1]
        lead, trail, norms = split(row)
        leads.append(lead), trails.append(trail), lanes.append(norms)
        i_ref[rows, :] = upright(inverse(norms))
    tail = jnp.concatenate([jnp.concatenate(leads, 0), jnp.concatenate(trails, 0)], 1).astype(BF16)
    norm_ref[...] = jnp.concatenate(lanes, 0)
    s_ref[...] = inverse(norm_ref[...])
    for step, out in ((1, out_1), (3, out_3), (2, out_2), (0, own_ref)):
        b = lax.rem(y + step, 4)
        for zl in (0, 1):
            b_ref[zl * SUB : (zl + 1) * SUB, :] = a_ref[sub(slot(4 * b + core + 2 * zl)), :]
        cols = two_cols(s_ref, core, b)
        for k, i in enumerate(base_subs(core, b)[::2]):
            pair = pl.ds(pl.multiple_of(slot(i) * SUB, 2 * SUB), 2 * SUB)
            part = dot(a_ref[pair, :], b_ref[...], 1)
            if step:
                scale = i_ref[pair, :]
                part = raised(part, jnp.concatenate([scale, scale], 1), cols).astype(BF16)
            out[k * 2 * SUB : (k + 1) * 2 * SUB, :] = part
        for zl in (0, 1):
            here = slice(zl * SUB, (zl + 1) * SUB)
            i = slot(more_sub(core, b, zl))
            part = dot(a_ref[sub(i), :], b_ref[here, :], 1)
            if step:
                part = raised(part, i_ref[sub(i), :], cols[:, here]).astype(BF16)
            out[BASE:ROWS, here] = part
        if step:
            out[ROWS:, :] = tail


def left_second(at_ref, own_ref, norm_ref, in_1, in_3, in_2, *refs):
    outs, (e_ref, s_ref, lead_ref, trail_ref, n_ref) = refs[:8], refs[8:]
    zh, y, zl, core = (at_ref[i] for i in (1, 2, 3, 4))
    squares = jnp.square(norm_ref[...])
    for k, ref in enumerate((in_1, in_3, in_2)):
        tail = ref[ROWS:, :].astype(F32)
        norms = tail[:, :SUB] + tail[:, SUB:]
        squares += jnp.square(norms)
        s_ref[k] = norms
    lead_ref[...], trail_ref[...], n_ref[...] = split(jnp.sqrt(squares))
    s_ref[3] = inverse(n_ref[...])
    sources = [(ref, k) for k, ref in enumerate((in_1, in_3, in_2))]
    cols = [two_cols(s_ref.at[k], core, y) for k in range(4)]
    r = lambda k, i: upright(s_ref.at[k][pl.ds(i, 1), :])
    for j, i in enumerate(base_subs(core, y)):
        rows = slice(j * SUB, (j + 1) * SUB)
        part = own_ref[rows, :]
        for ref, k in sources:
            scale = r(k, i)
            part += root(ref[rows, :].astype(F32), jnp.concatenate([scale, scale], 1), cols[k])
        scale = r(3, i)
        e_ref[rows, :] = raised(part, jnp.concatenate([scale, scale], 1), cols[3])
    for l in (0, 1):
        here = slice(l * SUB, (l + 1) * SUB)
        i = more_sub(core, y, l)
        part = own_ref[BASE:ROWS, here]
        for ref, k in sources:
            part += root(ref[BASE:ROWS, here].astype(F32), r(k, i), cols[k][:, here])
        e_ref[BASE:ROWS, here] = raised(part, r(3, i), cols[3][:, here])
    for step, out in zip((*Z_STEPS, 0), outs):
        z = lax.rem(2 * zh + zl + step, 8)
        to_h, to_l = z // 2, lax.rem(z, 2)
        lanes = tile(to_l)
        out[:256, :] = e_ref[pl.ds(pl.multiple_of(to_h * 256, 256), 256), lanes].astype(out.dtype)
        out[256:384, :] = e_ref[BASE:ROWS, lanes].astype(out.dtype)
        first = 4 * to_h + (core ^ (to_h > y).astype(jnp.int32))
        picks = [first, first + 2, more_sub(core, y, to_l), 4 * y + 2 * to_l + core]
        tail = [ref[pl.ds(i, 1), :] for ref in ((lead_ref, trail_ref) if step else (n_ref,)) for i in picks]
        out[384:, :] = padded(tail, 16).astype(out.dtype)


def left_third(scale, at_ref, *refs):
    sources, (base_ref, more_ref, same_ref, other_ref, sum_ref) = refs[:8], refs[8:]
    zh, y, zl = at_ref[1], at_ref[2], at_ref[3]
    for k, ref in enumerate(sources):
        tail = ref[384:, :].astype(F32)
        norms = tail[0:4] if k == 0 else tail[0:4] + tail[4:8]
        for j in range(3):
            rows = slice(j * SUB, (j + 1) * SUB)
            part = root(ref[rows, :].astype(F32), upright(norms[j : j + 1]), norms[3:4]) * scale
            if k == 0:
                sum_ref[rows, :] = part
            else:
                sum_ref[rows, :] += part
    first, second, more = (sum_ref[j * SUB : (j + 1) * SUB, :] for j in range(3))
    base_ref[...] = sum_ref[:256, :]
    more_ref[...] = more
    same_ref[...] = jnp.where(zh == y, more, jnp.where(zl == 0, first, second)).T
    other_ref[...] = jnp.where(zl == 0, second, first).T


def left_last(at_ref, base_ref, more_ref, same_ref, other_ref, out_ref):
    zh, y, zl, core = (at_ref[i] for i in (1, 2, 3, 4))
    n, parity, diagonal = 2 * zl + core, core ^ (zh > y).astype(jnp.int32), zh == y
    out_ref[sub(parity), :] = base_ref[:SUB, :]
    out_ref[sub(parity + 2), :] = base_ref[SUB:, :]
    out_ref[sub(jnp.where(diagonal, lax.rem(n + 3, 4), 2 * zl + 1 - parity)), :] = same_ref[...]
    out_ref[sub(jnp.where(diagonal, lax.rem(n + 1, 4), 2 * (1 - zl) + 1 - parity)), :] = jnp.where(
        diagonal, more_ref[...], other_ref[...]
    )


def last(at_ref, *refs):
    left_last(at_ref, *refs[:4], refs[6])
    right_last(at_ref, *refs[4:6], refs[7])


def mirror(step):
    def to(x, zh, y, zl, core):
        if zh != y:
            return (x, y, zh, zl ^ step, core ^ (zh > y))
        n = (2 * zl + core + 1 - step) % 4
        return (x, zh, y, n // 2, n % 2)

    return to


def along_z(step):
    def to(x, zh, y, zl, core):
        z = (2 * zh + zl + step) % 8
        return (x, z // 2, y, z % 2, core)

    return to


def shards(gradient):
    rows, width = gradient.shape
    row, col = lax.axis_index("row"), lax.axis_index("col")
    x, zh, y, zl, core = row // 4, row % 4, col // 4, col // 2 % 2, col % 2
    at = jnp.stack([x, zh, y, zl, core, x, x, x]).astype(jnp.int32)
    barrier = lax.optimization_barrier
    half = width // 2

    cut = lambda parity: lax.dynamic_slice_in_dim(gradient, parity * half, half, 1)
    near, gradient = barrier((cut((zh + 1) % 2), gradient))
    near = send(near, lambda x, zh, y, zl, core: (x, 2 * core + (zh + 1) % 2, y, zl, zh // 2))

    window = [((rows, WINDOW), BF16), ((512, 512), BF16), ((512, 128), F32)]
    half_part, whole_part = ((HALF_ROWS + 16, WINDOW), BF16), ((BLOCK + 16, WINDOW), BF16)
    over_x = lambda s, v: send(v, lambda x, zh, y, zl, core: (x + s, zh, y, zl, core))
    far_1, far_3 = run(right_far, [half_part] * 2, window, at, gradient)
    far_1, far_3 = over_x(1, far_1), over_x(3, far_3)
    add = lambda s, v: run(
        functools.partial(right_near, s), [whole_part], window + [((BLOCK, 256), F32)], at, gradient, v
    )[0]
    code_1, code_3 = add(1, far_1), add(3, far_3)
    right_1, right_3 = over_x(1, code_1), over_x(3, code_3)
    near, far, _ = barrier((near, cut(zh % 2), code_3))
    far = send(far, lambda x, zh, y, zl, core: (x, 2 * core + zh % 2, y, zl, zh // 2))

    gradient, _ = barrier((gradient, (code_1, code_3)))
    product_own, norms_own = run(
        right_product, [((BLOCK, WINDOW), F32), ((8, WINDOW), F32)], window, at, gradient
    )

    near, far, product_own = barrier((near, far, product_own))
    swap = lambda x, zh, y, zl, core: (x, zh, y, zl, 1 - core)
    far_2, near_2 = send(far, swap), send(near, swap)

    piece = (CHUNK, WIDTH + 128)
    code_1, code_3, code_2, right_own = run(
        right_second,
        [(piece, BF16)] * 3 + [(piece, F32)],
        [((512, 128), F32), ((512, WINDOW), F32), ((640, 512), F32)],
        at,
        product_own,
        norms_own,
        right_1,
        right_3,
    )
    over_z = lambda s, v: send(v, lambda x, zh, y, zl, core: (x, zh + s, y, zl, core))
    right_1, right_3 = over_z(1, code_1), over_z(3, code_3)

    far, near, far_2, near_2, _ = barrier((far, near, far_2, near_2, code_1))
    packed = (ROWS + 16, 256)
    left_1, left_3, left_2, left_own, norms = run(
        left_first,
        [(packed, BF16)] * 3 + [((ROWS, 256), F32), ((16, SUB), F32)],
        [((2048, half), BF16), ((256, half), BF16), ((2048, SUB), F32), ((16, SUB), F32)],
        at,
        far,
        near,
        far_2,
        near_2,
    )
    over_y = lambda s, v: send(v, lambda x, zh, y, zl, core: (x, zh, y + s, zl, core))
    left_1, left_3 = over_y(1, left_1), over_y(3, left_3)
    left_2, right_1, right_3 = barrier((left_2, right_1, right_3))
    left_1, left_3, code_2, right_1, right_3 = barrier((left_1, left_3, code_2, right_1, right_3))
    left_2, right_2 = over_y(2, left_2), over_z(2, code_2)

    piece = (400, SUB)
    codes = run(
        left_second,
        [(piece, BF16)] * 7 + [(piece, F32)],
        [((ROWS, 256), F32), ((4, 16, SUB), F32)] + [((16, SUB), F32)] * 3,
        at,
        left_own,
        norms,
        left_1,
        left_3,
        left_2,
    )
    arrived = [send(code, along_z(s)) for s, code in zip(Z_STEPS, codes)]
    right_1, right_3, _ = barrier((right_1, right_3, codes))

    right_base, image = run(
        functools.partial(right_third, 1.0 / (rows * 16)),
        [((CHUNK, WINDOW), F32), ((CHUNK, IMAGE), F32)],
        [((1024, 128), F32), ((11, 128), F32)],
        at,
        right_own,
        right_1,
        right_3,
        right_2,
    )
    arrived, image = barrier((arrived, image))
    image = over_x(1, image)

    square = ((SUB, SUB), F32)
    base, more, same, other = run(
        functools.partial(left_third, 1.0 / (width * 16)),
        [((256, SUB), F32), square, square, square],
        [((384, SUB), F32)],
        at,
        codes[7],
        *arrived,
    )
    same, other = send(same, mirror(0)), send(other, mirror(1))
    left_gram, right_gram = run(
        last, [((512, SUB), F32), ((CHUNK, width), F32)], [], at, base, more, same, other, right_base, image
    )
    return (left_gram, right_gram)


def solution(mesh):
    in_specs = (P("row", "col"),)
    out_specs = (P("row", "col"), P(("col", "row"), None))
    return jax.shard_map(shards, mesh=mesh, in_specs=in_specs, out_specs=out_specs, check_vma=False)
```

```python
import functools
import itertools

import jax
import jax.numpy as jnp
from jax import lax
from jax.experimental import pallas as pl
from jax.experimental.pallas import tpu as pltpu
from jax.sharding import PartitionSpec as P

F32, BF16 = jnp.float32, jnp.bfloat16

SIZES = (4, 4, 4, 2, 2)
PLACES = list(itertools.product(*(range(n) for n in SIZES)))
STEPS = (1, 3, 2)
Z_STEPS = (4, 3, 5, 2, 6, 1, 7)


def number(place):
    x, zh, y, zl, core = (p % n for p, n in zip(place, SIZES))
    return (4 * x + zh) * 16 + 4 * y + 2 * zl + core


def send(array, to):
    return lax.ppermute(array, ("row", "col"), [(number(p), number(to(*p))) for p in PLACES])


POWER = 13
LIFT = 120 / POWER
LOG_LIFT = LIFT * 0.6931471805599453


def split(norms):
    lead = norms.astype(BF16).astype(F32)
    trail = (norms - lead).astype(BF16).astype(F32)
    return lead, trail, lead + trail


def inverse(norms):
    return jnp.where(norms > 0, 1.0 / jnp.where(norms > 0, norms, 1.0), 0.0)


def raised(value, rows, cols):
    ratio = value * rows * (cols * 2.0**LIFT)
    p2 = ratio * ratio
    p4 = p2 * p2
    return p4 * p4 * (p4 * ratio)


def root(code, rows, cols):
    size = jnp.exp(jnp.log(jnp.abs(code)) * (1.0 / POWER) - LOG_LIFT)
    return jnp.where(code < 0, -size, size) * (rows * cols)


def upright(row):
    parts = [row[:, i : i + 128] for i in range(0, row.shape[1], 128)]
    return jnp.concatenate([jnp.broadcast_to(p, (128, 128)).T for p in parts], 0)


def dot(left, right, dim):
    return lax.dot_general(
        left, right, (((dim,), (dim,)), ((), ())), preferred_element_type=F32
    )


def run(body, outs, scratch, *args):
    smem, vmem = pl.BlockSpec(memory_space=pltpu.SMEM), pl.BlockSpec(memory_space=pltpu.VMEM)
    return pl.pallas_call(
        body,
        out_shape=[jax.ShapeDtypeStruct(shape, dtype) for shape, dtype in outs],
        in_specs=[smem] + [vmem] * (len(args) - 1),
        out_specs=[vmem] * len(outs),
        scratch_shapes=[pltpu.VMEM(shape, dtype) for shape, dtype in scratch],
        cost_estimate=pl.CostEstimate(flops=1000, bytes_accessed=1000, transcendentals=0),
        compiler_params=pltpu.CompilerParams(vmem_limit_bytes=48 * 1024 * 1024),
    )(*args)


BLOCK, CHUNK, TILES, WINDOW, IMAGE = 448, 112, 14, 1408, 384
WIDTH = WINDOW + IMAGE


def first_tile(d):
    return 7 * (d // 2) + 3 * (d % 2)


def lead_in(d):
    return 64 * (d % 2)


def tile(i):
    return pl.ds(pl.multiple_of(i * 128, 128), 128)


HALF_ROWS = BLOCK // 2
PARTS = [slice(i, min(i + 256, WINDOW)) for i in range(0, WINDOW, 256)]


def fill_window(g_ref, w_ref, l_ref, d):
    for t in range(11):
        w_ref[:, t * 128 : (t + 1) * 128] = g_ref[:, tile(lax.rem(first_tile(d) + t, TILES))]
    l_ref[...] = w_ref[:, :512].T


def tile_after(d):
    return pl.ds(pl.multiple_of(128 * (d % 2), 128), IMAGE)


def column_norms(w_ref):
    return jnp.sqrt(jnp.sum(jnp.square(w_ref[...].astype(F32)), 0, keepdims=True))


def padded(rows, count):
    rows = jnp.concatenate(rows, 0)
    return jnp.concatenate([rows, jnp.zeros((count - rows.shape[0], rows.shape[1]), F32)], 0)


def rows_of(r_ref, norms, d, start=0, count=BLOCK):
    r_ref[...] = upright(norms[:, :512])
    return r_ref[pl.ds(pl.multiple_of(lead_in(d) + start, 16), count), :]


def wide(rows, lanes):
    return rows if lanes.stop - lanes.start == 128 else jnp.concatenate([rows, rows], 1)


def product(l_ref, w_ref, lanes, d):
    left = l_ref[pl.ds(pl.multiple_of(lead_in(d), 64), BLOCK), :]
    return jnp.dot(left, w_ref[:, lanes], preferred_element_type=F32)


def right_far(at_ref, g_ref, out_a, out_b, w_ref, l_ref, r_ref):
    d = lax.rem(at_ref[0] + 2, 4)
    fill_window(g_ref, w_ref, l_ref, d)
    lead, trail, norms = split(column_norms(w_ref))
    tail = padded([lead, trail], 16).astype(BF16)
    cols = inverse(norms)
    rows = rows_of(r_ref, cols, d)
    for ref in (out_a, out_b):
        ref[HALF_ROWS:, :] = tail
    for lanes in PARTS:
        code = raised(product(l_ref, w_ref, lanes, d), wide(rows, lanes), cols[:, lanes]).astype(BF16)
        out_a[:HALF_ROWS, lanes] = code[:HALF_ROWS]
        out_b[:HALF_ROWS, lanes] = code[HALF_ROWS:]


def right_near(step, at_ref, g_ref, in_ref, out_ref, w_ref, l_ref, r_ref, p_ref):
    d = lax.rem(at_ref[0] + step, 4)
    start = 0 if step == 1 else HALF_ROWS
    fill_window(g_ref, w_ref, l_ref, d)
    tail = in_ref[HALF_ROWS:, :].astype(F32)
    theirs = tail[0:1] + tail[1:2]
    their_rows = rows_of(r_ref, theirs, d, start, HALF_ROWS)
    lead, trail, norms = split(jnp.sqrt(jnp.square(column_norms(w_ref)) + jnp.square(theirs)))
    out_ref[BLOCK:, :] = padded([lead, trail], 16).astype(BF16)
    cols = inverse(norms)
    rows = rows_of(r_ref, cols, d)
    here = slice(start, start + HALF_ROWS)
    for lanes in PARTS:
        part = p_ref.at[:, : lanes.stop - lanes.start]
        part[...] = product(l_ref, w_ref, lanes, d)
        part[here, :] += root(in_ref[:HALF_ROWS, lanes].astype(F32), wide(their_rows, lanes), theirs[:, lanes])
        out_ref[:BLOCK, lanes] = raised(part[...], wide(rows, lanes), cols[:, lanes]).astype(BF16)


def right_second(at_ref, g_ref, in_1, in_3, out_1, out_3, out_2, own_ref, w_ref, l_ref, r_ref, e_ref, t_ref):
    d, zh = at_ref[0], at_ref[1]
    fill_window(g_ref, w_ref, l_ref, d)
    squares, theirs = jnp.square(column_norms(w_ref)), []
    for ref in (in_1, in_3):
        tail = ref[BLOCK:, :].astype(F32)
        norms = tail[0:1] + tail[1:2]
        squares += jnp.square(norms)
        theirs.append((ref, norms, rows_of(r_ref, norms, d)))
    lead, trail, norms = split(jnp.sqrt(squares))
    cols = inverse(norms)
    rows = rows_of(r_ref, cols, d)
    begin = pl.multiple_of(lead_in(d), 64)
    e_ref[:64, :] = jnp.zeros((64, WINDOW), F32)
    e_ref[BLOCK:, :] = jnp.zeros((64, WINDOW), F32)
    for lanes in PARTS:
        part = product(l_ref, w_ref, lanes, d)
        for ref, their_cols, their_rows in theirs:
            part += root(ref[:BLOCK, lanes].astype(F32), wide(their_rows, lanes), their_cols[:, lanes])
        e_ref[pl.ds(begin, BLOCK), lanes] = raised(part, wide(rows, lanes), cols[:, lanes])
    for i in range(5):
        for j in range(4):
            t_ref[i * 128 : (i + 1) * 128, j * 128 : (j + 1) * 128] = e_ref[
                j * 128 : (j + 1) * 128, 384 + i * 128 : 512 + i * 128
            ].T
    tails = [jnp.concatenate([v[:, t * 128 : (t + 1) * 128] for t in range(11)], 0) for v in (lead, trail, norms)]
    for step, ref in ((1, out_1), (3, out_3), (2, out_2), (0, own_ref)):
        chunk = lax.rem(zh + step, 4) * CHUNK
        piece = e_ref[pl.ds(pl.multiple_of(begin + chunk, 16), CHUNK), :]
        image = t_ref[pl.ds(pl.multiple_of(64 + begin + chunk, 16), CHUNK), tile_after(d)]
        ref[:, :WINDOW] = piece.astype(ref.dtype)
        ref[:, WINDOW:WIDTH] = image.astype(ref.dtype)
        ref[:, WIDTH:] = padded(tails[:2] if step else tails[2:], CHUNK).astype(ref.dtype)


def right_third(scale, at_ref, own_ref, in_1, in_3, in_2, out_ref, image_ref, r_ref, n_ref):
    d, zh = at_ref[0], at_ref[1]
    begin = pl.multiple_of(lead_in(d) + zh * CHUNK, 16)
    for i, ref in enumerate((own_ref, in_1, in_3, in_2)):
        tail = ref[:, WIDTH:].astype(F32)
        n_ref[...] = tail[:11] if i == 0 else tail[:11] + tail[11:22]
        for t in range(8):
            r_ref[t * 128 : (t + 1) * 128, :] = upright(n_ref[t : t + 1, :])
        rows = r_ref[pl.ds(begin, CHUNK), :]
        image_rows = r_ref[pl.ds(pl.multiple_of(448 + begin, 16), CHUNK), :]
        for t in range(14):
            lanes = slice(t * 128, (t + 1) * 128)
            code = ref[:, lanes].astype(F32)
            if t < 11:
                to, here, part = out_ref, lanes, root(code, rows, n_ref[t : t + 1, :])
            else:
                here = slice((t - 11) * 128, (t - 10) * 128)
                cols = n_ref[pl.ds(t - 11 + lax.rem(d, 2), 1), :]
                to, part = image_ref, root(code, image_rows, cols)
            if i == 0:
                to[:, here] = part * scale
            else:
                to[:, here] += part * scale


def right_last(at_ref, base_ref, image_ref, out_ref):
    d = at_ref[0]
    for t in range(14):
        ref, i = (base_ref, t) if t < 11 else (image_ref, t - 11)
        out_ref[:, tile(lax.rem(first_tile(d) + t, TILES))] = ref[:, i * 128 : (i + 1) * 128]


SUB, BASE, ROWS = 128, 1024, 1152


def sub(i):
    return pl.ds(pl.multiple_of(i * SUB, SUB), SUB)


def base_subs(core, b):
    return [4 * a + (core ^ (a > b).astype(jnp.int32)) + 2 * h for a in range(4) for h in (0, 1)]


def slot(i):
    return i // 4 * 4 + 2 * (i % 2) + i // 2 % 2


def more_sub(core, b, zl):
    return 4 * b + lax.rem(2 * zl + core + 1, 4)


def two_cols(ref, core, b):
    return jnp.concatenate([ref[pl.ds(4 * b + core + 2 * zl, 1), :] for zl in (0, 1)], 1)


def left_first(at_ref, far, near, far_2, near_2, out_1, out_3, out_2, own_ref, norm_ref, a_ref, b_ref, i_ref, s_ref):
    zh, y, core = at_ref[1], at_ref[2], at_ref[4]
    for p, ref in enumerate((far, near, far_2, near_2)):
        j = 2 * ((p // 2) ^ core) + lax.rem(p + zh, 2)
        for m in range(4):
            a_ref[sub(4 * j + slot(m)), :] = ref[m * SUB : (m + 1) * SUB, :]
    leads, trails, lanes = [], [], []
    for i in range(16):
        rows = slice(slot(i) * SUB, (slot(i) + 1) * SUB)
        squares = jnp.sum(jnp.square(a_ref[rows, :].astype(F32)), 1, keepdims=True)
        row = jnp.broadcast_to(jnp.sqrt(squares), (SUB, SUB)).T[0:1]
        lead, trail, norms = split(row)
        leads.append(lead), trails.append(trail), lanes.append(norms)
        i_ref[rows, :] = upright(inverse(norms))
    tail = jnp.concatenate([jnp.concatenate(leads, 0), jnp.concatenate(trails, 0)], 1).astype(BF16)
    norm_ref[...] = jnp.concatenate(lanes, 0)
    s_ref[...] = inverse(norm_ref[...])
    for step, out in ((1, out_1), (3, out_3), (2, out_2), (0, own_ref)):
        b = lax.rem(y + step, 4)
        for zl in (0, 1):
            b_ref[zl * SUB : (zl + 1) * SUB, :] = a_ref[sub(slot(4 * b + core + 2 * zl)), :]
        cols = two_cols(s_ref, core, b)
        for k, i in enumerate(base_subs(core, b)[::2]):
            pair = pl.ds(pl.multiple_of(slot(i) * SUB, 2 * SUB), 2 * SUB)
            part = dot(a_ref[pair, :], b_ref[...], 1)
            if step:
                scale = i_ref[pair, :]
                part = raised(part, jnp.concatenate([scale, scale], 1), cols).astype(BF16)
            out[k * 2 * SUB : (k + 1) * 2 * SUB, :] = part
        for zl in (0, 1):
            here = slice(zl * SUB, (zl + 1) * SUB)
            i = slot(more_sub(core, b, zl))
            part = dot(a_ref[sub(i), :], b_ref[here, :], 1)
            if step:
                part = raised(part, i_ref[sub(i), :], cols[:, here]).astype(BF16)
            out[BASE:ROWS, here] = part
        if step:
            out[ROWS:, :] = tail


def left_second(at_ref, own_ref, norm_ref, in_1, in_3, in_2, *refs):
    outs, (e_ref, s_ref, lead_ref, trail_ref, n_ref) = refs[:8], refs[8:]
    zh, y, zl, core = (at_ref[i] for i in (1, 2, 3, 4))
    squares = jnp.square(norm_ref[...])
    for k, ref in enumerate((in_1, in_3, in_2)):
        tail = ref[ROWS:, :].astype(F32)
        norms = tail[:, :SUB] + tail[:, SUB:]
        squares += jnp.square(norms)
        s_ref[k] = norms
    lead_ref[...], trail_ref[...], n_ref[...] = split(jnp.sqrt(squares))
    s_ref[3] = inverse(n_ref[...])
    sources = [(ref, k) for k, ref in enumerate((in_1, in_3, in_2))]
    cols = [two_cols(s_ref.at[k], core, y) for k in range(4)]
    r = lambda k, i: upright(s_ref.at[k][pl.ds(i, 1), :])
    for j, i in enumerate(base_subs(core, y)):
        rows = slice(j * SUB, (j + 1) * SUB)
        part = own_ref[rows, :]
        for ref, k in sources:
            scale = r(k, i)
            part += root(ref[rows, :].astype(F32), jnp.concatenate([scale, scale], 1), cols[k])
        scale = r(3, i)
        e_ref[rows, :] = raised(part, jnp.concatenate([scale, scale], 1), cols[3])
    for l in (0, 1):
        here = slice(l * SUB, (l + 1) * SUB)
        i = more_sub(core, y, l)
        part = own_ref[BASE:ROWS, here]
        for ref, k in sources:
            part += root(ref[BASE:ROWS, here].astype(F32), r(k, i), cols[k][:, here])
        e_ref[BASE:ROWS, here] = raised(part, r(3, i), cols[3][:, here])
    for step, out in zip((*Z_STEPS, 0), outs):
        z = lax.rem(2 * zh + zl + step, 8)
        to_h, to_l = z // 2, lax.rem(z, 2)
        lanes = tile(to_l)
        out[:256, :] = e_ref[pl.ds(pl.multiple_of(to_h * 256, 256), 256), lanes].astype(out.dtype)
        out[256:384, :] = e_ref[BASE:ROWS, lanes].astype(out.dtype)
        first = 4 * to_h + (core ^ (to_h > y).astype(jnp.int32))
        picks = [first, first + 2, more_sub(core, y, to_l), 4 * y + 2 * to_l + core]
        tail = [ref[pl.ds(i, 1), :] for ref in ((lead_ref, trail_ref) if step else (n_ref,)) for i in picks]
        out[384:, :] = padded(tail, 16).astype(out.dtype)


def left_third(scale, at_ref, *refs):
    sources, (base_ref, more_ref, same_ref, other_ref, sum_ref) = refs[:8], refs[8:]
    zh, y, zl = at_ref[1], at_ref[2], at_ref[3]
    for k, ref in enumerate(sources):
        tail = ref[384:, :].astype(F32)
        norms = tail[0:4] if k == 0 else tail[0:4] + tail[4:8]
        for j in range(3):
            rows = slice(j * SUB, (j + 1) * SUB)
            part = root(ref[rows, :].astype(F32), upright(norms[j : j + 1]), norms[3:4]) * scale
            if k == 0:
                sum_ref[rows, :] = part
            else:
                sum_ref[rows, :] += part
    first, second, more = (sum_ref[j * SUB : (j + 1) * SUB, :] for j in range(3))
    base_ref[...] = sum_ref[:256, :]
    more_ref[...] = more
    same_ref[...] = jnp.where(zh == y, more, jnp.where(zl == 0, first, second)).T
    other_ref[...] = jnp.where(zl == 0, second, first).T


def left_last(at_ref, base_ref, more_ref, same_ref, other_ref, out_ref):
    zh, y, zl, core = (at_ref[i] for i in (1, 2, 3, 4))
    n, parity, diagonal = 2 * zl + core, core ^ (zh > y).astype(jnp.int32), zh == y
    out_ref[sub(parity), :] = base_ref[:SUB, :]
    out_ref[sub(parity + 2), :] = base_ref[SUB:, :]
    out_ref[sub(jnp.where(diagonal, lax.rem(n + 3, 4), 2 * zl + 1 - parity)), :] = same_ref[...]
    out_ref[sub(jnp.where(diagonal, lax.rem(n + 1, 4), 2 * (1 - zl) + 1 - parity)), :] = jnp.where(
        diagonal, more_ref[...], other_ref[...]
    )


def last(at_ref, *refs):
    left_last(at_ref, *refs[:4], refs[6])
    right_last(at_ref, *refs[4:6], refs[7])


def mirror(step):
    def to(x, zh, y, zl, core):
        if zh != y:
            return (x, y, zh, zl ^ step, core ^ (zh > y))
        n = (2 * zl + core + 1 - step) % 4
        return (x, zh, y, n // 2, n % 2)

    return to


def along_z(step):
    def to(x, zh, y, zl, core):
        z = (2 * zh + zl + step) % 8
        return (x, z // 2, y, z % 2, core)

    return to


def shards(gradient):
    rows, width = gradient.shape
    row, col = lax.axis_index("row"), lax.axis_index("col")
    x, zh, y, zl, core = row // 4, row % 4, col // 4, col // 2 % 2, col % 2
    at = jnp.stack([x, zh, y, zl, core, x, x, x]).astype(jnp.int32)
    barrier = lax.optimization_barrier
    half = width // 2

    cut = lambda parity: lax.dynamic_slice_in_dim(gradient, parity * half, half, 1)
    near, gradient = barrier((cut((zh + 1) % 2), gradient))
    near = send(near, lambda x, zh, y, zl, core: (x, 2 * core + (zh + 1) % 2, y, zl, zh // 2))

    window = [((rows, WINDOW), BF16), ((512, 512), BF16), ((512, 128), F32)]
    half_part, whole_part = ((HALF_ROWS + 16, WINDOW), BF16), ((BLOCK + 16, WINDOW), BF16)
    over_x = lambda s, v: send(v, lambda x, zh, y, zl, core: (x + s, zh, y, zl, core))
    far_1, far_3 = run(right_far, [half_part] * 2, window, at, gradient)
    far_1, far_3 = over_x(1, far_1), over_x(3, far_3)
    add = lambda s, v: run(
        functools.partial(right_near, s), [whole_part], window + [((BLOCK, 256), F32)], at, gradient, v
    )[0]
    code_1, code_3 = add(1, far_1), add(3, far_3)
    right_1, right_3 = over_x(1, code_1), over_x(3, code_3)
    near, far, _ = barrier((near, cut(zh % 2), code_3))
    far = send(far, lambda x, zh, y, zl, core: (x, 2 * core + zh % 2, y, zl, zh // 2))

    near, far, _ = barrier((near, far, code_1))
    swap = lambda x, zh, y, zl, core: (x, zh, y, zl, 1 - core)
    far_2, near_2 = send(far, swap), send(near, swap)

    piece = (CHUNK, WIDTH + 128)
    code_1, code_3, code_2, right_own = run(
        right_second,
        [(piece, BF16)] * 3 + [(piece, F32)],
        window + [((512, WINDOW), F32), ((640, 512), F32)],
        at,
        gradient,
        right_1,
        right_3,
    )
    over_z = lambda s, v: send(v, lambda x, zh, y, zl, core: (x, zh + s, y, zl, core))
    right_2 = over_z(2, code_2)

    far, near, far_2, near_2, _ = barrier((far, near, far_2, near_2, code_2))
    packed = (ROWS + 16, 256)
    left_1, left_3, left_2, left_own, norms = run(
        left_first,
        [(packed, BF16)] * 3 + [((ROWS, 256), F32), ((16, SUB), F32)],
        [((2048, half), BF16), ((256, half), BF16), ((2048, SUB), F32), ((16, SUB), F32)],
        at,
        far,
        near,
        far_2,
        near_2,
    )
    over_y = lambda s, v: send(v, lambda x, zh, y, zl, core: (x, zh, y + s, zl, core))
    left_1, left_3 = over_y(1, left_1), over_y(3, left_3)
    left_2, right_2 = barrier((left_2, right_2))
    left_1, left_3, code_1, code_3, right_2 = barrier((left_1, left_3, code_1, code_3, right_2))
    left_2, right_1, right_3 = over_y(2, left_2), over_z(1, code_1), over_z(3, code_3)

    piece = (400, SUB)
    codes = run(
        left_second,
        [(piece, BF16)] * 7 + [(piece, F32)],
        [((ROWS, 256), F32), ((4, 16, SUB), F32)] + [((16, SUB), F32)] * 3,
        at,
        left_own,
        norms,
        left_1,
        left_3,
        left_2,
    )
    arrived = [send(code, along_z(s)) for s, code in zip(Z_STEPS, codes)]
    right_1, right_3, _ = barrier((right_1, right_3, codes))

    right_base, image = run(
        functools.partial(right_third, 1.0 / (rows * 16)),
        [((CHUNK, WINDOW), F32), ((CHUNK, IMAGE), F32)],
        [((1024, 128), F32), ((11, 128), F32)],
        at,
        right_own,
        right_1,
        right_3,
        right_2,
    )
    arrived, image = barrier((arrived, image))
    image = over_x(1, image)

    square = ((SUB, SUB), F32)
    base, more, same, other = run(
        functools.partial(left_third, 1.0 / (width * 16)),
        [((256, SUB), F32), square, square, square],
        [((384, SUB), F32)],
        at,
        codes[7],
        *arrived,
    )
    same, other = send(same, mirror(0)), send(other, mirror(1))
    left_gram, right_gram = run(
        last, [((512, SUB), F32), ((CHUNK, width), F32)], [], at, base, more, same, other, right_base, image
    )
    return (left_gram, right_gram)


def solution(mesh):
    in_specs = (P("row", "col"),)
    out_specs = (P("row", "col"), P(("col", "row"), None))
    return jax.shard_map(shards, mesh=mesh, in_specs=in_specs, out_specs=out_specs, check_vma=False)
```

```python
import functools
import itertools

import jax
import jax.numpy as jnp
from jax import lax
from jax.experimental import pallas as pl
from jax.experimental.pallas import tpu as pltpu
from jax.sharding import PartitionSpec as P

F32, BF16 = jnp.float32, jnp.bfloat16

SIZES = (4, 4, 4, 2, 2)
PLACES = list(itertools.product(*(range(n) for n in SIZES)))
STEPS = (1, 3, 2)
Z_STEPS = (1, 4, 7, 3, 5, 2, 6)


def number(place):
    x, zh, y, zl, core = (p % n for p, n in zip(place, SIZES))
    return (4 * x + zh) * 16 + 4 * y + 2 * zl + core


def send(array, to):
    return lax.ppermute(array, ("row", "col"), [(number(p), number(to(*p))) for p in PLACES])


POWER = 13
LIFT = 120 / POWER
LOG_LIFT = LIFT * 0.6931471805599453


def split(norms):
    lead = norms.astype(BF16).astype(F32)
    trail = (norms - lead).astype(BF16).astype(F32)
    return lead, trail, lead + trail


def inverse(norms):
    return jnp.where(norms > 0, 1.0 / jnp.where(norms > 0, norms, 1.0), 0.0)


def raised(value, rows, cols):
    ratio = value * rows * (cols * 2.0**LIFT)
    p2 = ratio * ratio
    p4 = p2 * p2
    return p4 * p4 * (p4 * ratio)


def root(code, rows, cols):
    size = jnp.exp(jnp.log(jnp.abs(code)) * (1.0 / POWER) - LOG_LIFT)
    return jnp.where(code < 0, -size, size) * (rows * cols)


def upright(row):
    parts = [row[:, i : i + 128] for i in range(0, row.shape[1], 128)]
    return jnp.concatenate([jnp.broadcast_to(p, (128, 128)).T for p in parts], 0)


def dot(left, right, dim):
    return lax.dot_general(
        left, right, (((dim,), (dim,)), ((), ())), preferred_element_type=F32
    )


def run(body, outs, scratch, *args):
    smem, vmem = pl.BlockSpec(memory_space=pltpu.SMEM), pl.BlockSpec(memory_space=pltpu.VMEM)
    return pl.pallas_call(
        body,
        out_shape=[jax.ShapeDtypeStruct(shape, dtype) for shape, dtype in outs],
        in_specs=[smem] + [vmem] * (len(args) - 1),
        out_specs=[vmem] * len(outs),
        scratch_shapes=[pltpu.VMEM(shape, dtype) for shape, dtype in scratch],
        cost_estimate=pl.CostEstimate(flops=1000, bytes_accessed=1000, transcendentals=0),
        compiler_params=pltpu.CompilerParams(vmem_limit_bytes=48 * 1024 * 1024),
    )(*args)


BLOCK, CHUNK, TILES, WINDOW, IMAGE = 448, 112, 14, 1408, 384
WIDTH = WINDOW + IMAGE


def first_tile(d):
    return 7 * (d // 2) + 3 * (d % 2)


def lead_in(d):
    return 64 * (d % 2)


def tile(i):
    return pl.ds(pl.multiple_of(i * 128, 128), 128)


HALF_ROWS = BLOCK // 2
PARTS = [slice(i, min(i + 256, WINDOW)) for i in range(0, WINDOW, 256)]


def fill_window(g_ref, w_ref, l_ref, d):
    for t in range(11):
        w_ref[:, t * 128 : (t + 1) * 128] = g_ref[:, tile(lax.rem(first_tile(d) + t, TILES))]
    l_ref[...] = w_ref[:, :512].T


def tile_after(d):
    return pl.ds(pl.multiple_of(128 * (d % 2), 128), IMAGE)


def column_norms(w_ref):
    return jnp.sqrt(jnp.sum(jnp.square(w_ref[...].astype(F32)), 0, keepdims=True))


def padded(rows, count):
    rows = jnp.concatenate(rows, 0)
    return jnp.concatenate([rows, jnp.zeros((count - rows.shape[0], rows.shape[1]), F32)], 0)


def rows_of(r_ref, norms, d, start=0, count=BLOCK):
    r_ref[...] = upright(norms[:, :512])
    return r_ref[pl.ds(pl.multiple_of(lead_in(d) + start, 16), count), :]


def wide(rows, lanes):
    return rows if lanes.stop - lanes.start == 128 else jnp.concatenate([rows, rows], 1)


def product(l_ref, w_ref, lanes, d):
    left = l_ref[pl.ds(pl.multiple_of(lead_in(d), 64), BLOCK), :]
    return jnp.dot(left, w_ref[:, lanes], preferred_element_type=F32)


def right_far(at_ref, g_ref, out_a, out_b, w_ref, l_ref, r_ref):
    d = lax.rem(at_ref[0] + 2, 4)
    fill_window(g_ref, w_ref, l_ref, d)
    lead, trail, norms = split(column_norms(w_ref))
    tail = padded([lead, trail], 16).astype(BF16)
    cols = inverse(norms)
    rows = rows_of(r_ref, cols, d)
    for ref in (out_a, out_b):
        ref[HALF_ROWS:, :] = tail
    for lanes in PARTS:
        code = raised(product(l_ref, w_ref, lanes, d), wide(rows, lanes), cols[:, lanes]).astype(BF16)
        out_a[:HALF_ROWS, lanes] = code[:HALF_ROWS]
        out_b[:HALF_ROWS, lanes] = code[HALF_ROWS:]


def right_near(step, at_ref, g_ref, in_ref, out_ref, w_ref, l_ref, r_ref, p_ref):
    d = lax.rem(at_ref[0] + step, 4)
    start = 0 if step == 1 else HALF_ROWS
    fill_window(g_ref, w_ref, l_ref, d)
    tail = in_ref[HALF_ROWS:, :].astype(F32)
    theirs = tail[0:1] + tail[1:2]
    their_rows = rows_of(r_ref, theirs, d, start, HALF_ROWS)
    lead, trail, norms = split(jnp.sqrt(jnp.square(column_norms(w_ref)) + jnp.square(theirs)))
    out_ref[BLOCK:, :] = padded([lead, trail], 16).astype(BF16)
    cols = inverse(norms)
    rows = rows_of(r_ref, cols, d)
    here = slice(start, start + HALF_ROWS)
    for lanes in PARTS:
        part = p_ref.at[:, : lanes.stop - lanes.start]
        part[...] = product(l_ref, w_ref, lanes, d)
        part[here, :] += root(in_ref[:HALF_ROWS, lanes].astype(F32), wide(their_rows, lanes), theirs[:, lanes])
        out_ref[:BLOCK, lanes] = raised(part[...], wide(rows, lanes), cols[:, lanes]).astype(BF16)


def right_product(at_ref, g_ref, out_ref, norm_ref, w_ref, l_ref, r_ref):
    d = at_ref[0]
    fill_window(g_ref, w_ref, l_ref, d)
    norm_ref[...] = jnp.broadcast_to(column_norms(w_ref), (8, WINDOW))
    for lanes in PARTS:
        out_ref[:, lanes] = product(l_ref, w_ref, lanes, d)


def right_second(at_ref, p_ref, norm_ref, in_1, in_3, out_1, out_3, out_2, own_ref, r_ref, e_ref, t_ref):
    d, zh = at_ref[0], at_ref[1]
    squares, theirs = jnp.square(norm_ref[0:1, :]), []
    for ref in (in_1, in_3):
        tail = ref[BLOCK:, :].astype(F32)
        norms = tail[0:1] + tail[1:2]
        squares += jnp.square(norms)
        theirs.append((ref, norms, rows_of(r_ref, norms, d)))
    lead, trail, norms = split(jnp.sqrt(squares))
    cols = inverse(norms)
    rows = rows_of(r_ref, cols, d)
    begin = pl.multiple_of(lead_in(d), 64)
    e_ref[:64, :] = jnp.zeros((64, WINDOW), F32)
    e_ref[BLOCK:, :] = jnp.zeros((64, WINDOW), F32)
    for lanes in PARTS:
        part = p_ref[:, lanes]
        for ref, their_cols, their_rows in theirs:
            part += root(ref[:BLOCK, lanes].astype(F32), wide(their_rows, lanes), their_cols[:, lanes])
        e_ref[pl.ds(begin, BLOCK), lanes] = raised(part, wide(rows, lanes), cols[:, lanes])
    for i in range(5):
        for j in range(4):
            t_ref[i * 128 : (i + 1) * 128, j * 128 : (j + 1) * 128] = e_ref[
                j * 128 : (j + 1) * 128, 384 + i * 128 : 512 + i * 128
            ].T
    tails = [jnp.concatenate([v[:, t * 128 : (t + 1) * 128] for t in range(11)], 0) for v in (lead, trail, norms)]
    for step, ref in ((1, out_1), (3, out_3), (2, out_2), (0, own_ref)):
        chunk = lax.rem(zh + step, 4) * CHUNK
        piece = e_ref[pl.ds(pl.multiple_of(begin + chunk, 16), CHUNK), :]
        image = t_ref[pl.ds(pl.multiple_of(64 + begin + chunk, 16), CHUNK), tile_after(d)]
        ref[:, :WINDOW] = piece.astype(ref.dtype)
        ref[:, WINDOW:WIDTH] = image.astype(ref.dtype)
        ref[:, WIDTH:] = padded(tails[:2] if step else tails[2:], CHUNK).astype(ref.dtype)


def right_third(scale, at_ref, own_ref, in_1, in_3, in_2, out_ref, image_ref, r_ref, n_ref):
    d, zh = at_ref[0], at_ref[1]
    begin = pl.multiple_of(lead_in(d) + zh * CHUNK, 16)
    for i, ref in enumerate((own_ref, in_1, in_3, in_2)):
        tail = ref[:, WIDTH:].astype(F32)
        n_ref[...] = tail[:11] if i == 0 else tail[:11] + tail[11:22]
        for t in range(8):
            r_ref[t * 128 : (t + 1) * 128, :] = upright(n_ref[t : t + 1, :])
        rows = r_ref[pl.ds(begin, CHUNK), :]
        image_rows = r_ref[pl.ds(pl.multiple_of(448 + begin, 16), CHUNK), :]
        for t in range(14):
            lanes = slice(t * 128, (t + 1) * 128)
            code = ref[:, lanes].astype(F32)
            if t < 11:
                to, here, part = out_ref, lanes, root(code, rows, n_ref[t : t + 1, :])
            else:
                here = slice((t - 11) * 128, (t - 10) * 128)
                cols = n_ref[pl.ds(t - 11 + lax.rem(d, 2), 1), :]
                to, part = image_ref, root(code, image_rows, cols)
            if i == 0:
                to[:, here] = part * scale
            else:
                to[:, here] += part * scale


def right_last(at_ref, base_ref, image_ref, out_ref):
    d = at_ref[0]
    for t in range(14):
        ref, i = (base_ref, t) if t < 11 else (image_ref, t - 11)
        out_ref[:, tile(lax.rem(first_tile(d) + t, TILES))] = ref[:, i * 128 : (i + 1) * 128]


SUB, BASE, ROWS = 128, 1024, 1152


def sub(i):
    return pl.ds(pl.multiple_of(i * SUB, SUB), SUB)


def base_subs(core, b):
    return [4 * a + (core ^ (a > b).astype(jnp.int32)) + 2 * h for a in range(4) for h in (0, 1)]


def slot(i):
    return i // 4 * 4 + 2 * (i % 2) + i // 2 % 2


def more_sub(core, b, zl):
    return 4 * b + lax.rem(2 * zl + core + 1, 4)


def two_cols(ref, core, b):
    return jnp.concatenate([ref[pl.ds(4 * b + core + 2 * zl, 1), :] for zl in (0, 1)], 1)


def left_first(at_ref, far, near, far_2, near_2, out_1, out_3, out_2, own_ref, norm_ref, a_ref, b_ref, i_ref, s_ref):
    zh, y, core = at_ref[1], at_ref[2], at_ref[4]
    for p, ref in enumerate((far, near, far_2, near_2)):
        j = 2 * ((p // 2) ^ core) + lax.rem(p + zh, 2)
        for m in range(4):
            a_ref[sub(4 * j + slot(m)), :] = ref[m * SUB : (m + 1) * SUB, :]
    leads, trails, lanes = [], [], []
    for i in range(16):
        rows = slice(slot(i) * SUB, (slot(i) + 1) * SUB)
        squares = jnp.sum(jnp.square(a_ref[rows, :].astype(F32)), 1, keepdims=True)
        row = jnp.broadcast_to(jnp.sqrt(squares), (SUB, SUB)).T[0:1]
        lead, trail, norms = split(row)
        leads.append(lead), trails.append(trail), lanes.append(norms)
        i_ref[rows, :] = upright(inverse(norms))
    tail = jnp.concatenate([jnp.concatenate(leads, 0), jnp.concatenate(trails, 0)], 1).astype(BF16)
    norm_ref[...] = jnp.concatenate(lanes, 0)
    s_ref[...] = inverse(norm_ref[...])
    for step, out in ((1, out_1), (3, out_3), (2, out_2), (0, own_ref)):
        b = lax.rem(y + step, 4)
        for zl in (0, 1):
            b_ref[zl * SUB : (zl + 1) * SUB, :] = a_ref[sub(slot(4 * b + core + 2 * zl)), :]
        cols = two_cols(s_ref, core, b)
        for k, i in enumerate(base_subs(core, b)[::2]):
            pair = pl.ds(pl.multiple_of(slot(i) * SUB, 2 * SUB), 2 * SUB)
            part = dot(a_ref[pair, :], b_ref[...], 1)
            if step:
                scale = i_ref[pair, :]
                part = raised(part, jnp.concatenate([scale, scale], 1), cols).astype(BF16)
            out[k * 2 * SUB : (k + 1) * 2 * SUB, :] = part
        for zl in (0, 1):
            here = slice(zl * SUB, (zl + 1) * SUB)
            i = slot(more_sub(core, b, zl))
            part = dot(a_ref[sub(i), :], b_ref[here, :], 1)
            if step:
                part = raised(part, i_ref[sub(i), :], cols[:, here]).astype(BF16)
            out[BASE:ROWS, here] = part
        if step:
            out[ROWS:, :] = tail


def left_second(at_ref, own_ref, norm_ref, in_1, in_3, in_2, *refs):
    outs, (e_ref, s_ref, lead_ref, trail_ref, n_ref) = refs[:8], refs[8:]
    zh, y, zl, core = (at_ref[i] for i in (1, 2, 3, 4))
    squares = jnp.square(norm_ref[...])
    for k, ref in enumerate((in_1, in_3, in_2)):
        tail = ref[ROWS:, :].astype(F32)
        norms = tail[:, :SUB] + tail[:, SUB:]
        squares += jnp.square(norms)
        s_ref[k] = norms
    lead_ref[...], trail_ref[...], n_ref[...] = split(jnp.sqrt(squares))
    s_ref[3] = inverse(n_ref[...])
    sources = [(ref, k) for k, ref in enumerate((in_1, in_3, in_2))]
    cols = [two_cols(s_ref.at[k], core, y) for k in range(4)]
    r = lambda k, i: upright(s_ref.at[k][pl.ds(i, 1), :])
    for j, i in enumerate(base_subs(core, y)):
        rows = slice(j * SUB, (j + 1) * SUB)
        part = own_ref[rows, :]
        for ref, k in sources:
            scale = r(k, i)
            part += root(ref[rows, :].astype(F32), jnp.concatenate([scale, scale], 1), cols[k])
        scale = r(3, i)
        e_ref[rows, :] = raised(part, jnp.concatenate([scale, scale], 1), cols[3])
    for l in (0, 1):
        here = slice(l * SUB, (l + 1) * SUB)
        i = more_sub(core, y, l)
        part = own_ref[BASE:ROWS, here]
        for ref, k in sources:
            part += root(ref[BASE:ROWS, here].astype(F32), r(k, i), cols[k][:, here])
        e_ref[BASE:ROWS, here] = raised(part, r(3, i), cols[3][:, here])
    for step, out in zip((*Z_STEPS, 0), outs):
        z = lax.rem(2 * zh + zl + step, 8)
        to_h, to_l = z // 2, lax.rem(z, 2)
        lanes = tile(to_l)
        out[:256, :] = e_ref[pl.ds(pl.multiple_of(to_h * 256, 256), 256), lanes].astype(out.dtype)
        out[256:384, :] = e_ref[BASE:ROWS, lanes].astype(out.dtype)
        first = 4 * to_h + (core ^ (to_h > y).astype(jnp.int32))
        picks = [first, first + 2, more_sub(core, y, to_l), 4 * y + 2 * to_l + core]
        tail = [ref[pl.ds(i, 1), :] for ref in ((lead_ref, trail_ref) if step else (n_ref,)) for i in picks]
        out[384:, :] = padded(tail, 16).astype(out.dtype)


def left_third(scale, at_ref, *refs):
    sources, (base_ref, more_ref, same_ref, other_ref, sum_ref) = refs[:8], refs[8:]
    zh, y, zl = at_ref[1], at_ref[2], at_ref[3]
    for k, ref in enumerate(sources):
        tail = ref[384:, :].astype(F32)
        norms = tail[0:4] if k == 0 else tail[0:4] + tail[4:8]
        for j in range(3):
            rows = slice(j * SUB, (j + 1) * SUB)
            part = root(ref[rows, :].astype(F32), upright(norms[j : j + 1]), norms[3:4]) * scale
            if k == 0:
                sum_ref[rows, :] = part
            else:
                sum_ref[rows, :] += part
    first, second, more = (sum_ref[j * SUB : (j + 1) * SUB, :] for j in range(3))
    base_ref[...] = sum_ref[:256, :]
    more_ref[...] = more
    same_ref[...] = jnp.where(zh == y, more, jnp.where(zl == 0, first, second)).T
    other_ref[...] = jnp.where(zl == 0, second, first).T


def left_last(at_ref, base_ref, more_ref, same_ref, other_ref, out_ref):
    zh, y, zl, core = (at_ref[i] for i in (1, 2, 3, 4))
    n, parity, diagonal = 2 * zl + core, core ^ (zh > y).astype(jnp.int32), zh == y
    out_ref[sub(parity), :] = base_ref[:SUB, :]
    out_ref[sub(parity + 2), :] = base_ref[SUB:, :]
    out_ref[sub(jnp.where(diagonal, lax.rem(n + 3, 4), 2 * zl + 1 - parity)), :] = same_ref[...]
    out_ref[sub(jnp.where(diagonal, lax.rem(n + 1, 4), 2 * (1 - zl) + 1 - parity)), :] = jnp.where(
        diagonal, more_ref[...], other_ref[...]
    )


def last(at_ref, *refs):
    left_last(at_ref, *refs[:4], refs[6])
    right_last(at_ref, *refs[4:6], refs[7])


def mirror(step):
    def to(x, zh, y, zl, core):
        if zh != y:
            return (x, y, zh, zl ^ step, core ^ (zh > y))
        n = (2 * zl + core + 1 - step) % 4
        return (x, zh, y, n // 2, n % 2)

    return to


def along_z(step):
    def to(x, zh, y, zl, core):
        z = (2 * zh + zl + step) % 8
        return (x, z // 2, y, z % 2, core)

    return to


def shards(gradient):
    rows, width = gradient.shape
    row, col = lax.axis_index("row"), lax.axis_index("col")
    x, zh, y, zl, core = row // 4, row % 4, col // 4, col // 2 % 2, col % 2
    at = jnp.stack([x, zh, y, zl, core, x, x, x]).astype(jnp.int32)
    barrier = lax.optimization_barrier
    half = width // 2

    cut = lambda parity: lax.dynamic_slice_in_dim(gradient, parity * half, half, 1)
    near, gradient = barrier((cut((zh + 1) % 2), gradient))
    near = send(near, lambda x, zh, y, zl, core: (x, 2 * core + (zh + 1) % 2, y, zl, zh // 2))

    window = [((rows, WINDOW), BF16), ((512, 512), BF16), ((512, 128), F32)]
    half_part, whole_part = ((HALF_ROWS + 16, WINDOW), BF16), ((BLOCK + 16, WINDOW), BF16)
    over_x = lambda s, v: send(v, lambda x, zh, y, zl, core: (x + s, zh, y, zl, core))
    far_1, far_3 = run(right_far, [half_part] * 2, window, at, gradient)
    far_1, far_3 = over_x(1, far_1), over_x(3, far_3)
    add = lambda s, v: run(
        functools.partial(right_near, s), [whole_part], window + [((BLOCK, 256), F32)], at, gradient, v
    )[0]
    code_1, code_3 = add(1, far_1), add(3, far_3)
    right_1, right_3 = over_x(1, code_1), over_x(3, code_3)
    near, far, _ = barrier((near, cut(zh % 2), code_3))
    far = send(far, lambda x, zh, y, zl, core: (x, 2 * core + zh % 2, y, zl, zh // 2))

    gradient, _ = barrier((gradient, (code_1, code_3)))
    product_own, norms_own = run(
        right_product, [((BLOCK, WINDOW), F32), ((8, WINDOW), F32)], window, at, gradient
    )

    near, far, product_own = barrier((near, far, product_own))
    swap = lambda x, zh, y, zl, core: (x, zh, y, zl, 1 - core)
    far_2, near_2 = send(far, swap), send(near, swap)

    piece = (CHUNK, WIDTH + 128)
    code_1, code_3, code_2, right_own = run(
        right_second,
        [(piece, BF16)] * 3 + [(piece, F32)],
        [((512, 128), F32), ((512, WINDOW), F32), ((640, 512), F32)],
        at,
        product_own,
        norms_own,
        right_1,
        right_3,
    )
    over_z = lambda s, v: send(v, lambda x, zh, y, zl, core: (x, zh + s, y, zl, core))
    right_1, right_3 = over_z(1, code_1), over_z(3, code_3)

    far, near, far_2, near_2, _ = barrier((far, near, far_2, near_2, code_1))
    packed = (ROWS + 16, 256)
    left_1, left_3, left_2, left_own, norms = run(
        left_first,
        [(packed, BF16)] * 3 + [((ROWS, 256), F32), ((16, SUB), F32)],
        [((2048, half), BF16), ((256, half), BF16), ((2048, SUB), F32), ((16, SUB), F32)],
        at,
        far,
        near,
        far_2,
        near_2,
    )
    over_y = lambda s, v: send(v, lambda x, zh, y, zl, core: (x, zh, y + s, zl, core))
    left_1, left_3 = over_y(1, left_1), over_y(3, left_3)
    left_2, right_1, right_3 = barrier((left_2, right_1, right_3))
    left_1, left_3, code_2, right_1, right_3 = barrier((left_1, left_3, code_2, right_1, right_3))
    left_2, right_2 = over_y(2, left_2), over_z(2, code_2)

    piece = (400, SUB)
    codes = run(
        left_second,
        [(piece, BF16)] * 7 + [(piece, F32)],
        [((ROWS, 256), F32), ((4, 16, SUB), F32)] + [((16, SUB), F32)] * 3,
        at,
        left_own,
        norms,
        left_1,
        left_3,
        left_2,
    )
    arrived = [send(code, along_z(s)) for s, code in zip(Z_STEPS, codes)]
    right_1, right_3, _ = barrier((right_1, right_3, codes))

    right_base, image = run(
        functools.partial(right_third, 1.0 / (rows * 16)),
        [((CHUNK, WINDOW), F32), ((CHUNK, IMAGE), F32)],
        [((1024, 128), F32), ((11, 128), F32)],
        at,
        right_own,
        right_1,
        right_3,
        right_2,
    )
    arrived, image = barrier((arrived, image))
    image = over_x(1, image)

    square = ((SUB, SUB), F32)
    base, more, same, other = run(
        functools.partial(left_third, 1.0 / (width * 16)),
        [((256, SUB), F32), square, square, square],
        [((384, SUB), F32)],
        at,
        codes[7],
        *arrived,
    )
    same, other = send(same, mirror(0)), send(other, mirror(1))
    left_gram, right_gram = run(
        last, [((512, SUB), F32), ((CHUNK, width), F32)], [], at, base, more, same, other, right_base, image
    )
    return (left_gram, right_gram)


def solution(mesh):
    in_specs = (P("row", "col"),)
    out_specs = (P("row", "col"), P(("col", "row"), None))
    return jax.shard_map(shards, mesh=mesh, in_specs=in_specs, out_specs=out_specs, check_vma=False)
```
